32 devices in a mesh: grp: 2 (over y), ao: 4 (over z), aux: 2 (over x), orb: 2 (over core).
Axes of the slice: x: 2, y: 2, z: 4, core: 2. Of those that a mesh axis runs over, the one named last changes fastest.
Arguments:
- integrals: bfloat16 [8, 2048, 1280], P(('grp', 'aux'), 'ao'), parts along dimension 0, may hold values from -0.15625 to 0.15625
- coeffs: bfloat16 [4096, 1024], P(('grp', 'ao'), 'orb'), parts along dimension 0, may hold values from -6 to 6
- pair_blocks: int32 [128, 2], P('grp'), parts along dimension 0, may hold values from 0 to 7, as said below
- pair_count: int32 [8], P('grp'), parts along dimension 0, may hold values from 1 to 16, as said below
- orbital_count: int32 [16], P('grp'), parts along dimension 0, may hold values from 256 to 1024, as said below
Outputs:
- exchange_blocks: float32 [256, 128, 256], P(('aux', 'orb'), ('grp', 'ao')), parts along dimension 1
The draws below stay inside these ranges and needn't reach their ends.
There are 2 independent parts, one for each index of `grp`. The reference program is written for one: setup_inputs(seed, part) draws one part's arguments, and reference() takes and returns one part's arrays. A program takes and returns all parts, laid end to end along the dimension named above; each array names one. Nothing has to cross between parts.
Inputs may be any that keep to these rules, and one draw needn't show every extreme that they name: `pair_blocks`: every row names blocks of two different block groups (a block group is the blocks b with equal b // 2), the first group the lower. Within the 16 rows of one owner, all blocks named from one block group are the same block; rows past the owner's count follow the same rule and are not used. `pair_count`: some owner has exactly 16 live slots and some owner exactly 1. Orbital i is significant on block b when i < orbital_count[b]; some block has all 1024, some exactly 256.
All inputs are finite; a program needn't handle non-finite values.
Results may differ from the reference program's by a relative error of at most 0.0039.
Values may be sent and summed in bfloat16 or wider, within the bound.
No kernel may reach another device: no remote copies, remote signals or barrier semaphores. Data moves between devices by JAX's collectives and lax.ppermute only.
A program may use at most 128 MiB of HBM per device.

```python
import math
import jax
import jax.numpy as jnp
from jax import lax

BLOCK = 256
AO_DEV = 2
WIN = 5
ORBS = 1024
PMAX = 16
NBAS = 2048
NBLK = 8
NAUX = 4
PAIR_SLOT_TOTAL = 64
N_AO = 4


def draw_pair_blocks(key, part):
    key = jax.random.fold_in(key, 11)
    first_key, secondary_sort_key, third_key = jax.random.split(key, 3)
    selected = jax.random.randint(first_key, (N_AO, N_AO), 0, AO_DEV)
    lower = jax.random.randint(secondary_sort_key, (N_AO, PMAX), 0, N_AO)
    stride = jax.random.randint(third_key, (N_AO, PMAX), 1, N_AO)
    partner_device = (lower + stride) % N_AO
    first = jnp.minimum(lower, partner_device)
    second = jnp.maximum(lower, partner_device)
    owner = jnp.arange(N_AO, dtype=jnp.int32)[:, None]
    block_first = first * AO_DEV + selected[owner, first]
    block_second = second * AO_DEV + selected[owner, second]
    return jnp.stack([block_first, block_second], -1).reshape(N_AO * PMAX, 2).astype(jnp.int32)


def draw_pair_count(key, part):
    key = jax.random.fold_in(key, 12)
    count_key, order_key = jax.random.split(key)
    counts = jax.random.randint(count_key, (N_AO,), 1, PMAX + 1)
    order = jax.random.permutation(order_key, N_AO)
    counts = counts.at[order[0]].set(PMAX).at[order[1]].set(1)
    return counts.astype(jnp.int32)


def draw_orbital_count(key, part):
    key = jax.random.fold_in(key, 13)
    count_key, order_key = jax.random.split(key)
    counts = jax.random.randint(count_key, (NBLK,), ORBS // 4, ORBS + 1)
    order = jax.random.permutation(order_key, NBLK)
    counts = counts.at[order[0]].set(ORBS).at[order[1]].set(ORBS // 4)
    return counts.astype(jnp.int32)


def block_levels(own_key, extent, shards, smallest, largest):
    def one(position, shards_of):
        heights = jax.random.uniform(jax.random.fold_in(jax.random.fold_in(own_key, 6), position), (shards_of,), jnp.float32, smallest / len(shards), largest / len(shards))
        return jnp.repeat(jnp.exp(heights), extent[position] // shards_of).reshape((-1,) + (1,) * (len(extent) - position - 1))

    gain = one(*shards[0])
    for cut in shards[1:]:
        gain = gain * one(*cut)
    return gain


def noise(rng, dims, width, limit, cuts=(), kind=jnp.bfloat16):
    values = width * jax.random.normal(rng, dims, jnp.float32)
    if cuts:
        values = values * block_levels(rng, dims, cuts, -0.22, 0.18)
    return jnp.clip(values, -limit, limit).astype(kind)


def setup_inputs(seed: int = 0, part: int = 0) -> dict:
    key_list = jax.random.split(jax.random.key(seed), 6)
    part_splits = jax.random.split(jax.random.fold_in(key_list[5], part), 6)
    return {
        "integrals": noise(part_splits[0], (NAUX, NBAS, WIN * BLOCK), (WIN * BLOCK) ** -0.5, 0.15625, ((0, 2), (1, 4))),
        "coeffs": noise(part_splits[1], (NBAS, ORBS), 1.0, 6.0, ((0, 4), (1, 2))),
        "pair_blocks": draw_pair_blocks(jax.random.fold_in(jax.random.fold_in(key_list[5], part), 71), part),
        "pair_count": draw_pair_count(jax.random.fold_in(jax.random.fold_in(key_list[5], part), 71), part),
        "orbital_count": draw_orbital_count(jax.random.fold_in(jax.random.fold_in(key_list[5], part), 71), part),
    }


def reference(integrals, coeffs, pair_blocks, pair_count, orbital_count):
    rim = WIN // 2 * BLOCK
    padded = jnp.pad(coeffs, ((rim, rim), (0, 0)))
    orbital_ids = jnp.arange(ORBS, dtype=jnp.int32)

    def transform(block_id):
        slab = lax.dynamic_slice_in_dim(integrals, block_id * BLOCK, BLOCK, 1).astype(jnp.float32)
        slot_range = lax.dynamic_slice_in_dim(padded, block_id * BLOCK, WIN * BLOCK, 0).astype(jnp.float32)
        values = jnp.einsum('pml,li->pmi', slab, slot_range)
        keep = orbital_ids < orbital_count[block_id]
        return jnp.where(keep[None, None, :], values, 0.0).astype(jnp.bfloat16)
    half = lax.map(transform, jnp.arange(NBLK, dtype=jnp.int32))
    slot_numbers = jnp.arange(PAIR_SLOT_TOTAL, dtype=jnp.int32)
    live = slot_numbers % PMAX < pair_count[slot_numbers // PMAX]

    def pair_block(slot):
        left = half[pair_blocks[slot, 0]].astype(jnp.float32)
        right = half[pair_blocks[slot, 1]].astype(jnp.float32)
        return jnp.einsum('pmi,pni->mn', left, right)
    blocks = lax.map(pair_block, slot_numbers)
    scaled = blocks * (1.0 / math.sqrt(NAUX * ORBS))
    scaled = jnp.where(live[:, None, None], scaled, 0.0).astype(jnp.float32)
    return jnp.transpose(scaled, (1, 0, 2))
```

```python
import functools
import math

import jax
import jax.numpy as jnp
from jax import lax
from jax.experimental import pallas as pl
from jax.experimental.pallas import tpu as pltpu
from jax.sharding import PartitionSpec as P

BLOCK = 256
AO_DEV = 2
WIN = 5
ORBS = 1024
CHUNKS = 2
VMEM_LIMIT = 40 * 1024 * 1024


def with_halo(cells, sides, width):
    for axis, dim in sides:
        count = lax.axis_size(axis)
        ends = count - 1
        head = lax.slice_in_dim(cells, 0, width, axis=dim)
        tail = lax.slice_in_dim(cells, cells.shape[dim] - width, cells.shape[dim], axis=dim)
        cells = jnp.concatenate(
            [
                lax.ppermute(tail, axis, [(i, (i + 1) % count) for i in range(ends)]),
                cells,
                lax.ppermute(head, axis, [((i + 1) % count, i) for i in range(ends)]),
            ],
            axis=dim,
        )
    return cells


def general_body(integrals, coeffs, pair_blocks, pair_count, orbital_count):
    orb_local = coeffs.shape[1]
    aux_devices = lax.axis_size("aux")
    total_aux = integrals.shape[0] * aux_devices
    rim = WIN // 2 * BLOCK
    extended = with_halo(coeffs, (("ao", 0),), rim)
    ao_here = lax.axis_index("ao")
    orbital_ids = lax.axis_index("orb") * orb_local + jnp.arange(orb_local, dtype=jnp.int32)
    pieces = []
    for offset in range(AO_DEV):
        slab = integrals[:, offset * BLOCK : (offset + 1) * BLOCK, :]
        slot_range = extended[offset * BLOCK : offset * BLOCK + WIN * BLOCK]
        values = jnp.einsum("pml,li->pmi", slab, slot_range, preferred_element_type=jnp.float32)
        limit = orbital_count[ao_here * AO_DEV + offset]
        values = jnp.where((orbital_ids < limit)[None, None, :], values, 0.0)
        pieces.append(values.astype(jnp.bfloat16))
    transformed = jnp.stack(pieces)
    owners = lax.axis_size("ao")
    table = pair_blocks.reshape(owners, -1, 2)
    slots = table.shape[1]
    live = jnp.arange(slots, dtype=jnp.int32)[None, :] < pair_count[:, None]
    touched = live[:, :, None] & (table // AO_DEV == ao_here)
    wanted = jnp.max(jnp.where(touched, table % AO_DEV, 0), axis=(1, 2))
    outgoing = transformed[wanted]
    received = lax.all_to_all(outgoing, "ao", split_axis=0, concat_axis=0, tiled=True)
    owned = table[ao_here]
    factor = 1.0 / math.sqrt(total_aux * ORBS)
    weights = jnp.where(live[ao_here], factor, 0.0).astype(jnp.float32)
    left_source = owned[:, 0] // AO_DEV
    right_source = owned[:, 1] // AO_DEV
    right_factors = received[right_source]
    lefts = received[left_source]
    term = jnp.einsum("spmi,spni->msn", lefts, right_factors, preferred_element_type=jnp.float32)
    return lax.psum_scatter(
        term * weights[None, :, None], ("aux", "orb"), scatter_dimension=0, tiled=True
    )


EARLY_PAIRS = ((0, 1), (0, 2), (1, 2))
LATE_PAIRS = ((0, 3), (1, 3), (2, 3))
ALL_PAIRS = EARLY_PAIRS + LATE_PAIRS


def transform_kernel(meta, integrals, prev, own, following, out0, out1, out2, out3, half):
    columns = own.shape[1]
    ids = lax.broadcasted_iota(jnp.int32, (BLOCK, columns), 1)
    mid = AO_DEV * BLOCK

    def dot(a, b):
        return jnp.dot(a, b, preferred_element_type=jnp.float32)

    for offset in range(AO_DEV):
        low = mid - offset * BLOCK
        for p in range(integrals.shape[0]):
            slab = integrals[p, offset * BLOCK : (offset + 1) * BLOCK, :]
            values = dot(slab[:, low : low + mid], own[...])
            values += dot(slab[:, :low], prev[offset * BLOCK :, :])
            values += dot(slab[:, low + mid :], following[: (offset + 1) * BLOCK, :])
            half[offset, p] = jnp.where(ids < meta[4 + offset], values, 0.0).astype(jnp.bfloat16)
    for s, out in enumerate((out0, out1, out2, out3)):
        out[...] = half[meta[s]]


def transform(meta, integrals, prev, own, following):
    shape = (integrals.shape[0], BLOCK, own.shape[1])
    vmem = pl.BlockSpec(memory_space=pltpu.VMEM)
    return pl.pallas_call(
        transform_kernel,
        out_shape=[jax.ShapeDtypeStruct(shape, jnp.bfloat16)] * 4,
        in_specs=[pl.BlockSpec(memory_space=pltpu.SMEM)] + [vmem] * 4,
        out_specs=[vmem] * 4,
        scratch_shapes=[pltpu.VMEM((AO_DEV, *shape), jnp.bfloat16)],
        compiler_params=pltpu.CompilerParams(vmem_limit_bytes=VMEM_LIMIT),
        cost_estimate=pl.CostEstimate(
            flops=2 * AO_DEV * math.prod(shape) * integrals.shape[2],
            bytes_accessed=2 * (integrals.size + 3 * own.size + 4 * math.prod(shape)),
            transcendentals=0,
        ),
        name="transform",
    )(meta, integrals, prev, own, following)


def pairs_kernel(pairs, used, meta, *refs):
    blocks = {s: refs[i * CHUNKS : (i + 1) * CHUNKS] for i, s in enumerate(used)}
    keep, give, grams = refs[len(used) * CHUNKS :]
    here, aux, orb = meta[0], meta[1], meta[2]

    def product(left, right):
        total = None
        for a, b in zip(blocks[left], blocks[right]):
            for p in range(a.shape[0]):
                part = lax.dot_general(
                    a[p], b[p], (((1,), (1,)), ((), ())), preferred_element_type=jnp.float32
                )
                total = part if total is None else total + part
        return total.reshape(grams.shape[1:])

    for bit in (0, 1):
        mine = [(k, a, b) for k, (a, b) in enumerate(pairs) if (a ^ b) >> 1 == bit]
        upper = (here >> bit) & 1
        for k, a, b in mine:

            @pl.when(upper == 0)
            def _(k=k, a=a, b=b):
                grams[k] = product(a, b)

            @pl.when(upper == 1)
            def _(k=k, a=a, b=b):
                grams[k] = product(b, a)

    for k in range(len(pairs)):
        for x in (0, 1):
            row = 2 * (aux ^ x)
            keep[x, k] = grams[k, row + orb]
            give[x, k] = grams[k, row + 1 - orb]


def pair_products(pairs, used, meta, blocks):
    shape = jax.ShapeDtypeStruct((2, len(pairs), BLOCK // 4, BLOCK), jnp.float32)
    vmem = pl.BlockSpec(memory_space=pltpu.VMEM)
    return pl.pallas_call(
        functools.partial(pairs_kernel, pairs, used),
        out_shape=[shape] * 2,
        in_specs=[pl.BlockSpec(memory_space=pltpu.SMEM)] + [vmem] * (len(used) * CHUNKS),
        out_specs=[vmem] * 2,
        scratch_shapes=[pltpu.VMEM((len(pairs), 4, BLOCK // 4, BLOCK), jnp.float32)],
        compiler_params=pltpu.CompilerParams(vmem_limit_bytes=VMEM_LIMIT),
        cost_estimate=pl.CostEstimate(
            flops=2 * len(pairs) * BLOCK * CHUNKS * blocks[0][0].size,
            bytes_accessed=2 * len(used) * CHUNKS * blocks[0][0].size + 16 * shape.size,
            transcendentals=0,
        ),
        name="pairs",
    )(meta, *[part for s in used for part in blocks[s]])


def spread_kernel(factor, place, keep0, got0, far0, keep1, got1, far1, out, sums):
    early = keep0.shape[1]
    sums[:early] = (keep0[0] + got0[0] + far0[...].astype(jnp.float32)) * factor
    sums[early:] = (keep1[0] + got1[0] + far1[...].astype(jnp.float32)) * factor
    rows, slots, width = out.shape
    slot = lax.broadcasted_iota(jnp.int32, (slots, width), 0)
    source = jnp.zeros((slots, width), jnp.int32)
    for s in range(slots):
        source = jnp.where(slot == s, place[s], source)
    masks = [source == k for k in range(sums.shape[0])]

    def one(m, carry):
        row = jnp.zeros((slots, width), jnp.float32)
        for k, mask in enumerate(masks):
            values = jnp.broadcast_to(sums[k, pl.ds(m, 1), :], (slots, width))
            row = jnp.where(mask, values, row)
        out[m] = row
        return carry

    lax.fori_loop(0, rows, one, 0, unroll=8)


def spread(factor, place, early, late):
    rows = BLOCK // 4
    slots = place.shape[0]
    vmem = pl.BlockSpec(memory_space=pltpu.VMEM)
    return pl.pallas_call(
        functools.partial(spread_kernel, factor),
        out_shape=jax.ShapeDtypeStruct((rows, slots, BLOCK), jnp.float32),
        in_specs=[pl.BlockSpec(memory_space=pltpu.SMEM)] + [vmem] * 6,
        out_specs=vmem,
        scratch_shapes=[pltpu.VMEM((len(ALL_PAIRS), rows, BLOCK), jnp.float32)],
        compiler_params=pltpu.CompilerParams(vmem_limit_bytes=VMEM_LIMIT),
        cost_estimate=pl.CostEstimate(
            flops=6 * rows * slots * BLOCK, bytes_accessed=4 * rows * slots * BLOCK, transcendentals=0
        ),
        name="spread",
    )(place, *early, *late)


SWAP = [(0, 1), (1, 0)]


def reduce_blocks(keep, give):
    got = lax.ppermute(give, "orb", SWAP)
    far = lax.ppermute(keep[1] + got[1], "aux", SWAP)
    return keep, got, far


def six_pair_body(integrals, coeffs, pair_blocks, pair_count, orbital_count):
    orb_local = coeffs.shape[1]
    width = orb_local // CHUNKS
    total_aux = integrals.shape[0] * lax.axis_size("aux")
    owners = lax.axis_size("ao")
    here, aux, orb = lax.axis_index("ao"), lax.axis_index("aux"), lax.axis_index("orb")
    up = [(i, i + 1) for i in range(owners - 1)]
    down = [(i + 1, i) for i in range(owners - 1)]

    parts = [lax.slice_in_dim(coeffs, c * width, (c + 1) * width, axis=1) for c in range(CHUNKS)]
    halos = [(lax.ppermute(part, "ao", up), lax.ppermute(part, "ao", down)) for part in parts]

    table = pair_blocks.reshape(owners, -1, 2)
    slots = table.shape[1]
    wanted = jnp.max(jnp.where(table // AO_DEV == here, table % AO_DEV, 0), axis=(1, 2))
    partners = here ^ jnp.arange(owners, dtype=jnp.int32)
    wanted = wanted[partners]
    counts = lax.dynamic_slice_in_dim(orbital_count, here * AO_DEV, AO_DEV) - orb * orb_local

    blocks = [[] for _ in range(owners)]
    for c, (part, (prev, following)) in enumerate(zip(parts, halos)):
        meta = jnp.concatenate([wanted, counts - c * width]).astype(jnp.int32)
        for s, piece in enumerate(transform(meta, integrals, prev, part, following)):
            blocks[s].append(piece)

    def fetch(s):
        swap = [(j, j ^ s) for j in range(owners)]
        return [lax.ppermute(piece, "ao", swap) for piece in blocks[s]]

    got = [blocks[0], None, None, None]
    got[2] = fetch(2)
    got[1] = fetch(1)
    got[3] = fetch(3)

    position = jnp.stack([here, aux, orb]).astype(jnp.int32)
    early = reduce_blocks(*pair_products(EARLY_PAIRS, (0, 1, 2), position, got))
    late = reduce_blocks(*pair_products(LATE_PAIRS, (0, 1, 2, 3), position, got))

    owned = lax.dynamic_index_in_dim(table, here, 0, keepdims=False) // AO_DEV ^ here
    lower, upper = jnp.min(owned, axis=1), jnp.max(owned, axis=1)
    place = jnp.full((slots,), len(ALL_PAIRS), jnp.int32)
    for k, (a, b) in enumerate(ALL_PAIRS):
        place = jnp.where((lower == a) & (upper == b), k, place)
    place = jnp.where(jnp.arange(slots) < pair_count[here], place, len(ALL_PAIRS))
    return spread(1.0 / math.sqrt(total_aux * ORBS), place, early, late)


def solution(mesh):
    sizes = dict(mesh.shape)
    body = general_body
    if sizes["ao"] == 4 and sizes["aux"] == 2 and sizes["orb"] == 2:
        body = six_pair_body
    return jax.shard_map(
        body,
        mesh=mesh,
        in_specs=(
            P(("grp", "aux"), "ao", None),
            P(("grp", "ao"), "orb"),
            P("grp", None),
            P("grp"),
            P("grp"),
        ),
        out_specs=P(("aux", "orb"), ("grp", "ao"), None),
        check_vma=False,
    )
```

```python
import functools
import math

import jax
import jax.numpy as jnp
from jax import lax
from jax.experimental import pallas as pl
from jax.experimental.pallas import tpu as pltpu
from jax.sharding import PartitionSpec as P

BLOCK = 256
AO_DEV = 2
WIN = 5
ORBS = 1024
CHUNKS = 2
VMEM_LIMIT = 40 * 1024 * 1024


def with_halo(cells, sides, width):
    for axis, dim in sides:
        count = lax.axis_size(axis)
        ends = count - 1
        head = lax.slice_in_dim(cells, 0, width, axis=dim)
        tail = lax.slice_in_dim(cells, cells.shape[dim] - width, cells.shape[dim], axis=dim)
        cells = jnp.concatenate(
            [
                lax.ppermute(tail, axis, [(i, (i + 1) % count) for i in range(ends)]),
                cells,
                lax.ppermute(head, axis, [((i + 1) % count, i) for i in range(ends)]),
            ],
            axis=dim,
        )
    return cells


def general_body(integrals, coeffs, pair_blocks, pair_count, orbital_count):
    orb_local = coeffs.shape[1]
    aux_devices = lax.axis_size("aux")
    total_aux = integrals.shape[0] * aux_devices
    rim = WIN // 2 * BLOCK
    extended = with_halo(coeffs, (("ao", 0),), rim)
    ao_here = lax.axis_index("ao")
    orbital_ids = lax.axis_index("orb") * orb_local + jnp.arange(orb_local, dtype=jnp.int32)
    pieces = []
    for offset in range(AO_DEV):
        slab = integrals[:, offset * BLOCK : (offset + 1) * BLOCK, :]
        slot_range = extended[offset * BLOCK : offset * BLOCK + WIN * BLOCK]
        values = jnp.einsum("pml,li->pmi", slab, slot_range, preferred_element_type=jnp.float32)
        limit = orbital_count[ao_here * AO_DEV + offset]
        values = jnp.where((orbital_ids < limit)[None, None, :], values, 0.0)
        pieces.append(values.astype(jnp.bfloat16))
    transformed = jnp.stack(pieces)
    owners = lax.axis_size("ao")
    table = pair_blocks.reshape(owners, -1, 2)
    slots = table.shape[1]
    live = jnp.arange(slots, dtype=jnp.int32)[None, :] < pair_count[:, None]
    touched = live[:, :, None] & (table // AO_DEV == ao_here)
    wanted = jnp.max(jnp.where(touched, table % AO_DEV, 0), axis=(1, 2))
    outgoing = transformed[wanted]
    received = lax.all_to_all(outgoing, "ao", split_axis=0, concat_axis=0, tiled=True)
    owned = table[ao_here]
    factor = 1.0 / math.sqrt(total_aux * ORBS)
    weights = jnp.where(live[ao_here], factor, 0.0).astype(jnp.float32)
    left_source = owned[:, 0] // AO_DEV
    right_source = owned[:, 1] // AO_DEV
    right_factors = received[right_source]
    lefts = received[left_source]
    term = jnp.einsum("spmi,spni->msn", lefts, right_factors, preferred_element_type=jnp.float32)
    return lax.psum_scatter(
        term * weights[None, :, None], ("aux", "orb"), scatter_dimension=0, tiled=True
    )


EARLY_PAIRS = ((0, 1), (0, 2), (1, 2))
LATE_PAIRS = ((0, 3), (1, 3), (2, 3))
ALL_PAIRS = EARLY_PAIRS + LATE_PAIRS


def dot(a, b):
    return jnp.dot(a, b, preferred_element_type=jnp.float32)


def central_kernel(integrals, own, *outs):
    mid = AO_DEV * BLOCK
    width = own.shape[1] // len(outs)
    for offset in range(AO_DEV):
        low = mid - offset * BLOCK
        for p in range(integrals.shape[0]):
            slab = integrals[p, offset * BLOCK : (offset + 1) * BLOCK, low : low + mid]
            for c, out in enumerate(outs):
                out[offset, p] = dot(slab, own[:, c * width : (c + 1) * width])


def central(integrals, own):
    shape = (AO_DEV, integrals.shape[0], BLOCK, own.shape[1] // CHUNKS)
    vmem = pl.BlockSpec(memory_space=pltpu.VMEM)
    return pl.pallas_call(
        central_kernel,
        out_shape=[jax.ShapeDtypeStruct(shape, jnp.float32)] * CHUNKS,
        in_specs=[vmem] * 2,
        out_specs=[vmem] * CHUNKS,
        cost_estimate=pl.CostEstimate(
            flops=2 * integrals.size // WIN * AO_DEV * own.shape[1],
            bytes_accessed=2 * integrals.size + 2 * own.size + 4 * CHUNKS * math.prod(shape),
            transcendentals=0,
        ),
        compiler_params=pltpu.CompilerParams(vmem_limit_bytes=VMEM_LIMIT),
        name="central",
    )(integrals, own)


def transform_kernel(meta, integrals, centre, outer, inner, out0, out1, out2, out3, half):
    columns = outer.shape[1]
    mid = AO_DEV * BLOCK

    def rims(prev, following):
        ids = lax.broadcasted_iota(jnp.int32, (BLOCK, columns), 1)
        for offset in range(AO_DEV):
            low = mid - offset * BLOCK
            for p in range(integrals.shape[0]):
                slab = integrals[p, offset * BLOCK : (offset + 1) * BLOCK, :]
                values = centre[offset, p]
                values += dot(slab[:, :low], prev[offset * BLOCK :, :])
                values += dot(slab[:, low + mid :], following[: (offset + 1) * BLOCK, :])
                half[offset, p] = jnp.where(ids < meta[4 + offset], values, 0.0).astype(jnp.bfloat16)

    odd = meta[6] & 1
    pl.when(odd == 0)(lambda: rims(inner, outer))
    pl.when(odd == 1)(lambda: rims(outer, inner))
    for s, out in enumerate((out0, out1, out2, out3)):
        out[...] = half[meta[s]]


def transform(meta, integrals, centre, outer, inner):
    shape = (integrals.shape[0], BLOCK, outer.shape[1])
    vmem = pl.BlockSpec(memory_space=pltpu.VMEM)
    return pl.pallas_call(
        transform_kernel,
        out_shape=[jax.ShapeDtypeStruct(shape, jnp.bfloat16)] * 4,
        in_specs=[pl.BlockSpec(memory_space=pltpu.SMEM)] + [vmem] * 4,
        out_specs=[vmem] * 4,
        scratch_shapes=[pltpu.VMEM((AO_DEV, *shape), jnp.bfloat16)],
        compiler_params=pltpu.CompilerParams(vmem_limit_bytes=VMEM_LIMIT),
        cost_estimate=pl.CostEstimate(
            flops=2 * AO_DEV * math.prod(shape) * integrals.shape[2] * 3 // WIN,
            bytes_accessed=2 * (integrals.size + 2 * outer.size + 4 * math.prod(shape)) + 4 * centre.size,
            transcendentals=0,
        ),
        name="transform",
    )(meta, integrals, centre, outer, inner)


def pairs_kernel(pairs, used, tied, meta, *refs):
    blocks = {s: refs[i * CHUNKS : (i + 1) * CHUNKS] for i, s in enumerate(used)}
    keep, give = refs[len(used) * CHUNKS + tied :][:2]
    grams = refs[-1]
    here, aux, orb = meta[0], meta[1], meta[2]

    def product(left, right):
        total = None
        for a, b in zip(blocks[left], blocks[right]):
            for p in range(a.shape[0]):
                part = lax.dot_general(
                    a[p], b[p], (((1,), (1,)), ((), ())), preferred_element_type=jnp.float32
                )
                total = part if total is None else total + part
        return total.reshape(grams.shape[1:])

    for bit in (0, 1):
        mine = [(k, a, b) for k, (a, b) in enumerate(pairs) if (a ^ b) >> 1 == bit]
        upper = (here >> bit) & 1
        for k, a, b in mine:

            @pl.when(upper == 0)
            def _(k=k, a=a, b=b):
                grams[k] = product(a, b)

            @pl.when(upper == 1)
            def _(k=k, a=a, b=b):
                grams[k] = product(b, a)

    for k in range(len(pairs)):
        for x in (0, 1):
            row = 2 * (aux ^ x)
            keep[x, k] = grams[k, row + orb]
            give[x, k] = grams[k, row + 1 - orb]


def pair_products(pairs, used, meta, blocks, tied=()):
    shape = jax.ShapeDtypeStruct((2, len(pairs), BLOCK // 4, BLOCK), jnp.float32)
    vmem = pl.BlockSpec(memory_space=pltpu.VMEM)
    anywhere = pl.BlockSpec(memory_space=pl.ANY)
    first = 1 + len(used) * CHUNKS
    return pl.pallas_call(
        functools.partial(pairs_kernel, pairs, used, len(tied)),
        out_shape=[shape] * 2 + [jax.ShapeDtypeStruct(t.shape, t.dtype) for t in tied],
        in_specs=[pl.BlockSpec(memory_space=pltpu.SMEM)]
        + [vmem] * (len(used) * CHUNKS)
        + [anywhere] * len(tied),
        out_specs=[vmem] * 2 + [anywhere] * len(tied),
        scratch_shapes=[pltpu.VMEM((len(pairs), 4, BLOCK // 4, BLOCK), jnp.float32)],
        input_output_aliases={first + i: 2 + i for i in range(len(tied))},
        compiler_params=pltpu.CompilerParams(vmem_limit_bytes=VMEM_LIMIT),
        cost_estimate=pl.CostEstimate(
            flops=2 * len(pairs) * BLOCK * CHUNKS * blocks[0][0].size,
            bytes_accessed=2 * len(used) * CHUNKS * blocks[0][0].size + 16 * shape.size,
            transcendentals=0,
        ),
        name="pairs",
    )(meta, *[part for s in used for part in blocks[s]], *tied)


def spread_kernel(factor, place, keep0, got0, far0, keep1, got1, far1, out, sums):
    early = keep0.shape[1]
    sums[:early] = (keep0[0] + got0[0] + far0[...].astype(jnp.float32)) * factor
    sums[early:] = (keep1[0] + got1[0] + far1[...].astype(jnp.float32)) * factor
    rows, slots, width = out.shape
    slot = lax.broadcasted_iota(jnp.int32, (slots, width), 0)
    source = jnp.zeros((slots, width), jnp.int32)
    for s in range(slots):
        source = jnp.where(slot == s, place[s], source)
    masks = [source == k for k in range(sums.shape[0])]

    def one(m, carry):
        row = jnp.zeros((slots, width), jnp.float32)
        for k, mask in enumerate(masks):
            values = jnp.broadcast_to(sums[k, pl.ds(m, 1), :], (slots, width))
            row = jnp.where(mask, values, row)
        out[m] = row
        return carry

    lax.fori_loop(0, rows, one, 0, unroll=8)


def spread(factor, place, early, late):
    rows = BLOCK // 4
    slots = place.shape[0]
    vmem = pl.BlockSpec(memory_space=pltpu.VMEM)
    return pl.pallas_call(
        functools.partial(spread_kernel, factor),
        out_shape=jax.ShapeDtypeStruct((rows, slots, BLOCK), jnp.float32),
        in_specs=[pl.BlockSpec(memory_space=pltpu.SMEM)] + [vmem] * 6,
        out_specs=vmem,
        scratch_shapes=[pltpu.VMEM((len(ALL_PAIRS), rows, BLOCK), jnp.float32)],
        compiler_params=pltpu.CompilerParams(vmem_limit_bytes=VMEM_LIMIT),
        cost_estimate=pl.CostEstimate(
            flops=6 * rows * slots * BLOCK, bytes_accessed=4 * rows * slots * BLOCK, transcendentals=0
        ),
        name="spread",
    )(place, *early, *late)


SWAP = [(0, 1), (1, 0)]


def reduce_blocks(keep, give):
    got = lax.ppermute(give, "orb", SWAP)
    far = lax.ppermute(keep[1] + got[1], "aux", SWAP)
    return keep, got, far


def six_pair_body(integrals, coeffs, pair_blocks, pair_count, orbital_count):
    orb_local = coeffs.shape[1]
    width = orb_local // CHUNKS
    total_aux = integrals.shape[0] * lax.axis_size("aux")
    owners = lax.axis_size("ao")
    here, aux, orb = lax.axis_index("ao"), lax.axis_index("aux"), lax.axis_index("orb")
    outside = [(0, 1), (1, 0), (2, 3), (3, 2)]
    inside = [(1, 2), (2, 1)]

    parts = [lax.slice_in_dim(coeffs, c * width, (c + 1) * width, axis=1) for c in range(CHUNKS)]
    halos = [(lax.ppermute(part, "ao", inside), lax.ppermute(part, "ao", outside)) for part in parts]
    centres = central(integrals, coeffs)

    table = pair_blocks.reshape(owners, -1, 2)
    slots = table.shape[1]
    wanted = jnp.max(jnp.where(table // AO_DEV == here, table % AO_DEV, 0), axis=(1, 2))
    partners = here ^ jnp.arange(owners, dtype=jnp.int32)
    wanted = wanted[partners]
    counts = lax.dynamic_slice_in_dim(orbital_count, here * AO_DEV, AO_DEV) - orb * orb_local

    blocks = [[] for _ in range(owners)]
    for c, (inner, outer) in enumerate(halos):
        meta = jnp.concatenate([wanted, counts - c * width, here[None]]).astype(jnp.int32)
        for s, piece in enumerate(transform(meta, integrals, centres[c], outer, inner)):
            blocks[s].append(piece)

    def fetch(s, piece):
        return lax.ppermute(piece, "ao", [(j, j ^ s) for j in range(owners)])

    position = jnp.stack([here, aux, orb]).astype(jnp.int32)
    got = [blocks[0], [], [], []]
    for c in range(CHUNKS):
        got[2].append(fetch(2, blocks[2][c]))
        got[1].append(fetch(1, blocks[1][c]))
    got[3] = [fetch(3, piece) for piece in blocks[3][:-1]]
    keep, give, last = pair_products(EARLY_PAIRS, (0, 1, 2), position, got, blocks[3][-1:])
    got[3].append(fetch(3, last))
    early = reduce_blocks(keep, give)
    late = reduce_blocks(*pair_products(LATE_PAIRS, (0, 1, 2, 3), position, got))

    owned = lax.dynamic_index_in_dim(table, here, 0, keepdims=False) // AO_DEV ^ here
    lower, upper = jnp.min(owned, axis=1), jnp.max(owned, axis=1)
    place = jnp.full((slots,), len(ALL_PAIRS), jnp.int32)
    for k, (a, b) in enumerate(ALL_PAIRS):
        place = jnp.where((lower == a) & (upper == b), k, place)
    place = jnp.where(jnp.arange(slots) < pair_count[here], place, len(ALL_PAIRS))
    return spread(1.0 / math.sqrt(total_aux * ORBS), place, early, late)


def solution(mesh):
    sizes = dict(mesh.shape)
    body = general_body
    if sizes["ao"] == 4 and sizes["aux"] == 2 and sizes["orb"] == 2:
        body = six_pair_body
    return jax.shard_map(
        body,
        mesh=mesh,
        in_specs=(
            P(("grp", "aux"), "ao", None),
            P(("grp", "ao"), "orb"),
            P("grp", None),
            P("grp"),
            P("grp"),
        ),
        out_specs=P(("aux", "orb"), ("grp", "ao"), None),
        check_vma=False,
    )
```

```python
import functools
import math

import jax
import jax.numpy as jnp
from jax import lax
from jax.experimental import pallas as pl
from jax.experimental.pallas import tpu as pltpu
from jax.sharding import PartitionSpec as P

BLOCK = 256
AO_DEV = 2
WIN = 5
ORBS = 1024
CHUNKS = 2
SPREAD_STEPS = 4
SPREAD_STEPS = 4
SPREAD_STEPS = 4
SPREAD_STEPS = 4
SPREAD_STEPS = 4
SPREAD_STEPS = 4
VMEM_LIMIT = 40 * 1024 * 1024


def with_halo(cells, sides, width):
    for axis, dim in sides:
        count = lax.axis_size(axis)
        ends = count - 1
        head = lax.slice_in_dim(cells, 0, width, axis=dim)
        tail = lax.slice_in_dim(cells, cells.shape[dim] - width, cells.shape[dim], axis=dim)
        cells = jnp.concatenate(
            [
                lax.ppermute(tail, axis, [(i, (i + 1) % count) for i in range(ends)]),
                cells,
                lax.ppermute(head, axis, [((i + 1) % count, i) for i in range(ends)]),
            ],
            axis=dim,
        )
    return cells


def general_body(integrals, coeffs, pair_blocks, pair_count, orbital_count):
    orb_local = coeffs.shape[1]
    aux_devices = lax.axis_size("aux")
    total_aux = integrals.shape[0] * aux_devices
    rim = WIN // 2 * BLOCK
    extended = with_halo(coeffs, (("ao", 0),), rim)
    ao_here = lax.axis_index("ao")
    orbital_ids = lax.axis_index("orb") * orb_local + jnp.arange(orb_local, dtype=jnp.int32)
    pieces = []
    for offset in range(AO_DEV):
        slab = integrals[:, offset * BLOCK : (offset + 1) * BLOCK, :]
        slot_range = extended[offset * BLOCK : offset * BLOCK + WIN * BLOCK]
        values = jnp.einsum("pml,li->pmi", slab, slot_range, preferred_element_type=jnp.float32)
        limit = orbital_count[ao_here * AO_DEV + offset]
        values = jnp.where((orbital_ids < limit)[None, None, :], values, 0.0)
        pieces.append(values.astype(jnp.bfloat16))
    transformed = jnp.stack(pieces)
    owners = lax.axis_size("ao")
    table = pair_blocks.reshape(owners, -1, 2)
    slots = table.shape[1]
    live = jnp.arange(slots, dtype=jnp.int32)[None, :] < pair_count[:, None]
    touched = live[:, :, None] & (table // AO_DEV == ao_here)
    wanted = jnp.max(jnp.where(touched, table % AO_DEV, 0), axis=(1, 2))
    outgoing = transformed[wanted]
    received = lax.all_to_all(outgoing, "ao", split_axis=0, concat_axis=0, tiled=True)
    owned = table[ao_here]
    factor = 1.0 / math.sqrt(total_aux * ORBS)
    weights = jnp.where(live[ao_here], factor, 0.0).astype(jnp.float32)
    left_source = owned[:, 0] // AO_DEV
    right_source = owned[:, 1] // AO_DEV
    right_factors = received[right_source]
    lefts = received[left_source]
    term = jnp.einsum("spmi,spni->msn", lefts, right_factors, preferred_element_type=jnp.float32)
    return lax.psum_scatter(
        term * weights[None, :, None], ("aux", "orb"), scatter_dimension=0, tiled=True
    )


EARLY_PAIRS = ((0, 1), (0, 2), (1, 2))
LATE_PAIRS = ((0, 3), (1, 3), (2, 3))
ALL_PAIRS = EARLY_PAIRS + LATE_PAIRS
GROUPS = 4
SWAP = [(0, 1), (1, 0)]
OUTSIDE = [(0, 1), (1, 0), (2, 3), (3, 2)]
INSIDE = [(1, 2), (2, 1)]

IN_HBM = pl.BlockSpec(memory_space=pltpu.HBM)
IN_VMEM = pl.BlockSpec(memory_space=pltpu.VMEM)
IN_SMEM = pl.BlockSpec(memory_space=pltpu.SMEM)


def like(shape, dtype):
    return jax.ShapeDtypeStruct(shape, dtype)


def local_call(kernel, name, out_shape, in_specs, out_specs, flops, scratch=()):
    moved = sum(math.prod(o.shape) * o.dtype.itemsize for o in out_shape)
    return pl.pallas_call(
        kernel,
        out_shape=out_shape,
        in_specs=in_specs,
        out_specs=out_specs,
        scratch_shapes=list(scratch),
        compiler_params=pltpu.CompilerParams(vmem_limit_bytes=VMEM_LIMIT),
        cost_estimate=pl.CostEstimate(flops=flops, bytes_accessed=2 * moved, transcendentals=0),
        name=name,
    )


def dot(a, b):
    return jnp.dot(a, b, preferred_element_type=jnp.float32)


def central_kernel(position, table, counts, integrals, *refs):
    parts, outs, scalars = refs[:CHUNKS], refs[CHUNKS:-1], refs[-1]
    mid = AO_DEV * BLOCK
    here, orb = position[0], position[2]
    slots = table.shape[1] // GROUPS
    for s in range(GROUPS):
        first = (here ^ s) * slots
        found = jnp.int32(0)
        for k in range(slots):
            for side in (0, 1):
                block = table[side, first + k]
                found = jnp.where(block // AO_DEV == here, block % AO_DEV, found)
        scalars[s] = found
    for offset in range(AO_DEV):
        scalars[GROUPS + offset] = counts[here * AO_DEV + offset] - orb * CHUNKS * parts[0].shape[1]
    for offset in range(AO_DEV):
        low = mid - offset * BLOCK
        for p in range(integrals.shape[0]):
            slab = integrals[p, offset * BLOCK : (offset + 1) * BLOCK, low : low + mid]
            for part, out in zip(parts, outs):
                out[offset, p] = dot(slab, part[...])


def central(position, table, counts, integrals, parts):
    shape = (AO_DEV, integrals.shape[0], BLOCK, parts[0].shape[1])
    *out, scalars = local_call(
        central_kernel,
        "central",
        [like(shape, jnp.float32)] * CHUNKS + [like((8,), jnp.int32)],
        [IN_SMEM] * 3 + [IN_VMEM] * (1 + CHUNKS),
        [IN_VMEM] * CHUNKS + [IN_SMEM],
        4 * integrals.size // WIN * CHUNKS * parts[0].shape[1],
    )(position, table, counts, integrals, *parts)
    return out, scalars


def transform_kernel(start, position, scalars, integrals, centre, outer, inner, *refs):
    outs, half = refs[:-1], refs[-1]
    columns = outer.shape[1]
    mid = AO_DEV * BLOCK

    def rims(prev, following):
        ids = start + lax.broadcasted_iota(jnp.int32, (BLOCK, columns), 1)
        for offset in range(AO_DEV):
            low = mid - offset * BLOCK
            for p in range(integrals.shape[0]):
                slab = integrals[p, offset * BLOCK : (offset + 1) * BLOCK, :]
                values = centre[offset, p]
                values += dot(slab[:, :low], prev[offset * BLOCK :, :])
                values += dot(slab[:, low + mid :], following[: (offset + 1) * BLOCK, :])
                live = ids < scalars[GROUPS + offset]
                half[offset, p] = jnp.where(live, values, 0.0).astype(jnp.bfloat16)

    odd = position[0] & 1
    pl.when(odd == 0)(lambda: rims(inner, outer))
    pl.when(odd == 1)(lambda: rims(outer, inner))
    for s, out in enumerate(outs[: GROUPS - 1]):
        out[...] = half[scalars[s]]
    first = 0
    for out in outs[GROUPS - 1 :]:
        for p in range(out.shape[0]):
            out[p] = half[scalars[GROUPS - 1], first + p]
        first += out.shape[0]


def transform(start, position, scalars, integrals, centre, outer, inner, cuts):
    aux_here = integrals.shape[0]
    shape = (BLOCK, outer.shape[1])
    return local_call(
        functools.partial(transform_kernel, start),
        "transform",
        [like((n, *shape), jnp.bfloat16) for n in [aux_here] * (GROUPS - 1) + cuts],
        [IN_SMEM] * 2 + [IN_VMEM] * 4,
        [IN_VMEM] * (GROUPS - 1 + len(cuts)),
        6 * AO_DEV * integrals.size * shape[1] // WIN,
        [pltpu.VMEM((AO_DEV, aux_here, *shape), jnp.bfloat16)],
    )(position, scalars, integrals, centre, outer, inner)


def form_pairs(pairs, position, blocks, keep, give, grams):
    here, aux, orb = position[0], position[1], position[2]
    slices = [[(ref, p) for ref in block for p in range(ref.shape[0])] for block in blocks]

    def product(left, right):
        total = None
        for (a, i), (b, j) in zip(slices[left], slices[right]):
            part = lax.dot_general(
                a[i], b[j], (((1,), (1,)), ((), ())), preferred_element_type=jnp.float32
            )
            total = part if total is None else total + part
        return total.reshape(grams.shape[1:])

    for bit in (0, 1):
        mine = [(k, a, b) for k, (a, b) in enumerate(pairs) if (a ^ b) >> 1 == bit]
        upper = (here >> bit) & 1

        @pl.when(upper == 0)
        def _(mine=mine):
            for k, a, b in mine:
                grams[k] = product(a, b)

        @pl.when(upper == 1)
        def _(mine=mine):
            for k, a, b in mine:
                grams[k] = product(b, a)

    for k in range(len(pairs)):
        for x in (0, 1):
            row = 2 * (aux ^ x)
            keep[x, k] = grams[k, row + orb]
            give[k][x] = grams[k, row + 1 - orb]


def early_kernel(position, table, live, *refs):
    used = 3 * CHUNKS
    blocks = [refs[i : i + CHUNKS] for i in range(0, used, CHUNKS)]
    keep, *give, place, grams = refs[used:]
    here = position[0]
    slots = place.shape[0]
    for s in range(slots):
        a = table[0, here * slots + s] // AO_DEV ^ here
        b = table[1, here * slots + s] // AO_DEV ^ here
        low, high = jnp.minimum(a, b), jnp.maximum(a, b)
        index = jnp.where(high == 3, low + 3, jnp.where(high == 2, low + 1, 0))
        place[s] = jnp.where(s < live[here], index, len(ALL_PAIRS))
    form_pairs(EARLY_PAIRS, position, blocks, keep, give, grams)


def late_kernel(sizes, position, *refs):
    blocks = []
    for size in sizes:
        blocks.append(refs[:size])
        refs = refs[size:]
    keep, *give, grams = refs
    form_pairs(LATE_PAIRS, position, blocks, keep, give, grams)


def pair_flops(pairs, blocks):
    return 2 * len(pairs) * BLOCK * CHUNKS * blocks[0][0].size


def shares(pairs):
    rows = BLOCK // 4
    keep = like((2, len(pairs), rows, BLOCK), jnp.float32)
    give = like((2, rows, BLOCK), jnp.float32)
    return [keep] + [give] * len(pairs), pltpu.VMEM((len(pairs), 4, rows, BLOCK), jnp.float32)


def early_pairs(position, table, live, blocks):
    out, grams = shares(EARLY_PAIRS)
    keep, *give, place = local_call(
        early_kernel,
        "early_pairs",
        out + [like((table.shape[1] // GROUPS,), jnp.int32)],
        [IN_SMEM] * 3 + [IN_VMEM] * (3 * CHUNKS),
        [IN_VMEM] * len(out) + [IN_SMEM],
        pair_flops(EARLY_PAIRS, blocks),
        [grams],
    )(position, table, live, *[part for block in blocks for part in block])
    return keep, give, place


def late_pairs(position, blocks):
    out, grams = shares(LATE_PAIRS)
    sizes = [len(block) for block in blocks]
    keep, *give = local_call(
        functools.partial(late_kernel, sizes),
        "late_pairs",
        out,
        [IN_SMEM] + [IN_VMEM] * sum(sizes),
        [IN_VMEM] * len(out),
        pair_flops(LATE_PAIRS, blocks),
        [grams],
    )(position, *[part for block in blocks for part in block])
    return keep, give


def spread_kernel(factor, place, *refs):
    *parts, out, sums, rows, sems = refs
    half = len(parts) // 2
    k = 0
    for kept, far, *got in (parts[:half], parts[half:]):
        for i, other in enumerate(got):
            sums[k] = (kept[0, i] + other[0] + far[i].astype(jnp.float32)) * factor
            k += 1
    total, slots, width = out.shape
    slot = lax.broadcasted_iota(jnp.int32, (slots, width), 0)
    source = jnp.zeros((slots, width), jnp.int32)
    for s in range(slots):
        source = jnp.where(slot == s, place[s], source)
    masks = [source == k for k in range(sums.shape[0])]

    def one(m, carry):
        row = jnp.zeros((slots, width), jnp.float32)
        for k, mask in enumerate(masks):
            values = jnp.broadcast_to(sums[k, pl.ds(m, 1), :], (slots, width))
            row = jnp.where(mask, values, row)
        rows[m] = row
        return carry

    step = total // SPREAD_STEPS
    copies = []
    for i in range(SPREAD_STEPS):
        lax.fori_loop(i * step, (i + 1) * step, one, 0, unroll=8)
        part = pl.ds(i * step, step)
        copies.append(pltpu.make_async_copy(rows.at[part], out.at[part], sems.at[i]))
        copies[-1].start()
    for copy in copies:
        copy.wait()


def spread(factor, place, *parts):
    rows = BLOCK // 4
    shape = (rows, place.shape[0], BLOCK)
    parts = [array for kept, far, got in parts for array in (kept, far, *got)]
    return local_call(
        functools.partial(spread_kernel, factor),
        "spread",
        [like(shape, jnp.float32)],
        [IN_SMEM] + [IN_VMEM] * len(parts),
        [IN_HBM],
        6 * math.prod(shape),
        [
            pltpu.VMEM((len(ALL_PAIRS), rows, BLOCK), jnp.float32),
            pltpu.VMEM(shape, jnp.float32),
            pltpu.SemaphoreType.DMA((SPREAD_STEPS,)),
        ],
    )(place, *parts)[0]


def across(kept, give):
    got = [lax.ppermute(one, "orb", SWAP) for one in give]
    share = jnp.stack([kept[1, k] + other[1] for k, other in enumerate(got)])
    return got, lax.ppermute(share.astype(jnp.bfloat16), "aux", SWAP)


def six_pair_body(integrals, coeffs, pair_blocks, pair_count, orbital_count):
    width = coeffs.shape[1] // CHUNKS
    total_aux = integrals.shape[0] * lax.axis_size("aux")
    position = jnp.stack([lax.axis_index(axis) for axis in ("ao", "aux", "orb")]).astype(jnp.int32)
    table = pair_blocks.T

    parts = [lax.slice_in_dim(coeffs, c * width, (c + 1) * width, axis=1) for c in range(CHUNKS)]
    halos = [
        (lax.ppermute(part, "ao", INSIDE), lax.ppermute(part, "ao", OUTSIDE)) for part in parts
    ]
    centres, scalars = central(position, table, orbital_count, integrals, parts)

    aux_here = integrals.shape[0]
    cuts = [[aux_here]] * (CHUNKS - 1) + [[1] * aux_here]
    blocks = [[] for _ in range(GROUPS)]
    for c, (inner, outer) in enumerate(halos):
        pieces = transform(c * width, position, scalars, integrals, centres[c], outer, inner, cuts[c])
        for s in range(GROUPS - 1):
            blocks[s].append(pieces[s])
        blocks[-1] += pieces[GROUPS - 1 :]

    def fetch(s, piece):
        return lax.ppermute(piece, "ao", [(j, j ^ s) for j in range(GROUPS)])

    middle = [fetch(2, piece) for piece in blocks[2]]
    near = [fetch(1, piece) for piece in blocks[1]]
    last = [fetch(3, piece) for piece in blocks[3][:-1]]
    kept0, give0, place = early_pairs(position, table, pair_count, [blocks[0], near, middle])
    piece, kept0 = lax.optimization_barrier((blocks[3][-1], kept0))
    last.append(fetch(3, piece))
    got0, far0 = across(kept0, give0)
    factor = 1.0 / math.sqrt(total_aux * ORBS)
    kept1, give1 = late_pairs(position, [blocks[0], near, middle, last])
    got1, far1 = across(kept1, give1)
    return spread(factor, place, (kept0, far0, got0), (kept1, far1, got1))


def solution(mesh):
    sizes = dict(mesh.shape)
    body = general_body
    if sizes["ao"] == 4 and sizes["aux"] == 2 and sizes["orb"] == 2:
        body = six_pair_body
    return jax.shard_map(
        body,
        mesh=mesh,
        in_specs=(
            P(("grp", "aux"), "ao", None),
            P(("grp", "ao"), "orb"),
            P("grp", None),
            P("grp"),
            P("grp"),
        ),
        out_specs=P(("aux", "orb"), ("grp", "ao"), None),
        check_vma=False,
    )
```

```python
import functools
import math

import jax
import jax.numpy as jnp
from jax import lax
from jax.experimental import pallas as pl
from jax.experimental.pallas import tpu as pltpu
from jax.sharding import PartitionSpec as P

BLOCK = 256
AO_DEV = 2
WIN = 5
ORBS = 1024
CHUNKS = 2
SPREAD_STEPS = 4
SPREAD_STEPS = 4
SPREAD_STEPS = 4
SPREAD_STEPS = 4
SPREAD_STEPS = 4
SPREAD_STEPS = 4
VMEM_LIMIT = 40 * 1024 * 1024


def with_halo(cells, sides, width):
    for axis, dim in sides:
        count = lax.axis_size(axis)
        ends = count - 1
        head = lax.slice_in_dim(cells, 0, width, axis=dim)
        tail = lax.slice_in_dim(cells, cells.shape[dim] - width, cells.shape[dim], axis=dim)
        cells = jnp.concatenate(
            [
                lax.ppermute(tail, axis, [(i, (i + 1) % count) for i in range(ends)]),
                cells,
                lax.ppermute(head, axis, [((i + 1) % count, i) for i in range(ends)]),
            ],
            axis=dim,
        )
    return cells


def general_body(integrals, coeffs, pair_blocks, pair_count, orbital_count):
    orb_local = coeffs.shape[1]
    aux_devices = lax.axis_size("aux")
    total_aux = integrals.shape[0] * aux_devices
    rim = WIN // 2 * BLOCK
    extended = with_halo(coeffs, (("ao", 0),), rim)
    ao_here = lax.axis_index("ao")
    orbital_ids = lax.axis_index("orb") * orb_local + jnp.arange(orb_local, dtype=jnp.int32)
    pieces = []
    for offset in range(AO_DEV):
        slab = integrals[:, offset * BLOCK : (offset + 1) * BLOCK, :]
        slot_range = extended[offset * BLOCK : offset * BLOCK + WIN * BLOCK]
        values = jnp.einsum("pml,li->pmi", slab, slot_range, preferred_element_type=jnp.float32)
        limit = orbital_count[ao_here * AO_DEV + offset]
        values = jnp.where((orbital_ids < limit)[None, None, :], values, 0.0)
        pieces.append(values.astype(jnp.bfloat16))
    transformed = jnp.stack(pieces)
    owners = lax.axis_size("ao")
    table = pair_blocks.reshape(owners, -1, 2)
    slots = table.shape[1]
    live = jnp.arange(slots, dtype=jnp.int32)[None, :] < pair_count[:, None]
    touched = live[:, :, None] & (table // AO_DEV == ao_here)
    wanted = jnp.max(jnp.where(touched, table % AO_DEV, 0), axis=(1, 2))
    outgoing = transformed[wanted]
    received = lax.all_to_all(outgoing, "ao", split_axis=0, concat_axis=0, tiled=True)
    owned = table[ao_here]
    factor = 1.0 / math.sqrt(total_aux * ORBS)
    weights = jnp.where(live[ao_here], factor, 0.0).astype(jnp.float32)
    left_source = owned[:, 0] // AO_DEV
    right_source = owned[:, 1] // AO_DEV
    right_factors = received[right_source]
    lefts = received[left_source]
    term = jnp.einsum("spmi,spni->msn", lefts, right_factors, preferred_element_type=jnp.float32)
    return lax.psum_scatter(
        term * weights[None, :, None], ("aux", "orb"), scatter_dimension=0, tiled=True
    )


EARLY_PAIRS = ((0, 1), (0, 2), (1, 2))
LATE_PAIRS = ((0, 3), (1, 3), (2, 3))
ALL_PAIRS = EARLY_PAIRS + LATE_PAIRS
GROUPS = 4
SWAP = [(0, 1), (1, 0)]
OUTSIDE = [(0, 1), (1, 0), (2, 3), (3, 2)]
INSIDE = [(1, 2), (2, 1)]

IN_HBM = pl.BlockSpec(memory_space=pltpu.HBM)
IN_VMEM = pl.BlockSpec(memory_space=pltpu.VMEM)
IN_SMEM = pl.BlockSpec(memory_space=pltpu.SMEM)


def like(shape, dtype):
    return jax.ShapeDtypeStruct(shape, dtype)


def local_call(kernel, name, out_shape, in_specs, out_specs, flops, scratch=()):
    moved = sum(math.prod(o.shape) * o.dtype.itemsize for o in out_shape)
    return pl.pallas_call(
        kernel,
        out_shape=out_shape,
        in_specs=in_specs,
        out_specs=out_specs,
        scratch_shapes=list(scratch),
        compiler_params=pltpu.CompilerParams(vmem_limit_bytes=VMEM_LIMIT),
        cost_estimate=pl.CostEstimate(flops=flops, bytes_accessed=2 * moved, transcendentals=0),
        name=name,
    )


def dot(a, b):
    return jnp.dot(a, b, preferred_element_type=jnp.float32)


def central_kernel(position, table, counts, integrals, *refs):
    parts, outs, scalars = refs[:CHUNKS], refs[CHUNKS:-1], refs[-1]
    mid = AO_DEV * BLOCK
    here, orb = position[0], position[2]
    slots = table.shape[1] // GROUPS
    named = jnp.where(table[...] // AO_DEV == here, table[...] % AO_DEV, 0).astype(jnp.float32)
    owner = lax.broadcasted_iota(jnp.int32, table.shape, 1) // slots
    for s in range(GROUPS):
        scalars[s] = jnp.max(jnp.where(owner == here ^ s, named, 0.0)).astype(jnp.int32)
    for offset in range(AO_DEV):
        scalars[GROUPS + offset] = counts[here * AO_DEV + offset] - orb * CHUNKS * parts[0].shape[1]
    for offset in range(AO_DEV):
        low = mid - offset * BLOCK
        for p in range(integrals.shape[0]):
            slab = integrals[p, offset * BLOCK : (offset + 1) * BLOCK, low : low + mid]
            for part, out in zip(parts, outs):
                out[offset, p] = dot(slab, part[...])


def central(position, table, counts, integrals, parts):
    shape = (AO_DEV, integrals.shape[0], BLOCK, parts[0].shape[1])
    *out, scalars = local_call(
        central_kernel,
        "central",
        [like(shape, jnp.float32)] * CHUNKS + [like((8,), jnp.int32)],
        [IN_SMEM, IN_VMEM, IN_SMEM] + [IN_VMEM] * (1 + CHUNKS),
        [IN_VMEM] * CHUNKS + [IN_SMEM],
        4 * integrals.size // WIN * CHUNKS * parts[0].shape[1],
    )(position, table, counts, integrals, *parts)
    return out, scalars


def transform_kernel(start, position, scalars, integrals, centre, outer, inner, *refs):
    outs, half = refs[:-1], refs[-1]
    columns = outer.shape[1]
    mid = AO_DEV * BLOCK

    def rims(prev, following):
        ids = start + lax.broadcasted_iota(jnp.int32, (BLOCK, columns), 1)
        for offset in range(AO_DEV):
            low = mid - offset * BLOCK
            for p in range(integrals.shape[0]):
                slab = integrals[p, offset * BLOCK : (offset + 1) * BLOCK, :]
                values = centre[offset, p]
                values += dot(slab[:, :low], prev[offset * BLOCK :, :])
                values += dot(slab[:, low + mid :], following[: (offset + 1) * BLOCK, :])
                live = ids < scalars[GROUPS + offset]
                half[offset, p] = jnp.where(live, values, 0.0).astype(jnp.bfloat16)

    odd = position[0] & 1
    pl.when(odd == 0)(lambda: rims(inner, outer))
    pl.when(odd == 1)(lambda: rims(outer, inner))
    for s, out in enumerate(outs):
        out[...] = half[scalars[s]]


def transform(start, position, scalars, integrals, centre, outer, inner):
    shape = (integrals.shape[0], BLOCK, outer.shape[1])
    return local_call(
        functools.partial(transform_kernel, start),
        "transform",
        [like(shape, jnp.bfloat16)] * GROUPS,
        [IN_SMEM] * 2 + [IN_VMEM] * 4,
        [IN_VMEM] * GROUPS,
        6 * AO_DEV * math.prod(shape) * integrals.shape[2] // WIN,
        [pltpu.VMEM((AO_DEV, *shape), jnp.bfloat16)],
    )(position, scalars, integrals, centre, outer, inner)


def form_pairs(pairs, position, blocks, grams):
    here = position[0]
    slices = [[(ref, p) for ref in block for p in range(ref.shape[0])] for block in blocks]

    def product(left, right):
        total = None
        for (a, i), (b, j) in zip(slices[left], slices[right]):
            part = lax.dot_general(
                a[i], b[j], (((1,), (1,)), ((), ())), preferred_element_type=jnp.float32
            )
            total = part if total is None else total + part
        return total.reshape(grams.shape[1:])

    for bit in (0, 1):
        mine = [(k, a, b) for k, (a, b) in enumerate(pairs) if (a ^ b) >> 1 == bit]
        upper = (here >> bit) & 1

        @pl.when(upper == 0)
        def _(mine=mine):
            for k, a, b in mine:
                grams[k] = product(a, b)

        @pl.when(upper == 1)
        def _(mine=mine):
            for k, a, b in mine:
                grams[k] = product(b, a)


def early_kernel(position, table, live, *refs):
    used = 3 * CHUNKS
    blocks = [refs[i : i + CHUNKS] for i in range(0, used, CHUNKS)]
    near, far, place, grams = refs[used:]
    here, aux, orb = position[0], position[1], position[2]
    slots = place.shape[0]
    for s in range(slots):
        a = table[0, here * slots + s] // AO_DEV ^ here
        b = table[1, here * slots + s] // AO_DEV ^ here
        low, high = jnp.minimum(a, b), jnp.maximum(a, b)
        index = jnp.where(high == 3, low + 3, jnp.where(high == 2, low + 1, 0))
        place[s] = jnp.where(s < live[here], index, len(ALL_PAIRS))
    form_pairs(EARLY_PAIRS, position, blocks, grams)
    for k in range(len(EARLY_PAIRS)):
        for core in (0, 1):
            near[core, k] = grams[k, 2 * aux + (orb ^ core)]
            far[core, k] = grams[k, 2 * (1 - aux) + (orb ^ core)].astype(jnp.bfloat16)


def late_kernel(position, *refs):
    used = GROUPS * CHUNKS
    blocks = [refs[i : i + CHUNKS] for i in range(0, used, CHUNKS)]
    keep, give, grams = refs[used:]
    aux, orb = position[1], position[2]
    form_pairs(LATE_PAIRS, position, blocks, grams)
    for k in range(len(LATE_PAIRS)):
        for chip in (0, 1):
            row = 2 * (aux ^ chip)
            keep[chip, k] = grams[k, row + orb]
            give[chip, k] = grams[k, row + 1 - orb]


def pair_flops(pairs, blocks):
    return 2 * len(pairs) * BLOCK * CHUNKS * blocks[0][0].size


def quarters(pairs):
    rows = BLOCK // 4
    return (2, len(pairs), rows, BLOCK), pltpu.VMEM((len(pairs), 4, rows, BLOCK), jnp.float32)


def early_pairs(position, table, live, blocks):
    shape, grams = quarters(EARLY_PAIRS)
    return local_call(
        early_kernel,
        "early_pairs",
        [
            like(shape, jnp.float32),
            like(shape, jnp.bfloat16),
            like((table.shape[1] // GROUPS,), jnp.int32),
        ],
        [IN_SMEM] * 3 + [IN_VMEM] * (3 * CHUNKS),
        [IN_VMEM] * 2 + [IN_SMEM],
        pair_flops(EARLY_PAIRS, blocks),
        [grams],
    )(position, table, live, *[part for block in blocks for part in block])


def late_pairs(position, blocks):
    shape, grams = quarters(LATE_PAIRS)
    return local_call(
        late_kernel,
        "late_pairs",
        [like(shape, jnp.float32)] * 2,
        [IN_SMEM] + [IN_VMEM] * (GROUPS * CHUNKS),
        [IN_VMEM] * 2,
        pair_flops(LATE_PAIRS, blocks),
        [grams],
    )(position, *[part for block in blocks for part in block])


def spread_kernel(factor, place, near0, far0, got0, near1, got1, far1, out, sums, rows, sems):
    early = near0.shape[1]
    sums[:early] = (near0[0] + far0[0].astype(jnp.float32) + got0[...]) * factor
    sums[early:] = (near1[0] + got1[0] + far1[...].astype(jnp.float32)) * factor
    total, slots, width = out.shape
    slot = lax.broadcasted_iota(jnp.int32, (slots, width), 0)
    source = jnp.zeros((slots, width), jnp.int32)
    for s in range(slots):
        source = jnp.where(slot == s, place[s], source)
    masks = [source == k for k in range(sums.shape[0])]

    def one(m, carry):
        row = jnp.zeros((slots, width), jnp.float32)
        for k, mask in enumerate(masks):
            values = jnp.broadcast_to(sums[k, pl.ds(m, 1), :], (slots, width))
            row = jnp.where(mask, values, row)
        rows[m] = row
        return carry

    step = total // SPREAD_STEPS
    copies = []
    for i in range(SPREAD_STEPS):
        lax.fori_loop(i * step, (i + 1) * step, one, 0, unroll=8)
        part = pl.ds(i * step, step)
        copies.append(pltpu.make_async_copy(rows.at[part], out.at[part], sems.at[i]))
        copies[-1].start()
    for copy in copies:
        copy.wait()


def spread(factor, place, *parts):
    rows = BLOCK // 4
    shape = (rows, place.shape[0], BLOCK)
    return local_call(
        functools.partial(spread_kernel, factor),
        "spread",
        [like(shape, jnp.float32)],
        [IN_SMEM] + [IN_VMEM] * len(parts),
        [IN_HBM],
        6 * math.prod(shape),
        [
            pltpu.VMEM((len(ALL_PAIRS), rows, BLOCK), jnp.float32),
            pltpu.VMEM(shape, jnp.float32),
            pltpu.SemaphoreType.DMA((SPREAD_STEPS,)),
        ],
    )(place, *parts)[0]


def six_pair_body(integrals, coeffs, pair_blocks, pair_count, orbital_count):
    width = coeffs.shape[1] // CHUNKS
    total_aux = integrals.shape[0] * lax.axis_size("aux")
    position = jnp.stack([lax.axis_index(axis) for axis in ("ao", "aux", "orb")]).astype(jnp.int32)
    table = pair_blocks.T

    parts = [lax.slice_in_dim(coeffs, c * width, (c + 1) * width, axis=1) for c in range(CHUNKS)]
    halos = [
        (lax.ppermute(part, "ao", INSIDE), lax.ppermute(part, "ao", OUTSIDE)) for part in parts
    ]
    centres, scalars = central(position, table, orbital_count, integrals, parts)

    blocks = [[] for _ in range(GROUPS)]
    for c, (inner, outer) in enumerate(halos):
        pieces = transform(c * width, position, scalars, integrals, centres[c], outer, inner)
        for block, piece in zip(blocks, pieces):
            block.append(piece)

    def fetch(s):
        swap = [(j, j ^ s) for j in range(GROUPS)]
        return [lax.ppermute(piece, "ao", swap) for piece in blocks[s]]

    got = [blocks[0], fetch(1), fetch(2)]
    near0, across0, place = early_pairs(position, table, pair_count, got)
    far0 = lax.ppermute(across0, "aux", SWAP)
    got.append(fetch(3))
    near1, give1 = late_pairs(position, got)
    got1 = lax.ppermute(give1, "orb", SWAP)
    far1 = lax.ppermute((near1[1] + got1[1]).astype(jnp.bfloat16), "aux", SWAP)
    got0 = lax.ppermute(near0[1] + far0[1].astype(jnp.float32), "orb", SWAP)
    factor = 1.0 / math.sqrt(total_aux * ORBS)
    return spread(factor, place, near0, far0, got0, near1, got1, far1)


def solution(mesh):
    sizes = dict(mesh.shape)
    body = general_body
    if sizes["ao"] == 4 and sizes["aux"] == 2 and sizes["orb"] == 2:
        body = six_pair_body
    return jax.shard_map(
        body,
        mesh=mesh,
        in_specs=(
            P(("grp", "aux"), "ao", None),
            P(("grp", "ao"), "orb"),
            P("grp", None),
            P("grp"),
            P("grp"),
        ),
        out_specs=P(("aux", "orb"), ("grp", "ao"), None),
        check_vma=False,
    )
```

```python
import functools
import math

import jax
import jax.numpy as jnp
from jax import lax
from jax.experimental import pallas as pl
from jax.experimental.pallas import tpu as pltpu
from jax.sharding import PartitionSpec as P

BLOCK = 256
AO_DEV = 2
WIN = 5
ORBS = 1024
CHUNKS = 2
SPREAD_STEPS = 4
SPREAD_STEPS = 4
SPREAD_STEPS = 4
SPREAD_STEPS = 4
SPREAD_STEPS = 4
SPREAD_STEPS = 4
VMEM_LIMIT = 40 * 1024 * 1024
LEAD_FLOPS = 1 << 32


def with_halo(cells, sides, width):
    for axis, dim in sides:
        count = lax.axis_size(axis)
        ends = count - 1
        head = lax.slice_in_dim(cells, 0, width, axis=dim)
        tail = lax.slice_in_dim(cells, cells.shape[dim] - width, cells.shape[dim], axis=dim)
        cells = jnp.concatenate(
            [
                lax.ppermute(tail, axis, [(i, (i + 1) % count) for i in range(ends)]),
                cells,
                lax.ppermute(head, axis, [((i + 1) % count, i) for i in range(ends)]),
            ],
            axis=dim,
        )
    return cells


def general_body(integrals, coeffs, pair_blocks, pair_count, orbital_count):
    orb_local = coeffs.shape[1]
    aux_devices = lax.axis_size("aux")
    total_aux = integrals.shape[0] * aux_devices
    rim = WIN // 2 * BLOCK
    extended = with_halo(coeffs, (("ao", 0),), rim)
    ao_here = lax.axis_index("ao")
    orbital_ids = lax.axis_index("orb") * orb_local + jnp.arange(orb_local, dtype=jnp.int32)
    pieces = []
    for offset in range(AO_DEV):
        slab = integrals[:, offset * BLOCK : (offset + 1) * BLOCK, :]
        slot_range = extended[offset * BLOCK : offset * BLOCK + WIN * BLOCK]
        values = jnp.einsum("pml,li->pmi", slab, slot_range, preferred_element_type=jnp.float32)
        limit = orbital_count[ao_here * AO_DEV + offset]
        values = jnp.where((orbital_ids < limit)[None, None, :], values, 0.0)
        pieces.append(values.astype(jnp.bfloat16))
    transformed = jnp.stack(pieces)
    owners = lax.axis_size("ao")
    table = pair_blocks.reshape(owners, -1, 2)
    slots = table.shape[1]
    live = jnp.arange(slots, dtype=jnp.int32)[None, :] < pair_count[:, None]
    touched = live[:, :, None] & (table // AO_DEV == ao_here)
    wanted = jnp.max(jnp.where(touched, table % AO_DEV, 0), axis=(1, 2))
    outgoing = transformed[wanted]
    received = lax.all_to_all(outgoing, "ao", split_axis=0, concat_axis=0, tiled=True)
    owned = table[ao_here]
    factor = 1.0 / math.sqrt(total_aux * ORBS)
    weights = jnp.where(live[ao_here], factor, 0.0).astype(jnp.float32)
    left_source = owned[:, 0] // AO_DEV
    right_source = owned[:, 1] // AO_DEV
    right_factors = received[right_source]
    lefts = received[left_source]
    term = jnp.einsum("spmi,spni->msn", lefts, right_factors, preferred_element_type=jnp.float32)
    return lax.psum_scatter(
        term * weights[None, :, None], ("aux", "orb"), scatter_dimension=0, tiled=True
    )


EARLY_PAIRS = ((0, 1), (0, 2), (1, 2))
LATE_PAIRS = ((0, 3), (1, 3), (2, 3))
ALL_PAIRS = EARLY_PAIRS + LATE_PAIRS
GROUPS = 4
SWAP = [(0, 1), (1, 0)]
OUTSIDE = [(0, 1), (1, 0), (2, 3), (3, 2)]
INSIDE = [(1, 2), (2, 1)]

IN_HBM = pl.BlockSpec(memory_space=pltpu.HBM)
IN_VMEM = pl.BlockSpec(memory_space=pltpu.VMEM)
IN_SMEM = pl.BlockSpec(memory_space=pltpu.SMEM)


def like(shape, dtype):
    return jax.ShapeDtypeStruct(shape, dtype)


def local_call(kernel, name, out_shape, in_specs, out_specs, flops, scratch=()):
    moved = sum(math.prod(o.shape) * o.dtype.itemsize for o in out_shape)
    return pl.pallas_call(
        kernel,
        out_shape=out_shape,
        in_specs=in_specs,
        out_specs=out_specs,
        scratch_shapes=list(scratch),
        compiler_params=pltpu.CompilerParams(vmem_limit_bytes=VMEM_LIMIT),
        cost_estimate=pl.CostEstimate(flops=flops, bytes_accessed=2 * moved, transcendentals=0),
        name=name,
    )


def dot(a, b):
    return jnp.dot(a, b, preferred_element_type=jnp.float32)


def where_kernel(position, out):
    for i in range(position.shape[0]):
        out[i] = position[i]


def where(position):
    return local_call(
        where_kernel, "where", [like(position.shape, jnp.int32)], [IN_SMEM], [IN_SMEM], LEAD_FLOPS
    )(position)[0]


def tables_kernel(position, counts, table, scalars):
    here, orb = position[0], position[2]
    slots = table.shape[1] // GROUPS
    named = jnp.where(table[...] // AO_DEV == here, table[...] % AO_DEV, 0).astype(jnp.float32)
    owner = lax.broadcasted_iota(jnp.int32, table.shape, 1) // slots
    for s in range(GROUPS):
        scalars[s] = jnp.max(jnp.where(owner == here ^ s, named, 0.0)).astype(jnp.int32)
    for offset in range(AO_DEV):
        scalars[GROUPS + offset] = counts[here * AO_DEV + offset] - orb * (ORBS // 2)


def tables(position, counts, table):
    return local_call(
        tables_kernel,
        "tables",
        [like((8,), jnp.int32)],
        [IN_SMEM] * 2 + [IN_VMEM],
        [IN_SMEM],
        table.size,
    )(position, counts, table)[0]


def transform_kernel(start, position, scalars, integrals, own, outer, inner, *refs):
    outs, half = refs[:-1], refs[-1]
    mid = AO_DEV * BLOCK

    def blocks(prev, following):
        ids = start + lax.broadcasted_iota(jnp.int32, (BLOCK, own.shape[1]), 1)
        for offset in range(AO_DEV):
            low = mid - offset * BLOCK
            live = ids < scalars[GROUPS + offset]
            for p in range(integrals.shape[0]):
                slab = integrals[p, offset * BLOCK : (offset + 1) * BLOCK, :]
                values = dot(slab[:, low : low + mid], own[...])
                values += dot(slab[:, :low], prev[offset * BLOCK :, :])
                values += dot(slab[:, low + mid :], following[: (offset + 1) * BLOCK, :])
                half[offset, p] = jnp.where(live, values, 0.0).astype(jnp.bfloat16)

    odd = position[0] & 1
    pl.when(odd == 0)(lambda: blocks(inner, outer))
    pl.when(odd == 1)(lambda: blocks(outer, inner))
    for s, out in enumerate(outs):
        out[...] = half[scalars[s]]


def transform(start, position, scalars, integrals, own, outer, inner):
    shape = (integrals.shape[0], BLOCK, own.shape[1])
    return local_call(
        functools.partial(transform_kernel, start),
        "transform",
        [like(shape, jnp.bfloat16)] * GROUPS,
        [IN_SMEM] * 2 + [IN_VMEM] * 4,
        [IN_VMEM] * GROUPS,
        2 * AO_DEV * math.prod(shape) * integrals.shape[2],
        [pltpu.VMEM((AO_DEV, *shape), jnp.bfloat16)],
    )(position, scalars, integrals, own, outer, inner)


def form_pairs(pairs, position, blocks, grams):
    here = position[0]
    slices = [[(ref, p) for ref in block for p in range(ref.shape[0])] for block in blocks]

    def product(left, right):
        total = None
        for (a, i), (b, j) in zip(slices[left], slices[right]):
            part = lax.dot_general(
                a[i], b[j], (((1,), (1,)), ((), ())), preferred_element_type=jnp.float32
            )
            total = part if total is None else total + part
        return total.reshape(grams.shape[1:])

    for bit in (0, 1):
        mine = [(k, a, b) for k, (a, b) in enumerate(pairs) if (a ^ b) >> 1 == bit]
        upper = (here >> bit) & 1

        @pl.when(upper == 0)
        def _(mine=mine):
            for k, a, b in mine:
                grams[k] = product(a, b)

        @pl.when(upper == 1)
        def _(mine=mine):
            for k, a, b in mine:
                grams[k] = product(b, a)


def early_kernel(position, table, live, *refs):
    used = 3 * CHUNKS
    blocks = [refs[i : i + CHUNKS] for i in range(0, used, CHUNKS)]
    near, far, place, grams = refs[used:]
    here, aux, orb = position[0], position[1], position[2]
    slots = place.shape[0]
    for s in range(slots):
        a = table[0, here * slots + s] // AO_DEV ^ here
        b = table[1, here * slots + s] // AO_DEV ^ here
        low, high = jnp.minimum(a, b), jnp.maximum(a, b)
        index = jnp.where(high == 3, low + 3, jnp.where(high == 2, low + 1, 0))
        place[s] = jnp.where(s < live[here], index, len(ALL_PAIRS))
    form_pairs(EARLY_PAIRS, position, blocks, grams)
    for k in range(len(EARLY_PAIRS)):
        for core in (0, 1):
            near[core, k] = grams[k, 2 * aux + (orb ^ core)]
            far[core, k] = grams[k, 2 * (1 - aux) + (orb ^ core)].astype(jnp.bfloat16)


def late_kernel(position, *refs):
    used = GROUPS * CHUNKS
    blocks = [refs[i : i + CHUNKS] for i in range(0, used, CHUNKS)]
    keep, give, grams = refs[used:]
    aux, orb = position[1], position[2]
    form_pairs(LATE_PAIRS, position, blocks, grams)
    for k in range(len(LATE_PAIRS)):
        for chip in (0, 1):
            row = 2 * (aux ^ chip)
            keep[chip, k] = grams[k, row + orb]
            give[chip, k] = grams[k, row + 1 - orb]


def pair_flops(pairs, blocks):
    return 2 * len(pairs) * BLOCK * CHUNKS * blocks[0][0].size


def quarters(pairs):
    rows = BLOCK // 4
    return (2, len(pairs), rows, BLOCK), pltpu.VMEM((len(pairs), 4, rows, BLOCK), jnp.float32)


def early_pairs(position, table, live, blocks):
    shape, grams = quarters(EARLY_PAIRS)
    return local_call(
        early_kernel,
        "early_pairs",
        [
            like(shape, jnp.float32),
            like(shape, jnp.bfloat16),
            like((table.shape[1] // GROUPS,), jnp.int32),
        ],
        [IN_SMEM] * 3 + [IN_VMEM] * (3 * CHUNKS),
        [IN_VMEM] * 2 + [IN_SMEM],
        pair_flops(EARLY_PAIRS, blocks),
        [grams],
    )(position, table, live, *[part for block in blocks for part in block])


def late_pairs(position, blocks):
    shape, grams = quarters(LATE_PAIRS)
    return local_call(
        late_kernel,
        "late_pairs",
        [like(shape, jnp.float32)] * 2,
        [IN_SMEM] + [IN_VMEM] * (GROUPS * CHUNKS),
        [IN_VMEM] * 2,
        pair_flops(LATE_PAIRS, blocks),
        [grams],
    )(position, *[part for block in blocks for part in block])


def spread_kernel(factor, place, near0, far0, got0, near1, got1, far1, out, sums, rows, sems):
    early = near0.shape[1]
    sums[:early] = (near0[0] + far0[0].astype(jnp.float32) + got0[...]) * factor
    sums[early:] = (near1[0] + got1[0] + far1[...].astype(jnp.float32)) * factor
    total, slots, width = out.shape
    slot = lax.broadcasted_iota(jnp.int32, (slots, width), 0)
    source = jnp.zeros((slots, width), jnp.int32)
    for s in range(slots):
        source = jnp.where(slot == s, place[s], source)
    masks = [source == k for k in range(sums.shape[0])]

    def one(m, carry):
        row = jnp.zeros((slots, width), jnp.float32)
        for k, mask in enumerate(masks):
            values = jnp.broadcast_to(sums[k, pl.ds(m, 1), :], (slots, width))
            row = jnp.where(mask, values, row)
        rows[m] = row
        return carry

    step = total // SPREAD_STEPS
    copies = []
    for i in range(SPREAD_STEPS):
        lax.fori_loop(i * step, (i + 1) * step, one, 0, unroll=8)
        part = pl.ds(i * step, step)
        copies.append(pltpu.make_async_copy(rows.at[part], out.at[part], sems.at[i]))
        copies[-1].start()
    for copy in copies:
        copy.wait()


def spread(factor, place, *parts):
    rows = BLOCK // 4
    shape = (rows, place.shape[0], BLOCK)
    return local_call(
        functools.partial(spread_kernel, factor),
        "spread",
        [like(shape, jnp.float32)],
        [IN_SMEM] + [IN_VMEM] * len(parts),
        [IN_HBM],
        6 * math.prod(shape),
        [
            pltpu.VMEM((len(ALL_PAIRS), rows, BLOCK), jnp.float32),
            pltpu.VMEM(shape, jnp.float32),
            pltpu.SemaphoreType.DMA((SPREAD_STEPS,)),
        ],
    )(place, *parts)[0]


def six_pair_body(integrals, coeffs, pair_blocks, pair_count, orbital_count):
    width = coeffs.shape[1] // CHUNKS
    total_aux = integrals.shape[0] * lax.axis_size("aux")
    position = jnp.stack([lax.axis_index(axis) for axis in ("ao", "aux", "orb")]).astype(jnp.int32)
    table = pair_blocks.T

    parts = [lax.slice_in_dim(coeffs, 0, width, axis=1)]
    position, rest = lax.optimization_barrier((where(position), coeffs))
    for c in range(1, CHUNKS):
        parts.append(lax.slice_in_dim(rest, c * width, (c + 1) * width, axis=1))
    inner = [lax.ppermute(part, "ao", INSIDE) for part in parts]
    outer = [lax.ppermute(part, "ao", OUTSIDE) for part in parts]
    scalars = tables(position, orbital_count, table)

    blocks = [[] for _ in range(GROUPS)]
    for c, part in enumerate(parts):
        pieces = transform(c * width, position, scalars, integrals, part, outer[c], inner[c])
        for block, piece in zip(blocks, pieces):
            block.append(piece)

    def fetch(s):
        swap = [(j, j ^ s) for j in range(GROUPS)]
        return [lax.ppermute(piece, "ao", swap) for piece in blocks[s]]

    got = [blocks[0], fetch(1), fetch(2)]
    near0, across0, place = early_pairs(position, table, pair_count, got)
    far0 = lax.ppermute(across0, "aux", SWAP)
    got.append(fetch(3))
    near1, give1 = late_pairs(position, got)
    got1 = lax.ppermute(give1, "orb", SWAP)
    far1 = lax.ppermute((near1[1] + got1[1]).astype(jnp.bfloat16), "aux", SWAP)
    got0 = lax.ppermute(near0[1] + far0[1].astype(jnp.float32), "orb", SWAP)
    factor = 1.0 / math.sqrt(total_aux * ORBS)
    return spread(factor, place, near0, far0, got0, near1, got1, far1)


def solution(mesh):
    sizes = dict(mesh.shape)
    body = general_body
    if sizes["ao"] == 4 and sizes["aux"] == 2 and sizes["orb"] == 2:
        body = six_pair_body
    return jax.shard_map(
        body,
        mesh=mesh,
        in_specs=(
            P(("grp", "aux"), "ao", None),
            P(("grp", "ao"), "orb"),
            P("grp", None),
            P("grp"),
            P("grp"),
        ),
        out_specs=P(("aux", "orb"), ("grp", "ao"), None),
        check_vma=False,
    )
```

```python
import functools
import math

import jax
import jax.numpy as jnp
from jax import lax
from jax.experimental import pallas as pl
from jax.experimental.pallas import tpu as pltpu
from jax.sharding import PartitionSpec as P

BLOCK = 256
AO_DEV = 2
WIN = 5
ORBS = 1024
CHUNKS = 2
SPREAD_STEPS = 4
SPREAD_STEPS = 4
SPREAD_STEPS = 4
SPREAD_STEPS = 4
SPREAD_STEPS = 4
SPREAD_STEPS = 4
VMEM_LIMIT = 40 * 1024 * 1024
LEAD_FLOPS = 1 << 32


def with_halo(cells, sides, width):
    for axis, dim in sides:
        count = lax.axis_size(axis)
        ends = count - 1
        head = lax.slice_in_dim(cells, 0, width, axis=dim)
        tail = lax.slice_in_dim(cells, cells.shape[dim] - width, cells.shape[dim], axis=dim)
        cells = jnp.concatenate(
            [
                lax.ppermute(tail, axis, [(i, (i + 1) % count) for i in range(ends)]),
                cells,
                lax.ppermute(head, axis, [((i + 1) % count, i) for i in range(ends)]),
            ],
            axis=dim,
        )
    return cells


def general_body(integrals, coeffs, pair_blocks, pair_count, orbital_count):
    orb_local = coeffs.shape[1]
    aux_devices = lax.axis_size("aux")
    total_aux = integrals.shape[0] * aux_devices
    rim = WIN // 2 * BLOCK
    extended = with_halo(coeffs, (("ao", 0),), rim)
    ao_here = lax.axis_index("ao")
    orbital_ids = lax.axis_index("orb") * orb_local + jnp.arange(orb_local, dtype=jnp.int32)
    pieces = []
    for offset in range(AO_DEV):
        slab = integrals[:, offset * BLOCK : (offset + 1) * BLOCK, :]
        slot_range = extended[offset * BLOCK : offset * BLOCK + WIN * BLOCK]
        values = jnp.einsum("pml,li->pmi", slab, slot_range, preferred_element_type=jnp.float32)
        limit = orbital_count[ao_here * AO_DEV + offset]
        values = jnp.where((orbital_ids < limit)[None, None, :], values, 0.0)
        pieces.append(values.astype(jnp.bfloat16))
    transformed = jnp.stack(pieces)
    owners = lax.axis_size("ao")
    table = pair_blocks.reshape(owners, -1, 2)
    slots = table.shape[1]
    live = jnp.arange(slots, dtype=jnp.int32)[None, :] < pair_count[:, None]
    touched = live[:, :, None] & (table // AO_DEV == ao_here)
    wanted = jnp.max(jnp.where(touched, table % AO_DEV, 0), axis=(1, 2))
    outgoing = transformed[wanted]
    received = lax.all_to_all(outgoing, "ao", split_axis=0, concat_axis=0, tiled=True)
    owned = table[ao_here]
    factor = 1.0 / math.sqrt(total_aux * ORBS)
    weights = jnp.where(live[ao_here], factor, 0.0).astype(jnp.float32)
    left_source = owned[:, 0] // AO_DEV
    right_source = owned[:, 1] // AO_DEV
    right_factors = received[right_source]
    lefts = received[left_source]
    term = jnp.einsum("spmi,spni->msn", lefts, right_factors, preferred_element_type=jnp.float32)
    return lax.psum_scatter(
        term * weights[None, :, None], ("aux", "orb"), scatter_dimension=0, tiled=True
    )


EARLY_PAIRS = ((0, 1), (0, 2), (1, 2))
LATE_PAIRS = ((0, 3), (1, 3), (2, 3))
ALL_PAIRS = EARLY_PAIRS + LATE_PAIRS
GROUPS = 4
SWAP = [(0, 1), (1, 0)]
OUTSIDE = [(0, 1), (1, 0), (2, 3), (3, 2)]
INSIDE = [(1, 2), (2, 1)]

IN_HBM = pl.BlockSpec(memory_space=pltpu.HBM)
IN_VMEM = pl.BlockSpec(memory_space=pltpu.VMEM)


def like(shape, dtype):
    return jax.ShapeDtypeStruct(shape, dtype)


def local_call(kernel, name, out_shape, inputs, flops, scratch=(), out_spec=IN_VMEM):
    moved = sum(math.prod(o.shape) * o.dtype.itemsize for o in out_shape)
    return pl.pallas_call(
        kernel,
        out_shape=out_shape,
        in_specs=[IN_VMEM] * inputs,
        out_specs=[out_spec] * len(out_shape),
        scratch_shapes=list(scratch),
        compiler_params=pltpu.CompilerParams(vmem_limit_bytes=VMEM_LIMIT),
        cost_estimate=pl.CostEstimate(flops=flops, bytes_accessed=2 * moved, transcendentals=0),
        name=name,
    )


def dot(a, b):
    return jnp.dot(a, b, preferred_element_type=jnp.float32)


def lead_kernel(out):
    out[...] = jnp.zeros_like(out)


def lead():
    return local_call(lead_kernel, "lead", [like((8, 128), jnp.int32)], 0, LEAD_FLOPS)()[0]


def scalar_at(values, index):
    ids = lax.broadcasted_iota(jnp.int32, values.shape, 1)
    return jnp.sum(jnp.where(ids == index, values, 0).astype(jnp.float32))


def tables_kernel(first, counts, table, wants):
    here, orb = lax.axis_index("ao"), lax.axis_index("orb")
    slots = table.shape[1] // GROUPS
    named = jnp.where(table[...] // AO_DEV == here, table[...] % AO_DEV, 0).astype(jnp.float32)
    owner = lax.broadcasted_iota(jnp.int32, table.shape, 1) // slots
    rows = [jnp.max(jnp.where(owner == here ^ s, named, 0.0)) for s in range(GROUPS)]
    for offset in range(AO_DEV):
        count = scalar_at(counts[...], here * AO_DEV + offset)
        rows.append(count - (orb * (ORBS // 2)).astype(jnp.float32))
    row = lax.broadcasted_iota(jnp.int32, wants.shape, 0)
    out = first[0, 0:1].astype(jnp.float32).reshape(1, 1) + jnp.zeros(wants.shape, jnp.float32)
    for k, value in enumerate(rows):
        out = jnp.where(row == k, value, out)
    wants[...] = out.astype(jnp.int32)


def tables(first, counts, table, width):
    return local_call(
        tables_kernel, "tables", [like((8, width), jnp.int32)], 3, table.size
    )(first, counts.reshape(1, -1), table)[0]


def transform_kernel(start, wants, integrals, own, outer, inner, *outs):
    mid = AO_DEV * BLOCK

    def blocks(prev, following):
        ids = start + lax.broadcasted_iota(jnp.int32, (BLOCK, own.shape[1]), 1)
        for p in range(integrals.shape[0]):
            both = []
            for offset in range(AO_DEV):
                low = mid - offset * BLOCK
                slab = integrals[p, offset * BLOCK : (offset + 1) * BLOCK, :]
                values = dot(slab[:, low : low + mid], own[...])
                values += dot(slab[:, :low], prev[offset * BLOCK :, :])
                values += dot(slab[:, low + mid :], following[: (offset + 1) * BLOCK, :])
                live = ids < wants[GROUPS + offset : GROUPS + offset + 1, :]
                both.append(jnp.where(live, values, 0.0))
            for s, out in enumerate(outs):
                out[p] = jnp.where(wants[s : s + 1, :] == 0, *both).astype(jnp.bfloat16)

    odd = lax.axis_index("ao") & 1
    pl.when(odd == 0)(lambda: blocks(inner, outer))
    pl.when(odd == 1)(lambda: blocks(outer, inner))


def transform(start, wants, integrals, own, outer, inner):
    shape = (integrals.shape[0], BLOCK, own.shape[1])
    return local_call(
        functools.partial(transform_kernel, start),
        "transform",
        [like(shape, jnp.bfloat16)] * GROUPS,
        5,
        2 * AO_DEV * math.prod(shape) * integrals.shape[2],
    )(wants, integrals, own, outer, inner)


def form_pairs(pairs, blocks, grams):
    here = lax.axis_index("ao")
    slices = [[(ref, p) for ref in block for p in range(ref.shape[0])] for block in blocks]

    def product(left, right):
        total = None
        for (a, i), (b, j) in zip(slices[left], slices[right]):
            part = lax.dot_general(
                a[i], b[j], (((1,), (1,)), ((), ())), preferred_element_type=jnp.float32
            )
            total = part if total is None else total + part
        return total.reshape(grams.shape[1:])

    for bit in (0, 1):
        mine = [(k, a, b) for k, (a, b) in enumerate(pairs) if (a ^ b) >> 1 == bit]
        upper = (here >> bit) & 1

        @pl.when(upper == 0)
        def _(mine=mine):
            for k, a, b in mine:
                grams[k] = product(a, b)

        @pl.when(upper == 1)
        def _(mine=mine):
            for k, a, b in mine:
                grams[k] = product(b, a)


def early_kernel(live, table, *refs):
    used = 3 * CHUNKS
    blocks = [refs[i : i + CHUNKS] for i in range(0, used, CHUNKS)]
    near, far, place, grams = refs[used:]
    here, aux, orb = (lax.axis_index(axis) for axis in ("ao", "aux", "orb"))
    slots, width = place.shape
    slot = lax.broadcasted_iota(jnp.int32, (slots, table.shape[1]), 0)
    column = lax.broadcasted_iota(jnp.int32, (slots, table.shape[1]), 1)
    shown = column == here * slots + slot
    sides = []
    for side in (0, 1):
        group = (table[side : side + 1, :] // AO_DEV).astype(jnp.float32)
        group = jnp.sum(jnp.where(shown, group, 0.0), axis=1, keepdims=True)
        sides.append(group.astype(jnp.int32) ^ here)
    low, high = jnp.minimum(*sides), jnp.maximum(*sides)
    index = jnp.where(high == 3, low + 3, jnp.where(high == 2, low + 1, 0))
    slot = lax.broadcasted_iota(jnp.int32, (slots, width), 0)
    count = scalar_at(live[...], here).astype(jnp.int32)
    place[...] = jnp.where(slot < count, index, len(ALL_PAIRS))
    form_pairs(EARLY_PAIRS, blocks, grams)
    for k in range(len(EARLY_PAIRS)):
        for core in (0, 1):
            near[core, k] = grams[k, 2 * aux + (orb ^ core)]
            far[core, k] = grams[k, 2 * (1 - aux) + (orb ^ core)].astype(jnp.bfloat16)


def late_kernel(*refs):
    used = GROUPS * CHUNKS
    blocks = [refs[i : i + CHUNKS] for i in range(0, used, CHUNKS)]
    keep, give, grams = refs[used:]
    aux, orb = lax.axis_index("aux"), lax.axis_index("orb")
    form_pairs(LATE_PAIRS, blocks, grams)
    for k in range(len(LATE_PAIRS)):
        for chip in (0, 1):
            row = 2 * (aux ^ chip)
            keep[chip, k] = grams[k, row + orb]
            give[chip, k] = grams[k, row + 1 - orb]


def pair_flops(pairs, blocks):
    return 2 * len(pairs) * BLOCK * CHUNKS * blocks[0][0].size


def quarters(pairs):
    rows = BLOCK // 4
    return (2, len(pairs), rows, BLOCK), pltpu.VMEM((len(pairs), 4, rows, BLOCK), jnp.float32)


def early_pairs(live, table, blocks):
    shape, grams = quarters(EARLY_PAIRS)
    return local_call(
        early_kernel,
        "early_pairs",
        [
            like(shape, jnp.float32),
            like(shape, jnp.bfloat16),
            like((table.shape[1] // GROUPS, BLOCK), jnp.int32),
        ],
        2 + 3 * CHUNKS,
        pair_flops(EARLY_PAIRS, blocks),
        [grams],
    )(live.reshape(1, -1), table, *[part for block in blocks for part in block])


def late_pairs(blocks):
    shape, grams = quarters(LATE_PAIRS)
    return local_call(
        late_kernel,
        "late_pairs",
        [like(shape, jnp.float32)] * 2,
        GROUPS * CHUNKS,
        pair_flops(LATE_PAIRS, blocks),
        [grams],
    )(*[part for block in blocks for part in block])


def spread_kernel(factor, place, near0, far0, got0, near1, got1, far1, out, sums, rows, sems):
    early = near0.shape[1]
    sums[:early] = (near0[0] + far0[0].astype(jnp.float32) + got0[...]) * factor
    sums[early:] = (near1[0] + got1[0] + far1[...].astype(jnp.float32)) * factor
    total, slots, width = out.shape
    masks = [place[...] == k for k in range(sums.shape[0])]

    def one(m, carry):
        row = jnp.zeros((slots, width), jnp.float32)
        for k, mask in enumerate(masks):
            values = jnp.broadcast_to(sums[k, pl.ds(m, 1), :], (slots, width))
            row = jnp.where(mask, values, row)
        rows[m] = row
        return carry

    step = total // SPREAD_STEPS
    copies = []
    for i in range(SPREAD_STEPS):
        lax.fori_loop(i * step, (i + 1) * step, one, 0, unroll=8)
        part = pl.ds(i * step, step)
        copies.append(pltpu.make_async_copy(rows.at[part], out.at[part], sems.at[i]))
        copies[-1].start()
    for copy in copies:
        copy.wait()


def spread(factor, place, *parts):
    rows = BLOCK // 4
    shape = (rows, place.shape[0], BLOCK)
    return local_call(
        functools.partial(spread_kernel, factor),
        "spread",
        [like(shape, jnp.float32)],
        1 + len(parts),
        6 * math.prod(shape),
        [
            pltpu.VMEM((len(ALL_PAIRS), rows, BLOCK), jnp.float32),
            pltpu.VMEM(shape, jnp.float32),
            pltpu.SemaphoreType.DMA((SPREAD_STEPS,)),
        ],
        IN_HBM,
    )(place, *parts)[0]


def six_pair_body(integrals, coeffs, pair_blocks, pair_count, orbital_count):
    width = coeffs.shape[1] // CHUNKS
    total_aux = integrals.shape[0] * lax.axis_size("aux")
    table = pair_blocks.T

    parts = [lax.slice_in_dim(coeffs, 0, width, axis=1)]
    first, rest = lax.optimization_barrier((lead(), coeffs))
    for c in range(1, CHUNKS):
        parts.append(lax.slice_in_dim(rest, c * width, (c + 1) * width, axis=1))
    inner = [lax.ppermute(part, "ao", INSIDE) for part in parts]
    outer = [lax.ppermute(part, "ao", OUTSIDE) for part in parts]
    wants = tables(first, orbital_count, table, width)

    blocks = [[] for _ in range(GROUPS)]
    for c, part in enumerate(parts):
        pieces = transform(c * width, wants, integrals, part, outer[c], inner[c])
        for block, piece in zip(blocks, pieces):
            block.append(piece)

    def fetch(s):
        swap = [(j, j ^ s) for j in range(GROUPS)]
        return [lax.ppermute(piece, "ao", swap) for piece in blocks[s]]

    got = [blocks[0], fetch(1), fetch(2)]
    near0, across0, place = early_pairs(pair_count, table, got)
    far0 = lax.ppermute(across0, "aux", SWAP)
    got.append(fetch(3))
    near1, give1 = late_pairs(got)
    got1 = lax.ppermute(give1, "orb", SWAP)
    far1 = lax.ppermute((near1[1] + got1[1]).astype(jnp.bfloat16), "aux", SWAP)
    got0 = lax.ppermute(near0[1] + far0[1].astype(jnp.float32), "orb", SWAP)
    factor = 1.0 / math.sqrt(total_aux * ORBS)
    return spread(factor, place, near0, far0, got0, near1, got1, far1)


def solution(mesh):
    sizes = dict(mesh.shape)
    body = general_body
    if sizes["ao"] == 4 and sizes["aux"] == 2 and sizes["orb"] == 2:
        body = six_pair_body
    return jax.shard_map(
        body,
        mesh=mesh,
        in_specs=(
            P(("grp", "aux"), "ao", None),
            P(("grp", "ao"), "orb"),
            P("grp", None),
            P("grp"),
            P("grp"),
        ),
        out_specs=P(("aux", "orb"), ("grp", "ao"), None),
        check_vma=False,
    )
```

```python
import functools
import math

import jax
import jax.numpy as jnp
from jax import lax
from jax.experimental import pallas as pl
from jax.experimental.pallas import tpu as pltpu
from jax.sharding import PartitionSpec as P

BLOCK = 256
AO_DEV = 2
WIN = 5
ORBS = 1024
CHUNKS = 2
SPREAD_STEPS = 4
SPREAD_STEPS = 4
SPREAD_STEPS = 4
SPREAD_STEPS = 4
SPREAD_STEPS = 4
SPREAD_STEPS = 4
VMEM_LIMIT = 40 * 1024 * 1024
LEAD_FLOPS = 1 << 32


def with_halo(cells, sides, width):
    for axis, dim in sides:
        count = lax.axis_size(axis)
        ends = count - 1
        head = lax.slice_in_dim(cells, 0, width, axis=dim)
        tail = lax.slice_in_dim(cells, cells.shape[dim] - width, cells.shape[dim], axis=dim)
        cells = jnp.concatenate(
            [
                lax.ppermute(tail, axis, [(i, (i + 1) % count) for i in range(ends)]),
                cells,
                lax.ppermute(head, axis, [((i + 1) % count, i) for i in range(ends)]),
            ],
            axis=dim,
        )
    return cells


def general_body(integrals, coeffs, pair_blocks, pair_count, orbital_count):
    orb_local = coeffs.shape[1]
    aux_devices = lax.axis_size("aux")
    total_aux = integrals.shape[0] * aux_devices
    rim = WIN // 2 * BLOCK
    extended = with_halo(coeffs, (("ao", 0),), rim)
    ao_here = lax.axis_index("ao")
    orbital_ids = lax.axis_index("orb") * orb_local + jnp.arange(orb_local, dtype=jnp.int32)
    pieces = []
    for offset in range(AO_DEV):
        slab = integrals[:, offset * BLOCK : (offset + 1) * BLOCK, :]
        slot_range = extended[offset * BLOCK : offset * BLOCK + WIN * BLOCK]
        values = jnp.einsum("pml,li->pmi", slab, slot_range, preferred_element_type=jnp.float32)
        limit = orbital_count[ao_here * AO_DEV + offset]
        values = jnp.where((orbital_ids < limit)[None, None, :], values, 0.0)
        pieces.append(values.astype(jnp.bfloat16))
    transformed = jnp.stack(pieces)
    owners = lax.axis_size("ao")
    table = pair_blocks.reshape(owners, -1, 2)
    slots = table.shape[1]
    live = jnp.arange(slots, dtype=jnp.int32)[None, :] < pair_count[:, None]
    touched = live[:, :, None] & (table // AO_DEV == ao_here)
    wanted = jnp.max(jnp.where(touched, table % AO_DEV, 0), axis=(1, 2))
    outgoing = transformed[wanted]
    received = lax.all_to_all(outgoing, "ao", split_axis=0, concat_axis=0, tiled=True)
    owned = table[ao_here]
    factor = 1.0 / math.sqrt(total_aux * ORBS)
    weights = jnp.where(live[ao_here], factor, 0.0).astype(jnp.float32)
    left_source = owned[:, 0] // AO_DEV
    right_source = owned[:, 1] // AO_DEV
    right_factors = received[right_source]
    lefts = received[left_source]
    term = jnp.einsum("spmi,spni->msn", lefts, right_factors, preferred_element_type=jnp.float32)
    return lax.psum_scatter(
        term * weights[None, :, None], ("aux", "orb"), scatter_dimension=0, tiled=True
    )


EARLY_PAIRS = ((0, 1), (0, 2), (1, 2))
LATE_PAIRS = ((0, 3), (1, 3), (2, 3))
ALL_PAIRS = EARLY_PAIRS + LATE_PAIRS
GROUPS = 4
SWAP = [(0, 1), (1, 0)]
OUTSIDE = [(0, 1), (1, 0), (2, 3), (3, 2)]
INSIDE = [(1, 2), (2, 1)]

IN_HBM = pl.BlockSpec(memory_space=pltpu.HBM)
IN_VMEM = pl.BlockSpec(memory_space=pltpu.VMEM)


def like(shape, dtype):
    return jax.ShapeDtypeStruct(shape, dtype)


def local_call(kernel, name, out_shape, inputs, flops, scratch=(), out_spec=IN_VMEM):
    moved = sum(math.prod(o.shape) * o.dtype.itemsize for o in out_shape)
    return pl.pallas_call(
        kernel,
        out_shape=out_shape,
        in_specs=[IN_VMEM] * inputs,
        out_specs=[out_spec] * len(out_shape),
        scratch_shapes=list(scratch),
        compiler_params=pltpu.CompilerParams(vmem_limit_bytes=VMEM_LIMIT),
        cost_estimate=pl.CostEstimate(flops=flops, bytes_accessed=2 * moved, transcendentals=0),
        name=name,
    )


def dot(a, b):
    return jnp.dot(a, b, preferred_element_type=jnp.float32)


def lead_kernel(out):
    out[...] = jnp.zeros_like(out)


def lead():
    return local_call(lead_kernel, "lead", [like((8, 128), jnp.int32)], 0, LEAD_FLOPS)()[0]


def scalar_at(values, index):
    ids = lax.broadcasted_iota(jnp.int32, values.shape, 1)
    return jnp.sum(jnp.where(ids == index, values, 0).astype(jnp.float32))


def tables_kernel(first, counts, table, wants):
    here, orb = lax.axis_index("ao"), lax.axis_index("orb")
    slots = table.shape[1] // GROUPS
    named = jnp.where(table[...] // AO_DEV == here, table[...] % AO_DEV, 0).astype(jnp.float32)
    owner = lax.broadcasted_iota(jnp.int32, table.shape, 1) // slots
    rows = [jnp.max(jnp.where(owner == here ^ s, named, 0.0)) for s in range(GROUPS)]
    for offset in range(AO_DEV):
        count = scalar_at(counts[...], here * AO_DEV + offset)
        rows.append(count - (orb * (ORBS // 2)).astype(jnp.float32))
    row = lax.broadcasted_iota(jnp.int32, wants.shape, 0)
    out = first[0, 0:1].astype(jnp.float32).reshape(1, 1) + jnp.zeros(wants.shape, jnp.float32)
    for k, value in enumerate(rows):
        out = jnp.where(row == k, value, out)
    wants[...] = out.astype(jnp.int32)


def tables(first, counts, table, width):
    return local_call(
        tables_kernel, "tables", [like((8, width), jnp.int32)], 3, table.size
    )(first, counts.reshape(1, -1), table)[0]


def transform_kernel(start, wants, integrals, own, outer, inner, *outs):
    mid = AO_DEV * BLOCK

    def blocks(prev, following):
        ids = start + lax.broadcasted_iota(jnp.int32, (BLOCK, own.shape[1]), 1)
        for p in range(integrals.shape[0]):
            both = []
            for offset in range(AO_DEV):
                low = mid - offset * BLOCK
                slab = integrals[p, offset * BLOCK : (offset + 1) * BLOCK, :]
                values = dot(slab[:, low : low + mid], own[...])
                values += dot(slab[:, :low], prev[offset * BLOCK :, :])
                values += dot(slab[:, low + mid :], following[: (offset + 1) * BLOCK, :])
                live = ids < wants[GROUPS + offset : GROUPS + offset + 1, :]
                both.append(jnp.where(live, values, 0.0))
            for s, out in enumerate(outs):
                out[p] = jnp.where(wants[s : s + 1, :] == 0, *both).astype(jnp.bfloat16)

    odd = lax.axis_index("ao") & 1
    pl.when(odd == 0)(lambda: blocks(inner, outer))
    pl.when(odd == 1)(lambda: blocks(outer, inner))


def shared_kernel(start, wants, integrals, own, outer, inner, swapped, *refs):
    *outs, whole = refs
    aux = lax.axis_index("aux")
    width = inner.shape[1]
    whole[:, pl.ds(pl.multiple_of(aux * width, width), width)] = inner[...]
    whole[:, pl.ds(pl.multiple_of((1 - aux) * width, width), width)] = swapped[...]
    transform_kernel(start, wants, integrals, own, outer, whole, *outs)


def shared_transform(start, wants, integrals, own, outer, inner, swapped):
    shape = (integrals.shape[0], BLOCK, own.shape[1])
    return local_call(
        functools.partial(shared_kernel, start),
        "transform",
        [like(shape, jnp.bfloat16)] * GROUPS,
        6,
        2 * AO_DEV * math.prod(shape) * integrals.shape[2],
        [pltpu.VMEM(own.shape, jnp.bfloat16)],
    )(wants, integrals, own, outer, inner, swapped)


def transform(start, wants, integrals, own, outer, inner):
    shape = (integrals.shape[0], BLOCK, own.shape[1])
    return local_call(
        functools.partial(transform_kernel, start),
        "transform",
        [like(shape, jnp.bfloat16)] * GROUPS,
        5,
        2 * AO_DEV * math.prod(shape) * integrals.shape[2],
    )(wants, integrals, own, outer, inner)


def form_pairs(pairs, blocks, grams):
    here = lax.axis_index("ao")
    slices = [[(ref, p) for ref in block for p in range(ref.shape[0])] for block in blocks]

    def product(left, right):
        total = None
        for (a, i), (b, j) in zip(slices[left], slices[right]):
            part = lax.dot_general(
                a[i], b[j], (((1,), (1,)), ((), ())), preferred_element_type=jnp.float32
            )
            total = part if total is None else total + part
        return total.reshape(grams.shape[1:])

    for bit in (0, 1):
        mine = [(k, a, b) for k, (a, b) in enumerate(pairs) if (a ^ b) >> 1 == bit]
        upper = (here >> bit) & 1

        @pl.when(upper == 0)
        def _(mine=mine):
            for k, a, b in mine:
                grams[k] = product(a, b)

        @pl.when(upper == 1)
        def _(mine=mine):
            for k, a, b in mine:
                grams[k] = product(b, a)


def early_kernel(live, table, *refs):
    used = 3 * CHUNKS
    own, middle, next_to = [refs[i : i + CHUNKS] for i in range(0, used, CHUNKS)]
    blocks = own, next_to, middle
    near, far, place, grams = refs[used:]
    here, aux, orb = (lax.axis_index(axis) for axis in ("ao", "aux", "orb"))
    slots, width = place.shape
    slot = lax.broadcasted_iota(jnp.int32, (slots, table.shape[1]), 0)
    column = lax.broadcasted_iota(jnp.int32, (slots, table.shape[1]), 1)
    shown = column == here * slots + slot
    sides = []
    for side in (0, 1):
        group = (table[side : side + 1, :] // AO_DEV).astype(jnp.float32)
        group = jnp.sum(jnp.where(shown, group, 0.0), axis=1, keepdims=True)
        sides.append(group.astype(jnp.int32) ^ here)
    low, high = jnp.minimum(*sides), jnp.maximum(*sides)
    index = jnp.where(high == 3, low + 3, jnp.where(high == 2, low + 1, 0))
    slot = lax.broadcasted_iota(jnp.int32, (slots, width), 0)
    count = scalar_at(live[...], here).astype(jnp.int32)
    place[...] = jnp.where(slot < count, index, len(ALL_PAIRS))
    form_pairs(EARLY_PAIRS, blocks, grams)
    for k in range(len(EARLY_PAIRS)):
        for core in (0, 1):
            near[core, k] = grams[k, 2 * aux + (orb ^ core)]
            far[core, k] = grams[k, 2 * (1 - aux) + (orb ^ core)].astype(jnp.bfloat16)


def late_kernel(*refs):
    used = GROUPS * CHUNKS
    own, middle, next_to, last = [refs[i : i + CHUNKS] for i in range(0, used, CHUNKS)]
    blocks = own, next_to, middle, last
    keep, give, grams = refs[used:]
    aux, orb = lax.axis_index("aux"), lax.axis_index("orb")
    form_pairs(LATE_PAIRS, blocks, grams)
    for k in range(len(LATE_PAIRS)):
        for chip in (0, 1):
            row = 2 * (aux ^ chip)
            keep[chip, k] = grams[k, row + orb]
            give[chip, k] = grams[k, row + 1 - orb]


def pair_flops(pairs, blocks):
    return 2 * len(pairs) * BLOCK * CHUNKS * blocks[0][0].size


def quarters(pairs):
    rows = BLOCK // 4
    return (2, len(pairs), rows, BLOCK), pltpu.VMEM((len(pairs), 4, rows, BLOCK), jnp.float32)


def early_pairs(live, table, blocks):
    shape, grams = quarters(EARLY_PAIRS)
    return local_call(
        early_kernel,
        "early_pairs",
        [
            like(shape, jnp.float32),
            like(shape, jnp.bfloat16),
            like((table.shape[1] // GROUPS, BLOCK), jnp.int32),
        ],
        2 + 3 * CHUNKS,
        pair_flops(EARLY_PAIRS, blocks),
        [grams],
    )(live.reshape(1, -1), table, *blocks[0], *blocks[2], *blocks[1])


def late_pairs(blocks):
    shape, grams = quarters(LATE_PAIRS)
    return local_call(
        late_kernel,
        "late_pairs",
        [like(shape, jnp.float32)] * 2,
        GROUPS * CHUNKS,
        pair_flops(LATE_PAIRS, blocks),
        [grams],
    )(*blocks[0], *blocks[2], *blocks[1], *blocks[3])


def spread_kernel(factor, place, near0, far0, got0, near1, got1, far1, out, sums, rows, sems):
    early = near0.shape[1]
    sums[:early] = (near0[0] + far0[0].astype(jnp.float32) + got0[...]) * factor
    sums[early:] = (near1[0] + got1[0] + far1[...].astype(jnp.float32)) * factor
    total, slots, width = out.shape
    masks = [place[...] == k for k in range(sums.shape[0])]

    def one(m, carry):
        row = jnp.zeros((slots, width), jnp.float32)
        for k, mask in enumerate(masks):
            values = jnp.broadcast_to(sums[k, pl.ds(m, 1), :], (slots, width))
            row = jnp.where(mask, values, row)
        rows[m] = row
        return carry

    step = total // SPREAD_STEPS
    copies = []
    for i in range(SPREAD_STEPS):
        lax.fori_loop(i * step, (i + 1) * step, one, 0, unroll=8)
        part = pl.ds(i * step, step)
        copies.append(pltpu.make_async_copy(rows.at[part], out.at[part], sems.at[i]))
        copies[-1].start()
    for copy in copies:
        copy.wait()


def spread(factor, place, *parts):
    rows = BLOCK // 4
    shape = (rows, place.shape[0], BLOCK)
    return local_call(
        functools.partial(spread_kernel, factor),
        "spread",
        [like(shape, jnp.float32)],
        1 + len(parts),
        6 * math.prod(shape),
        [
            pltpu.VMEM((len(ALL_PAIRS), rows, BLOCK), jnp.float32),
            pltpu.VMEM(shape, jnp.float32),
            pltpu.SemaphoreType.DMA((SPREAD_STEPS,)),
        ],
        IN_HBM,
    )(place, *parts)[0]


def six_pair_body(integrals, coeffs, pair_blocks, pair_count, orbital_count):
    width = coeffs.shape[1] // CHUNKS
    total_aux = integrals.shape[0] * lax.axis_size("aux")
    table = pair_blocks.T

    half = width // 2
    parts = [lax.slice_in_dim(coeffs, 0, width, axis=1)]
    first, rest = lax.optimization_barrier((lead(), coeffs))
    parts.append(lax.slice_in_dim(rest, width, 2 * width, axis=1))
    mine = lax.dynamic_slice_in_dim(rest, width + lax.axis_index("aux") * half, half, axis=1)
    inner = [lax.ppermute(part, "ao", INSIDE) for part in (parts[0], mine)]
    outer = [lax.ppermute(part, "ao", OUTSIDE) for part in parts]
    wants = tables(first, orbital_count, table, width)

    pieces = list(transform(0, wants, integrals, parts[0], outer[0], inner[0]))
    blocks = [[piece] for piece in pieces]
    inner[1], blocks[0][0] = lax.optimization_barrier((inner[1], blocks[0][0]))
    swapped = lax.ppermute(inner[1], "aux", SWAP)
    pieces = shared_transform(
        width, wants, integrals, parts[1], outer[1], inner[1], swapped
    )
    for block, piece in zip(blocks, pieces):
        block.append(piece)

    def fetch(s):
        swap = [(j, j ^ s) for j in range(GROUPS)]
        return [lax.ppermute(piece, "ao", swap) for piece in blocks[s]]

    middle = fetch(2)
    got = [blocks[0], fetch(1), middle]
    near0, across0, place = early_pairs(pair_count, table, got)
    far0 = lax.ppermute(across0, "aux", SWAP)
    got.append(fetch(3))
    near1, give1 = late_pairs(got)
    got1 = lax.ppermute(give1, "orb", SWAP)
    far1 = lax.ppermute((near1[1] + got1[1]).astype(jnp.bfloat16), "aux", SWAP)
    got0 = lax.ppermute(near0[1] + far0[1].astype(jnp.float32), "orb", SWAP)
    factor = 1.0 / math.sqrt(total_aux * ORBS)
    return spread(factor, place, near0, far0, got0, near1, got1, far1)


def solution(mesh):
    sizes = dict(mesh.shape)
    body = general_body
    if sizes["ao"] == 4 and sizes["aux"] == 2 and sizes["orb"] == 2:
        body = six_pair_body
    return jax.shard_map(
        body,
        mesh=mesh,
        in_specs=(
            P(("grp", "aux"), "ao", None),
            P(("grp", "ao"), "orb"),
            P("grp", None),
            P("grp"),
            P("grp"),
        ),
        out_specs=P(("aux", "orb"), ("grp", "ao"), None),
        check_vma=False,
    )
```

```python
import functools
import math

import jax
import jax.numpy as jnp
from jax import lax
from jax.experimental import pallas as pl
from jax.experimental.pallas import tpu as pltpu
from jax.sharding import PartitionSpec as P

BLOCK = 256
AO_DEV = 2
WIN = 5
ORBS = 1024
CHUNKS = 2
SPREAD_STEPS = 4
SPREAD_STEPS = 4
SPREAD_STEPS = 4
SPREAD_STEPS = 4
SPREAD_STEPS = 4
SPREAD_STEPS = 4
VMEM_LIMIT = 40 * 1024 * 1024
LEAD_FLOPS = 1 << 32


def with_halo(cells, sides, width):
    for axis, dim in sides:
        count = lax.axis_size(axis)
        ends = count - 1
        head = lax.slice_in_dim(cells, 0, width, axis=dim)
        tail = lax.slice_in_dim(cells, cells.shape[dim] - width, cells.shape[dim], axis=dim)
        cells = jnp.concatenate(
            [
                lax.ppermute(tail, axis, [(i, (i + 1) % count) for i in range(ends)]),
                cells,
                lax.ppermute(head, axis, [((i + 1) % count, i) for i in range(ends)]),
            ],
            axis=dim,
        )
    return cells


def general_body(integrals, coeffs, pair_blocks, pair_count, orbital_count):
    orb_local = coeffs.shape[1]
    aux_devices = lax.axis_size("aux")
    total_aux = integrals.shape[0] * aux_devices
    rim = WIN // 2 * BLOCK
    extended = with_halo(coeffs, (("ao", 0),), rim)
    ao_here = lax.axis_index("ao")
    orbital_ids = lax.axis_index("orb") * orb_local + jnp.arange(orb_local, dtype=jnp.int32)
    pieces = []
    for offset in range(AO_DEV):
        slab = integrals[:, offset * BLOCK : (offset + 1) * BLOCK, :]
        slot_range = extended[offset * BLOCK : offset * BLOCK + WIN * BLOCK]
        values = jnp.einsum("pml,li->pmi", slab, slot_range, preferred_element_type=jnp.float32)
        limit = orbital_count[ao_here * AO_DEV + offset]
        values = jnp.where((orbital_ids < limit)[None, None, :], values, 0.0)
        pieces.append(values.astype(jnp.bfloat16))
    transformed = jnp.stack(pieces)
    owners = lax.axis_size("ao")
    table = pair_blocks.reshape(owners, -1, 2)
    slots = table.shape[1]
    live = jnp.arange(slots, dtype=jnp.int32)[None, :] < pair_count[:, None]
    touched = live[:, :, None] & (table // AO_DEV == ao_here)
    wanted = jnp.max(jnp.where(touched, table % AO_DEV, 0), axis=(1, 2))
    outgoing = transformed[wanted]
    received = lax.all_to_all(outgoing, "ao", split_axis=0, concat_axis=0, tiled=True)
    owned = table[ao_here]
    factor = 1.0 / math.sqrt(total_aux * ORBS)
    weights = jnp.where(live[ao_here], factor, 0.0).astype(jnp.float32)
    left_source = owned[:, 0] // AO_DEV
    right_source = owned[:, 1] // AO_DEV
    right_factors = received[right_source]
    lefts = received[left_source]
    term = jnp.einsum("spmi,spni->msn", lefts, right_factors, preferred_element_type=jnp.float32)
    return lax.psum_scatter(
        term * weights[None, :, None], ("aux", "orb"), scatter_dimension=0, tiled=True
    )


EARLY_PAIRS = ((0, 1), (0, 2), (1, 2))
LATE_PAIRS = ((0, 3), (1, 3), (2, 3))
ALL_PAIRS = EARLY_PAIRS + LATE_PAIRS
GROUPS = 4
SWAP = [(0, 1), (1, 0)]
OUTSIDE = [(0, 1), (1, 0), (2, 3), (3, 2)]
INSIDE = [(1, 2), (2, 1)]

IN_HBM = pl.BlockSpec(memory_space=pltpu.HBM)
IN_VMEM = pl.BlockSpec(memory_space=pltpu.VMEM)


def like(shape, dtype):
    return jax.ShapeDtypeStruct(shape, dtype)


def local_call(kernel, name, out_shape, inputs, flops, scratch=(), out_spec=IN_VMEM):
    moved = sum(math.prod(o.shape) * o.dtype.itemsize for o in out_shape)
    return pl.pallas_call(
        kernel,
        out_shape=out_shape,
        in_specs=[IN_VMEM] * inputs,
        out_specs=[out_spec] * len(out_shape),
        scratch_shapes=list(scratch),
        compiler_params=pltpu.CompilerParams(vmem_limit_bytes=VMEM_LIMIT),
        cost_estimate=pl.CostEstimate(flops=flops, bytes_accessed=2 * moved, transcendentals=0),
        name=name,
    )


def dot(a, b):
    return jnp.dot(a, b, preferred_element_type=jnp.float32)


def lead_kernel(out):
    out[...] = jnp.zeros_like(out)


def lead():
    return local_call(lead_kernel, "lead", [like((8, 128), jnp.int32)], 0, LEAD_FLOPS)()[0]


def scalar_at(values, index):
    ids = lax.broadcasted_iota(jnp.int32, values.shape, 1)
    return jnp.sum(jnp.where(ids == index, values, 0).astype(jnp.float32))


def tables_kernel(first, counts, table, wants):
    here, orb = lax.axis_index("ao"), lax.axis_index("orb")
    slots = table.shape[1] // GROUPS
    named = jnp.where(table[...] // AO_DEV == here, table[...] % AO_DEV, 0).astype(jnp.float32)
    owner = lax.broadcasted_iota(jnp.int32, table.shape, 1) // slots
    rows = [jnp.max(jnp.where(owner == here ^ s, named, 0.0)) for s in range(GROUPS)]
    for offset in range(AO_DEV):
        count = scalar_at(counts[...], here * AO_DEV + offset)
        rows.append(count - (orb * (ORBS // 2)).astype(jnp.float32))
    row = lax.broadcasted_iota(jnp.int32, wants.shape, 0)
    out = first[0, 0:1].astype(jnp.float32).reshape(1, 1) + jnp.zeros(wants.shape, jnp.float32)
    for k, value in enumerate(rows):
        out = jnp.where(row == k, value, out)
    wants[...] = out.astype(jnp.int32)


def tables(first, counts, table, width):
    return local_call(
        tables_kernel, "tables", [like((8, width), jnp.int32)], 3, table.size
    )(first, counts.reshape(1, -1), table)[0]


def central_kernel(integrals, coeffs, *outs):
    mid = AO_DEV * BLOCK
    width = coeffs.shape[1] // len(outs)
    for offset in range(AO_DEV):
        low = mid - offset * BLOCK
        for p in range(integrals.shape[0]):
            slab = integrals[p, offset * BLOCK : (offset + 1) * BLOCK, low : low + mid]
            for c, out in enumerate(outs):
                out[offset, p] = dot(slab, coeffs[:, c * width : (c + 1) * width])


def central(integrals, coeffs):
    shape = (AO_DEV, integrals.shape[0], BLOCK, coeffs.shape[1] // CHUNKS)
    return local_call(
        central_kernel,
        "central",
        [like(shape, jnp.float32)] * CHUNKS,
        2,
        4 * integrals.size // WIN * coeffs.shape[1],
    )(integrals, coeffs)


def transform_kernel(start, wants, integrals, centre, inner, outer, *outs):
    mid = AO_DEV * BLOCK

    def blocks(prev, following):
        ids = start + lax.broadcasted_iota(jnp.int32, (BLOCK, outer.shape[1]), 1)
        for p in range(integrals.shape[0]):
            both = []
            for offset in range(AO_DEV):
                low = mid - offset * BLOCK
                slab = integrals[p, offset * BLOCK : (offset + 1) * BLOCK, :]
                values = centre[offset, p]
                values += dot(slab[:, :low], prev[offset * BLOCK :, :])
                values += dot(slab[:, low + mid :], following[: (offset + 1) * BLOCK, :])
                live = ids < wants[GROUPS + offset : GROUPS + offset + 1, :]
                both.append(jnp.where(live, values, 0.0))
            for s, out in enumerate(outs):
                out[p] = jnp.where(wants[s : s + 1, :] == 0, *both).astype(jnp.bfloat16)

    odd = lax.axis_index("ao") & 1
    pl.when(odd == 0)(lambda: blocks(inner, outer))
    pl.when(odd == 1)(lambda: blocks(outer, inner))


def shared_kernel(start, wants, integrals, centre, inner, outer, swapped, *refs):
    *outs, whole = refs
    aux = lax.axis_index("aux")
    width = inner.shape[1]
    whole[:, pl.ds(pl.multiple_of(aux * width, width), width)] = inner[...]
    whole[:, pl.ds(pl.multiple_of((1 - aux) * width, width), width)] = swapped[...]
    transform_kernel(start, wants, integrals, centre, whole, outer, *outs)


def transform(kernel, start, wants, integrals, centre, inner, outer, *swapped):
    shape = (integrals.shape[0], BLOCK, outer.shape[1])
    return local_call(
        functools.partial(kernel, start),
        "transform",
        [like(shape, jnp.bfloat16)] * GROUPS,
        5 + len(swapped),
        6 * AO_DEV * math.prod(shape) * integrals.shape[2] // WIN,
        [pltpu.VMEM(outer.shape, jnp.bfloat16)] * len(swapped),
    )(wants, integrals, centre, inner, outer, *swapped)


def form_pairs(pairs, blocks, grams):
    here = lax.axis_index("ao")
    slices = [[(ref, p) for ref in block for p in range(ref.shape[0])] for block in blocks]

    def product(left, right):
        total = None
        for (a, i), (b, j) in zip(slices[left], slices[right]):
            part = lax.dot_general(
                a[i], b[j], (((1,), (1,)), ((), ())), preferred_element_type=jnp.float32
            )
            total = part if total is None else total + part
        return total.reshape(grams.shape[1:])

    for bit in (0, 1):
        mine = [(k, a, b) for k, (a, b) in enumerate(pairs) if (a ^ b) >> 1 == bit]
        upper = (here >> bit) & 1

        @pl.when(upper == 0)
        def _(mine=mine):
            for k, a, b in mine:
                grams[k] = product(a, b)

        @pl.when(upper == 1)
        def _(mine=mine):
            for k, a, b in mine:
                grams[k] = product(b, a)


def early_kernel(live, table, *refs):
    used = 3 * CHUNKS
    own, middle, next_to = [refs[i : i + CHUNKS] for i in range(0, used, CHUNKS)]
    blocks = own, next_to, middle
    near, far, place, grams = refs[used:]
    here, aux, orb = (lax.axis_index(axis) for axis in ("ao", "aux", "orb"))
    slots, width = place.shape
    slot = lax.broadcasted_iota(jnp.int32, (slots, table.shape[1]), 0)
    column = lax.broadcasted_iota(jnp.int32, (slots, table.shape[1]), 1)
    shown = column == here * slots + slot
    sides = []
    for side in (0, 1):
        group = (table[side : side + 1, :] // AO_DEV).astype(jnp.float32)
        group = jnp.sum(jnp.where(shown, group, 0.0), axis=1, keepdims=True)
        sides.append(group.astype(jnp.int32) ^ here)
    low, high = jnp.minimum(*sides), jnp.maximum(*sides)
    index = jnp.where(high == 3, low + 3, jnp.where(high == 2, low + 1, 0))
    slot = lax.broadcasted_iota(jnp.int32, (slots, width), 0)
    count = scalar_at(live[...], here).astype(jnp.int32)
    place[...] = jnp.where(slot < count, index, len(ALL_PAIRS))
    form_pairs(EARLY_PAIRS, blocks, grams)
    for k in range(len(EARLY_PAIRS)):
        for core in (0, 1):
            near[core, k] = grams[k, 2 * aux + (orb ^ core)]
            far[core, k] = grams[k, 2 * (1 - aux) + (orb ^ core)].astype(jnp.bfloat16)


def late_kernel(*refs):
    used = GROUPS * CHUNKS
    own, middle, next_to, last = [refs[i : i + CHUNKS] for i in range(0, used, CHUNKS)]
    blocks = own, next_to, middle, last
    keep, give, grams = refs[used:]
    aux, orb = lax.axis_index("aux"), lax.axis_index("orb")
    form_pairs(LATE_PAIRS, blocks, grams)
    for k in range(len(LATE_PAIRS)):
        for chip in (0, 1):
            row = 2 * (aux ^ chip)
            keep[chip, k] = grams[k, row + orb]
            give[chip, k] = grams[k, row + 1 - orb]


def pair_flops(pairs, blocks):
    return 2 * len(pairs) * BLOCK * CHUNKS * blocks[0][0].size


def quarters(pairs):
    rows = BLOCK // 4
    return (2, len(pairs), rows, BLOCK), pltpu.VMEM((len(pairs), 4, rows, BLOCK), jnp.float32)


def early_pairs(live, table, blocks):
    shape, grams = quarters(EARLY_PAIRS)
    return local_call(
        early_kernel,
        "early_pairs",
        [
            like(shape, jnp.float32),
            like(shape, jnp.bfloat16),
            like((table.shape[1] // GROUPS, BLOCK), jnp.int32),
        ],
        2 + 3 * CHUNKS,
        pair_flops(EARLY_PAIRS, blocks),
        [grams],
    )(live.reshape(1, -1), table, *blocks[0], *blocks[2], *blocks[1])


def late_pairs(blocks):
    shape, grams = quarters(LATE_PAIRS)
    return local_call(
        late_kernel,
        "late_pairs",
        [like(shape, jnp.float32)] * 2,
        GROUPS * CHUNKS,
        pair_flops(LATE_PAIRS, blocks),
        [grams],
    )(*blocks[0], *blocks[2], *blocks[1], *blocks[3])


def spread_kernel(factor, place, near0, far0, got0, near1, got1, far1, out, sums, rows, sems):
    early = near0.shape[1]
    sums[:early] = (near0[0] + far0[0].astype(jnp.float32) + got0[...]) * factor
    sums[early:] = (near1[0] + got1[0] + far1[...].astype(jnp.float32)) * factor
    total, slots, width = out.shape
    masks = [place[...] == k for k in range(sums.shape[0])]

    def one(m, carry):
        row = jnp.zeros((slots, width), jnp.float32)
        for k, mask in enumerate(masks):
            values = jnp.broadcast_to(sums[k, pl.ds(m, 1), :], (slots, width))
            row = jnp.where(mask, values, row)
        rows[m] = row
        return carry

    step = total // SPREAD_STEPS
    copies = []
    for i in range(SPREAD_STEPS):
        lax.fori_loop(i * step, (i + 1) * step, one, 0, unroll=8)
        part = pl.ds(i * step, step)
        copies.append(pltpu.make_async_copy(rows.at[part], out.at[part], sems.at[i]))
        copies[-1].start()
    for copy in copies:
        copy.wait()


def spread(factor, place, *parts):
    rows = BLOCK // 4
    shape = (rows, place.shape[0], BLOCK)
    return local_call(
        functools.partial(spread_kernel, factor),
        "spread",
        [like(shape, jnp.float32)],
        1 + len(parts),
        6 * math.prod(shape),
        [
            pltpu.VMEM((len(ALL_PAIRS), rows, BLOCK), jnp.float32),
            pltpu.VMEM(shape, jnp.float32),
            pltpu.SemaphoreType.DMA((SPREAD_STEPS,)),
        ],
        IN_HBM,
    )(place, *parts)[0]


def six_pair_body(integrals, coeffs, pair_blocks, pair_count, orbital_count):
    width = coeffs.shape[1] // CHUNKS
    total_aux = integrals.shape[0] * lax.axis_size("aux")
    table = pair_blocks.T

    half = width // 2
    direct = lax.slice_in_dim(coeffs, 0, width, axis=1)
    inner0 = lax.ppermute(direct, "ao", INSIDE)
    outer0 = lax.ppermute(direct, "ao", OUTSIDE)
    first, rest = lax.optimization_barrier((lead(), coeffs))
    wants = tables(first, orbital_count, table, width)
    centres = central(integrals, rest)
    wants, centres, rest = lax.optimization_barrier((wants, centres, rest))
    mine = lax.dynamic_slice_in_dim(rest, width + lax.axis_index("aux") * half, half, axis=1)
    inner1 = lax.ppermute(mine, "ao", INSIDE)
    outer1 = lax.ppermute(lax.slice_in_dim(rest, width, 2 * width, axis=1), "ao", OUTSIDE)

    pieces = list(transform(transform_kernel, 0, wants, integrals, centres[0], inner0, outer0))
    blocks = [[piece] for piece in pieces]
    inner1, blocks[0][0] = lax.optimization_barrier((inner1, blocks[0][0]))
    swapped = lax.ppermute(inner1, "aux", SWAP)
    pieces = transform(
        shared_kernel, width, wants, integrals, centres[1], inner1, outer1, swapped
    )
    for block, piece in zip(blocks, pieces):
        block.append(piece)

    def fetch(s):
        swap = [(j, j ^ s) for j in range(GROUPS)]
        return [lax.ppermute(piece, "ao", swap) for piece in blocks[s]]

    middle = fetch(2)
    got = [blocks[0], fetch(1), middle]
    near0, across0, place = early_pairs(pair_count, table, got)
    far0 = lax.ppermute(across0, "aux", SWAP)
    got.append(fetch(3))
    near1, give1 = late_pairs(got)
    got1 = lax.ppermute(give1, "orb", SWAP)
    far1 = lax.ppermute((near1[1] + got1[1]).astype(jnp.bfloat16), "aux", SWAP)
    got0 = lax.ppermute(near0[1] + far0[1].astype(jnp.float32), "orb", SWAP)
    factor = 1.0 / math.sqrt(total_aux * ORBS)
    return spread(factor, place, near0, far0, got0, near1, got1, far1)


def solution(mesh):
    sizes = dict(mesh.shape)
    body = general_body
    if sizes["ao"] == 4 and sizes["aux"] == 2 and sizes["orb"] == 2:
        body = six_pair_body
    return jax.shard_map(
        body,
        mesh=mesh,
        in_specs=(
            P(("grp", "aux"), "ao", None),
            P(("grp", "ao"), "orb"),
            P("grp", None),
            P("grp"),
            P("grp"),
        ),
        out_specs=P(("aux", "orb"), ("grp", "ao"), None),
        check_vma=False,
    )
```

```python
import functools
import math

import jax
import jax.numpy as jnp
from jax import lax
from jax.experimental import pallas as pl
from jax.experimental.pallas import tpu as pltpu
from jax.sharding import PartitionSpec as P

BLOCK = 256
AO_DEV = 2
WIN = 5
ORBS = 1024
CHUNKS = 2
SPREAD_STEPS = 4
SPREAD_STEPS = 4
SPREAD_STEPS = 4
SPREAD_STEPS = 4
SPREAD_STEPS = 4
SPREAD_STEPS = 4
VMEM_LIMIT = 40 * 1024 * 1024
LEAD_FLOPS = 1 << 32


def with_halo(cells, sides, width):
    for axis, dim in sides:
        count = lax.axis_size(axis)
        ends = count - 1
        head = lax.slice_in_dim(cells, 0, width, axis=dim)
        tail = lax.slice_in_dim(cells, cells.shape[dim] - width, cells.shape[dim], axis=dim)
        cells = jnp.concatenate(
            [
                lax.ppermute(tail, axis, [(i, (i + 1) % count) for i in range(ends)]),
                cells,
                lax.ppermute(head, axis, [((i + 1) % count, i) for i in range(ends)]),
            ],
            axis=dim,
        )
    return cells


def general_body(integrals, coeffs, pair_blocks, pair_count, orbital_count):
    orb_local = coeffs.shape[1]
    aux_devices = lax.axis_size("aux")
    total_aux = integrals.shape[0] * aux_devices
    rim = WIN // 2 * BLOCK
    extended = with_halo(coeffs, (("ao", 0),), rim)
    ao_here = lax.axis_index("ao")
    orbital_ids = lax.axis_index("orb") * orb_local + jnp.arange(orb_local, dtype=jnp.int32)
    pieces = []
    for offset in range(AO_DEV):
        slab = integrals[:, offset * BLOCK : (offset + 1) * BLOCK, :]
        slot_range = extended[offset * BLOCK : offset * BLOCK + WIN * BLOCK]
        values = jnp.einsum("pml,li->pmi", slab, slot_range, preferred_element_type=jnp.float32)
        limit = orbital_count[ao_here * AO_DEV + offset]
        values = jnp.where((orbital_ids < limit)[None, None, :], values, 0.0)
        pieces.append(values.astype(jnp.bfloat16))
    transformed = jnp.stack(pieces)
    owners = lax.axis_size("ao")
    table = pair_blocks.reshape(owners, -1, 2)
    slots = table.shape[1]
    live = jnp.arange(slots, dtype=jnp.int32)[None, :] < pair_count[:, None]
    touched = live[:, :, None] & (table // AO_DEV == ao_here)
    wanted = jnp.max(jnp.where(touched, table % AO_DEV, 0), axis=(1, 2))
    outgoing = transformed[wanted]
    received = lax.all_to_all(outgoing, "ao", split_axis=0, concat_axis=0, tiled=True)
    owned = table[ao_here]
    factor = 1.0 / math.sqrt(total_aux * ORBS)
    weights = jnp.where(live[ao_here], factor, 0.0).astype(jnp.float32)
    left_source = owned[:, 0] // AO_DEV
    right_source = owned[:, 1] // AO_DEV
    right_factors = received[right_source]
    lefts = received[left_source]
    term = jnp.einsum("spmi,spni->msn", lefts, right_factors, preferred_element_type=jnp.float32)
    return lax.psum_scatter(
        term * weights[None, :, None], ("aux", "orb"), scatter_dimension=0, tiled=True
    )


EARLY_PAIRS = ((0, 1), (0, 2), (1, 2))
LATE_PAIRS = ((0, 3),), ((1, 3), (2, 3))
ALL_PAIRS = EARLY_PAIRS + LATE_PAIRS[0] + LATE_PAIRS[1]
GROUPS = 4
SWAP = [(0, 1), (1, 0)]
OUTSIDE = [(0, 1), (1, 0), (2, 3), (3, 2)]
INSIDE = [(1, 2), (2, 1)]

IN_HBM = pl.BlockSpec(memory_space=pltpu.HBM)
IN_VMEM = pl.BlockSpec(memory_space=pltpu.VMEM)


def like(shape, dtype):
    return jax.ShapeDtypeStruct(shape, dtype)


def local_call(kernel, name, out_shape, inputs, flops, scratch=(), out_spec=IN_VMEM):
    moved = sum(math.prod(o.shape) * o.dtype.itemsize for o in out_shape)
    return pl.pallas_call(
        kernel,
        out_shape=out_shape,
        in_specs=[IN_VMEM] * inputs,
        out_specs=[out_spec] * len(out_shape),
        scratch_shapes=list(scratch),
        compiler_params=pltpu.CompilerParams(vmem_limit_bytes=VMEM_LIMIT),
        cost_estimate=pl.CostEstimate(flops=flops, bytes_accessed=2 * moved, transcendentals=0),
        name=name,
    )


def dot(a, b):
    return jnp.dot(a, b, preferred_element_type=jnp.float32)


def lead_kernel(out):
    out[...] = jnp.zeros_like(out)


def lead():
    return local_call(lead_kernel, "lead", [like((8, 128), jnp.int32)], 0, LEAD_FLOPS)()[0]


def scalar_at(values, index):
    ids = lax.broadcasted_iota(jnp.int32, values.shape, 1)
    return jnp.sum(jnp.where(ids == index, values, 0).astype(jnp.float32))


def tables_kernel(first, counts, table, wants):
    here, orb = lax.axis_index("ao"), lax.axis_index("orb")
    slots = table.shape[1] // GROUPS
    named = jnp.where(table[...] // AO_DEV == here, table[...] % AO_DEV, 0).astype(jnp.float32)
    owner = lax.broadcasted_iota(jnp.int32, table.shape, 1) // slots
    rows = [jnp.max(jnp.where(owner == here ^ s, named, 0.0)) for s in range(GROUPS)]
    for offset in range(AO_DEV):
        count = scalar_at(counts[...], here * AO_DEV + offset)
        rows.append(count - (orb * (ORBS // 2)).astype(jnp.float32))
    row = lax.broadcasted_iota(jnp.int32, wants.shape, 0)
    out = first[0, 0:1].astype(jnp.float32).reshape(1, 1) + jnp.zeros(wants.shape, jnp.float32)
    for k, value in enumerate(rows):
        out = jnp.where(row == k, value, out)
    wants[...] = out.astype(jnp.int32)


def tables(first, counts, table, width):
    return local_call(
        tables_kernel, "tables", [like((8, width), jnp.int32)], 3, table.size
    )(first, counts.reshape(1, -1), table)[0]


def transform_kernel(start, wants, integrals, own, outer, inner, *outs):
    mid = AO_DEV * BLOCK

    def blocks(prev, following):
        ids = start + lax.broadcasted_iota(jnp.int32, (BLOCK, own.shape[1]), 1)
        for p in range(integrals.shape[0]):
            both = []
            for offset in range(AO_DEV):
                low = mid - offset * BLOCK
                slab = integrals[p, offset * BLOCK : (offset + 1) * BLOCK, :]
                values = dot(slab[:, low : low + mid], own[...])
                values += dot(slab[:, :low], prev[offset * BLOCK :, :])
                values += dot(slab[:, low + mid :], following[: (offset + 1) * BLOCK, :])
                live = ids < wants[GROUPS + offset : GROUPS + offset + 1, :]
                both.append(jnp.where(live, values, 0.0))
            for s, out in enumerate(outs):
                out[p] = jnp.where(wants[s : s + 1, :] == 0, *both).astype(jnp.bfloat16)

    odd = lax.axis_index("ao") & 1
    pl.when(odd == 0)(lambda: blocks(inner, outer))
    pl.when(odd == 1)(lambda: blocks(outer, inner))


def shared_kernel(start, wants, integrals, own, outer, inner, swapped, *refs):
    *outs, whole = refs
    aux = lax.axis_index("aux")
    width = inner.shape[1]
    whole[:, pl.ds(pl.multiple_of(aux * width, width), width)] = inner[...]
    whole[:, pl.ds(pl.multiple_of((1 - aux) * width, width), width)] = swapped[...]
    transform_kernel(start, wants, integrals, own, outer, whole, *outs)


def shared_transform(start, wants, integrals, own, outer, inner, swapped):
    shape = (integrals.shape[0], BLOCK, own.shape[1])
    return local_call(
        functools.partial(shared_kernel, start),
        "transform",
        [like(shape, jnp.bfloat16)] * GROUPS,
        6,
        2 * AO_DEV * math.prod(shape) * integrals.shape[2],
        [pltpu.VMEM(own.shape, jnp.bfloat16)],
    )(wants, integrals, own, outer, inner, swapped)


def transform(start, wants, integrals, own, outer, inner):
    shape = (integrals.shape[0], BLOCK, own.shape[1])
    return local_call(
        functools.partial(transform_kernel, start),
        "transform",
        [like(shape, jnp.bfloat16)] * GROUPS,
        5,
        2 * AO_DEV * math.prod(shape) * integrals.shape[2],
    )(wants, integrals, own, outer, inner)


def form_pairs(pairs, blocks, grams):
    here = lax.axis_index("ao")
    slices = [[(ref, p) for ref in block for p in range(ref.shape[0])] for block in blocks]

    def product(left, right):
        total = None
        for (a, i), (b, j) in zip(slices[left], slices[right]):
            part = lax.dot_general(
                a[i], b[j], (((1,), (1,)), ((), ())), preferred_element_type=jnp.float32
            )
            total = part if total is None else total + part
        return total.reshape(grams.shape[1:])

    for bit in (0, 1):
        mine = [(k, a, b) for k, (a, b) in enumerate(pairs) if (a ^ b) >> 1 == bit]
        upper = (here >> bit) & 1

        @pl.when(upper == 0)
        def _(mine=mine):
            for k, a, b in mine:
                grams[k] = product(a, b)

        @pl.when(upper == 1)
        def _(mine=mine):
            for k, a, b in mine:
                grams[k] = product(b, a)


def early_kernel(live, table, *refs):
    used = 3 * CHUNKS
    own, middle, next_to = [refs[i : i + CHUNKS] for i in range(0, used, CHUNKS)]
    blocks = own, next_to, middle
    near, far, place, grams = refs[used:]
    here, aux, orb = (lax.axis_index(axis) for axis in ("ao", "aux", "orb"))
    slots, width = place.shape
    slot = lax.broadcasted_iota(jnp.int32, (slots, table.shape[1]), 0)
    column = lax.broadcasted_iota(jnp.int32, (slots, table.shape[1]), 1)
    shown = column == here * slots + slot
    sides = []
    for side in (0, 1):
        group = (table[side : side + 1, :] // AO_DEV).astype(jnp.float32)
        group = jnp.sum(jnp.where(shown, group, 0.0), axis=1, keepdims=True)
        sides.append(group.astype(jnp.int32) ^ here)
    low, high = jnp.minimum(*sides), jnp.maximum(*sides)
    index = jnp.where(high == 3, low + 3, jnp.where(high == 2, low + 1, 0))
    slot = lax.broadcasted_iota(jnp.int32, (slots, width), 0)
    count = scalar_at(live[...], here).astype(jnp.int32)
    place[...] = jnp.where(slot < count, index, len(ALL_PAIRS))
    form_pairs(EARLY_PAIRS, blocks, grams)
    for k in range(len(EARLY_PAIRS)):
        for core in (0, 1):
            near[core, k] = grams[k, 2 * aux + (orb ^ core)]
            far[core, k] = grams[k, 2 * (1 - aux) + (orb ^ core)].astype(jnp.bfloat16)


def late_kernel(pairs, *refs):
    used = GROUPS * CHUNKS
    own, middle, next_to, last = [refs[i : i + CHUNKS] for i in range(0, used, CHUNKS)]
    blocks = own, next_to, middle, last
    keep, give, grams = refs[used:]
    aux, orb = lax.axis_index("aux"), lax.axis_index("orb")
    form_pairs(pairs, blocks, grams)
    for k in range(len(pairs)):
        for chip in (0, 1):
            row = 2 * (aux ^ chip)
            keep[chip, k] = grams[k, row + orb]
            give[chip, k] = grams[k, row + 1 - orb]


def pair_flops(pairs, blocks):
    return 2 * len(pairs) * BLOCK * CHUNKS * blocks[0][0].size


def quarters(pairs):
    rows = BLOCK // 4
    return (2, len(pairs), rows, BLOCK), pltpu.VMEM((len(pairs), 4, rows, BLOCK), jnp.float32)


def early_pairs(live, table, blocks):
    shape, grams = quarters(EARLY_PAIRS)
    return local_call(
        early_kernel,
        "early_pairs",
        [
            like(shape, jnp.float32),
            like(shape, jnp.bfloat16),
            like((table.shape[1] // GROUPS, BLOCK), jnp.int32),
        ],
        2 + 3 * CHUNKS,
        pair_flops(EARLY_PAIRS, blocks),
        [grams],
    )(live.reshape(1, -1), table, *blocks[0], *blocks[2], *blocks[1])


def late_pairs(pairs, blocks):
    shape, grams = quarters(pairs)
    return local_call(
        functools.partial(late_kernel, pairs),
        "late_pairs",
        [like(shape, jnp.float32)] * 2,
        GROUPS * CHUNKS,
        pair_flops(pairs, blocks),
        [grams],
    )(*blocks[0], *blocks[2], *blocks[1], *blocks[3])


def spread_kernel(factor, place, near, far, got, *refs):
    *late, out, sums, rows, sems = refs
    done = near.shape[1]
    sums[:done] = (near[0] + far[0].astype(jnp.float32) + got[...]) * factor
    for i in range(0, len(late), 3):
        near, got, far = late[i : i + 3]
        more = done + near.shape[1]
        sums[done:more] = (near[0] + got[0] + far[...].astype(jnp.float32)) * factor
        done = more
    total, slots, width = out.shape
    masks = [place[...] == k for k in range(sums.shape[0])]

    def one(m, carry):
        row = jnp.zeros((slots, width), jnp.float32)
        for k, mask in enumerate(masks):
            values = jnp.broadcast_to(sums[k, pl.ds(m, 1), :], (slots, width))
            row = jnp.where(mask, values, row)
        rows[m] = row
        return carry

    step = total // SPREAD_STEPS
    copies = []
    for i in range(SPREAD_STEPS):
        lax.fori_loop(i * step, (i + 1) * step, one, 0, unroll=8)
        part = pl.ds(i * step, step)
        copies.append(pltpu.make_async_copy(rows.at[part], out.at[part], sems.at[i]))
        copies[-1].start()
    for copy in copies:
        copy.wait()


def spread(factor, place, *parts):
    rows = BLOCK // 4
    shape = (rows, place.shape[0], BLOCK)
    return local_call(
        functools.partial(spread_kernel, factor),
        "spread",
        [like(shape, jnp.float32)],
        1 + len(parts),
        6 * math.prod(shape),
        [
            pltpu.VMEM((len(ALL_PAIRS), rows, BLOCK), jnp.float32),
            pltpu.VMEM(shape, jnp.float32),
            pltpu.SemaphoreType.DMA((SPREAD_STEPS,)),
        ],
        IN_HBM,
    )(place, *parts)[0]


def six_pair_body(integrals, coeffs, pair_blocks, pair_count, orbital_count):
    width = coeffs.shape[1] // CHUNKS
    total_aux = integrals.shape[0] * lax.axis_size("aux")
    table = pair_blocks.T

    half = width // 2
    parts = [lax.slice_in_dim(coeffs, 0, width, axis=1)]
    first, rest = lax.optimization_barrier((lead(), coeffs))
    parts.append(lax.slice_in_dim(rest, width, 2 * width, axis=1))
    mine = lax.dynamic_slice_in_dim(rest, width + lax.axis_index("aux") * half, half, axis=1)
    inner = [lax.ppermute(part, "ao", INSIDE) for part in (parts[0], mine)]
    outer = [lax.ppermute(part, "ao", OUTSIDE) for part in parts]
    wants = tables(first, orbital_count, table, width)

    pieces = list(transform(0, wants, integrals, parts[0], outer[0], inner[0]))
    blocks = [[piece] for piece in pieces]
    inner[1], blocks[0][0] = lax.optimization_barrier((inner[1], blocks[0][0]))
    swapped = lax.ppermute(inner[1], "aux", SWAP)
    pieces = shared_transform(
        width, wants, integrals, parts[1], outer[1], inner[1], swapped
    )
    for block, piece in zip(blocks, pieces):
        block.append(piece)

    def fetch(s):
        swap = [(j, j ^ s) for j in range(GROUPS)]
        return [lax.ppermute(piece, "ao", swap) for piece in blocks[s]]

    middle = fetch(2)
    got = [blocks[0], fetch(1), middle]
    near0, across0, place = early_pairs(pair_count, table, got)
    far0 = lax.ppermute(across0, "aux", SWAP)
    got.append(fetch(3))
    late = []
    for near1, give1 in [late_pairs(pairs, got) for pairs in LATE_PAIRS]:
        got1 = lax.ppermute(give1, "orb", SWAP)
        far1 = lax.ppermute((near1[1] + got1[1]).astype(jnp.bfloat16), "aux", SWAP)
        late += [near1, got1, far1]
    got0 = lax.ppermute(near0[1] + far0[1].astype(jnp.float32), "orb", SWAP)
    factor = 1.0 / math.sqrt(total_aux * ORBS)
    return spread(factor, place, near0, far0, got0, *late)


def solution(mesh):
    sizes = dict(mesh.shape)
    body = general_body
    if sizes["ao"] == 4 and sizes["aux"] == 2 and sizes["orb"] == 2:
        body = six_pair_body
    return jax.shard_map(
        body,
        mesh=mesh,
        in_specs=(
            P(("grp", "aux"), "ao", None),
            P(("grp", "ao"), "orb"),
            P("grp", None),
            P("grp"),
            P("grp"),
        ),
        out_specs=P(("aux", "orb"), ("grp", "ao"), None),
        check_vma=False,
    )
```

```python
import functools
import math

import jax
import jax.numpy as jnp
from jax import lax
from jax.experimental import pallas as pl
from jax.experimental.pallas import tpu as pltpu
from jax.sharding import PartitionSpec as P

BLOCK = 256
AO_DEV = 2
WIN = 5
ORBS = 1024
CHUNKS = 2
SPREAD_STEPS = 4
SPREAD_STEPS = 4
SPREAD_STEPS = 4
SPREAD_STEPS = 4
SPREAD_STEPS = 4
SPREAD_STEPS = 4
VMEM_LIMIT = 40 * 1024 * 1024
LEAD_FLOPS = 1 << 32


def with_halo(cells, sides, width):
    for axis, dim in sides:
        count = lax.axis_size(axis)
        ends = count - 1
        head = lax.slice_in_dim(cells, 0, width, axis=dim)
        tail = lax.slice_in_dim(cells, cells.shape[dim] - width, cells.shape[dim], axis=dim)
        cells = jnp.concatenate(
            [
                lax.ppermute(tail, axis, [(i, (i + 1) % count) for i in range(ends)]),
                cells,
                lax.ppermute(head, axis, [((i + 1) % count, i) for i in range(ends)]),
            ],
            axis=dim,
        )
    return cells


def general_body(integrals, coeffs, pair_blocks, pair_count, orbital_count):
    orb_local = coeffs.shape[1]
    aux_devices = lax.axis_size("aux")
    total_aux = integrals.shape[0] * aux_devices
    rim = WIN // 2 * BLOCK
    extended = with_halo(coeffs, (("ao", 0),), rim)
    ao_here = lax.axis_index("ao")
    orbital_ids = lax.axis_index("orb") * orb_local + jnp.arange(orb_local, dtype=jnp.int32)
    pieces = []
    for offset in range(AO_DEV):
        slab = integrals[:, offset * BLOCK : (offset + 1) * BLOCK, :]
        slot_range = extended[offset * BLOCK : offset * BLOCK + WIN * BLOCK]
        values = jnp.einsum("pml,li->pmi", slab, slot_range, preferred_element_type=jnp.float32)
        limit = orbital_count[ao_here * AO_DEV + offset]
        values = jnp.where((orbital_ids < limit)[None, None, :], values, 0.0)
        pieces.append(values.astype(jnp.bfloat16))
    transformed = jnp.stack(pieces)
    owners = lax.axis_size("ao")
    table = pair_blocks.reshape(owners, -1, 2)
    slots = table.shape[1]
    live = jnp.arange(slots, dtype=jnp.int32)[None, :] < pair_count[:, None]
    touched = live[:, :, None] & (table // AO_DEV == ao_here)
    wanted = jnp.max(jnp.where(touched, table % AO_DEV, 0), axis=(1, 2))
    outgoing = transformed[wanted]
    received = lax.all_to_all(outgoing, "ao", split_axis=0, concat_axis=0, tiled=True)
    owned = table[ao_here]
    factor = 1.0 / math.sqrt(total_aux * ORBS)
    weights = jnp.where(live[ao_here], factor, 0.0).astype(jnp.float32)
    left_source = owned[:, 0] // AO_DEV
    right_source = owned[:, 1] // AO_DEV
    right_factors = received[right_source]
    lefts = received[left_source]
    term = jnp.einsum("spmi,spni->msn", lefts, right_factors, preferred_element_type=jnp.float32)
    return lax.psum_scatter(
        term * weights[None, :, None], ("aux", "orb"), scatter_dimension=0, tiled=True
    )


EARLY_PAIRS = ((0, 1), (0, 2), (1, 2))
LATE_PAIRS = ((0, 3), (1, 3), (2, 3))
ALL_PAIRS = EARLY_PAIRS + LATE_PAIRS
GROUPS = 4
SWAP = [(0, 1), (1, 0)]
OUTSIDE = [(0, 1), (1, 0), (2, 3), (3, 2)]
INSIDE = [(1, 2), (2, 1)]

IN_HBM = pl.BlockSpec(memory_space=pltpu.HBM)
IN_VMEM = pl.BlockSpec(memory_space=pltpu.VMEM)


def like(shape, dtype):
    return jax.ShapeDtypeStruct(shape, dtype)


def local_call(kernel, name, out_shape, inputs, flops, scratch=(), out_spec=IN_VMEM):
    moved = sum(math.prod(o.shape) * o.dtype.itemsize for o in out_shape)
    return pl.pallas_call(
        kernel,
        out_shape=out_shape,
        in_specs=[IN_VMEM] * inputs,
        out_specs=[out_spec] * len(out_shape),
        scratch_shapes=list(scratch),
        compiler_params=pltpu.CompilerParams(vmem_limit_bytes=VMEM_LIMIT),
        cost_estimate=pl.CostEstimate(flops=flops, bytes_accessed=2 * moved, transcendentals=0),
        name=name,
    )


def dot(a, b):
    return jnp.dot(a, b, preferred_element_type=jnp.float32)


def lead_kernel(out):
    out[...] = jnp.zeros_like(out)


def lead():
    return local_call(lead_kernel, "lead", [like((8, 128), jnp.int32)], 0, LEAD_FLOPS)()[0]


def scalar_at(values, index):
    ids = lax.broadcasted_iota(jnp.int32, values.shape, 1)
    return jnp.sum(jnp.where(ids == index, values, 0).astype(jnp.float32))


def tables_kernel(first, counts, table, wants):
    here, orb = lax.axis_index("ao"), lax.axis_index("orb")
    slots = table.shape[1] // GROUPS
    named = jnp.where(table[...] // AO_DEV == here, table[...] % AO_DEV, 0).astype(jnp.float32)
    owner = lax.broadcasted_iota(jnp.int32, table.shape, 1) // slots
    rows = [jnp.max(jnp.where(owner == here ^ s, named, 0.0)) for s in range(GROUPS)]
    for offset in range(AO_DEV):
        count = scalar_at(counts[...], here * AO_DEV + offset)
        rows.append(count - (orb * (ORBS // 2)).astype(jnp.float32))
    row = lax.broadcasted_iota(jnp.int32, wants.shape, 0)
    out = first[0, 0:1].astype(jnp.float32).reshape(1, 1) + jnp.zeros(wants.shape, jnp.float32)
    for k, value in enumerate(rows):
        out = jnp.where(row == k, value, out)
    wants[...] = out.astype(jnp.int32)


def tables(first, counts, table, width):
    return local_call(
        tables_kernel, "tables", [like((8, width), jnp.int32)], 3, table.size
    )(first, counts.reshape(1, -1), table)[0]


def transform_kernel(start, wants, integrals, own, outer, inner, *outs):
    mid = AO_DEV * BLOCK

    def blocks(prev, following):
        ids = start + lax.broadcasted_iota(jnp.int32, (BLOCK, own.shape[1]), 1)
        for p in range(integrals.shape[0]):
            both = []
            for offset in range(AO_DEV):
                low = mid - offset * BLOCK
                slab = integrals[p, offset * BLOCK : (offset + 1) * BLOCK, :]
                values = dot(slab[:, low : low + mid], own[...])
                values += dot(slab[:, :low], prev[offset * BLOCK :, :])
                values += dot(slab[:, low + mid :], following[: (offset + 1) * BLOCK, :])
                live = ids < wants[GROUPS + offset : GROUPS + offset + 1, :]
                both.append(jnp.where(live, values, 0.0))
            for s, out in enumerate(outs):
                out[p] = jnp.where(wants[s : s + 1, :] == 0, *both).astype(jnp.bfloat16)

    odd = lax.axis_index("ao") & 1
    pl.when(odd == 0)(lambda: blocks(inner, outer))
    pl.when(odd == 1)(lambda: blocks(outer, inner))


def shared_kernel(start, wants, integrals, own, outer, inner, swapped, *refs):
    *outs, whole = refs
    aux = lax.axis_index("aux")
    width = inner.shape[1]
    whole[:, pl.ds(pl.multiple_of(aux * width, width), width)] = inner[...]
    whole[:, pl.ds(pl.multiple_of((1 - aux) * width, width), width)] = swapped[...]
    transform_kernel(start, wants, integrals, own, outer, whole, *outs)


def shared_transform(start, wants, integrals, own, outer, inner, swapped):
    shape = (integrals.shape[0], BLOCK, own.shape[1])
    return local_call(
        functools.partial(shared_kernel, start),
        "transform",
        [like(shape, jnp.bfloat16)] * GROUPS,
        6,
        2 * AO_DEV * math.prod(shape) * integrals.shape[2],
        [pltpu.VMEM(own.shape, jnp.bfloat16)],
    )(wants, integrals, own, outer, inner, swapped)


def transform(start, wants, integrals, own, outer, inner):
    shape = (integrals.shape[0], BLOCK, own.shape[1])
    return local_call(
        functools.partial(transform_kernel, start),
        "transform",
        [like(shape, jnp.bfloat16)] * GROUPS,
        5,
        2 * AO_DEV * math.prod(shape) * integrals.shape[2],
    )(wants, integrals, own, outer, inner)


def form_pairs(pairs, blocks, grams):
    here = lax.axis_index("ao")
    slices = [[(ref, p) for ref in block for p in range(ref.shape[0])] for block in blocks]

    def product(left, right):
        total = None
        for (a, i), (b, j) in zip(slices[left], slices[right]):
            part = lax.dot_general(
                a[i], b[j], (((1,), (1,)), ((), ())), preferred_element_type=jnp.float32
            )
            total = part if total is None else total + part
        return total.reshape(grams.shape[1:])

    for bit in (0, 1):
        mine = [(k, a, b) for k, (a, b) in enumerate(pairs) if (a ^ b) >> 1 == bit]
        upper = (here >> bit) & 1

        @pl.when(upper == 0)
        def _(mine=mine):
            for k, a, b in mine:
                grams[k] = product(a, b)

        @pl.when(upper == 1)
        def _(mine=mine):
            for k, a, b in mine:
                grams[k] = product(b, a)


def early_kernel(live, table, *refs):
    own, (middle0, next0, _, middle1, next1), refs = refs[:CHUNKS], refs[CHUNKS:-4], refs[-4:]
    blocks = own, (next0, next1), (middle0, middle1)
    near, far, place, grams = refs
    here, aux, orb = (lax.axis_index(axis) for axis in ("ao", "aux", "orb"))
    slots, width = place.shape
    slot = lax.broadcasted_iota(jnp.int32, (slots, table.shape[1]), 0)
    column = lax.broadcasted_iota(jnp.int32, (slots, table.shape[1]), 1)
    shown = column == here * slots + slot
    sides = []
    for side in (0, 1):
        group = (table[side : side + 1, :] // AO_DEV).astype(jnp.float32)
        group = jnp.sum(jnp.where(shown, group, 0.0), axis=1, keepdims=True)
        sides.append(group.astype(jnp.int32) ^ here)
    low, high = jnp.minimum(*sides), jnp.maximum(*sides)
    index = jnp.where(high == 3, low + 3, jnp.where(high == 2, low + 1, 0))
    slot = lax.broadcasted_iota(jnp.int32, (slots, width), 0)
    count = scalar_at(live[...], here).astype(jnp.int32)
    place[...] = jnp.where(slot < count, index, len(ALL_PAIRS))
    form_pairs(EARLY_PAIRS, blocks, grams)
    for k in range(len(EARLY_PAIRS)):
        for core in (0, 1):
            near[core, k] = grams[k, 2 * aux + (orb ^ core)]
            far[core, k] = grams[k, 2 * (1 - aux) + (orb ^ core)].astype(jnp.bfloat16)


def late_kernel(*refs):
    used = GROUPS * CHUNKS
    own, middle, next_to, last = [refs[i : i + CHUNKS] for i in range(0, used, CHUNKS)]
    blocks = own, next_to, middle, last
    keep, give, grams = refs[used:]
    aux, orb = lax.axis_index("aux"), lax.axis_index("orb")
    form_pairs(LATE_PAIRS, blocks, grams)
    for k in range(len(LATE_PAIRS)):
        for chip in (0, 1):
            row = 2 * (aux ^ chip)
            keep[chip, k] = grams[k, row + orb]
            give[chip, k] = grams[k, row + 1 - orb]


def pair_flops(pairs, blocks):
    return 2 * len(pairs) * BLOCK * CHUNKS * blocks[0][0].size


def quarters(pairs):
    rows = BLOCK // 4
    return (2, len(pairs), rows, BLOCK), pltpu.VMEM((len(pairs), 4, rows, BLOCK), jnp.float32)


def early_pairs(live, table, blocks):
    shape, grams = quarters(EARLY_PAIRS)
    own, (next0, next1), (middle0, middle1), (last0, _) = blocks
    order = middle0, next0, last0, middle1, next1
    return local_call(
        early_kernel,
        "early_pairs",
        [
            like(shape, jnp.float32),
            like(shape, jnp.bfloat16),
            like((table.shape[1] // GROUPS, BLOCK), jnp.int32),
        ],
        3 + 3 * CHUNKS,
        pair_flops(EARLY_PAIRS, blocks),
        [grams],
    )(live.reshape(1, -1), table, *blocks[0], *order)


def late_pairs(blocks):
    shape, grams = quarters(LATE_PAIRS)
    return local_call(
        late_kernel,
        "late_pairs",
        [like(shape, jnp.float32)] * 2,
        GROUPS * CHUNKS,
        pair_flops(LATE_PAIRS, blocks),
        [grams],
    )(*blocks[0], *blocks[2], *blocks[1], *blocks[3])


def spread_kernel(factor, place, near0, far0, got0, near1, got1, far1, out, sums, rows, sems):
    early = near0.shape[1]
    sums[:early] = (near0[0] + far0[0].astype(jnp.float32) + got0[...]) * factor
    sums[early:] = (near1[0] + got1[0] + far1[...].astype(jnp.float32)) * factor
    total, slots, width = out.shape
    masks = [place[...] == k for k in range(sums.shape[0])]

    def one(m, carry):
        row = jnp.zeros((slots, width), jnp.float32)
        for k, mask in enumerate(masks):
            values = jnp.broadcast_to(sums[k, pl.ds(m, 1), :], (slots, width))
            row = jnp.where(mask, values, row)
        rows[m] = row
        return carry

    step = total // SPREAD_STEPS
    copies = []
    for i in range(SPREAD_STEPS):
        lax.fori_loop(i * step, (i + 1) * step, one, 0, unroll=8)
        part = pl.ds(i * step, step)
        copies.append(pltpu.make_async_copy(rows.at[part], out.at[part], sems.at[i]))
        copies[-1].start()
    for copy in copies:
        copy.wait()


def spread(factor, place, *parts):
    rows = BLOCK // 4
    shape = (rows, place.shape[0], BLOCK)
    return local_call(
        functools.partial(spread_kernel, factor),
        "spread",
        [like(shape, jnp.float32)],
        1 + len(parts),
        6 * math.prod(shape),
        [
            pltpu.VMEM((len(ALL_PAIRS), rows, BLOCK), jnp.float32),
            pltpu.VMEM(shape, jnp.float32),
            pltpu.SemaphoreType.DMA((SPREAD_STEPS,)),
        ],
        IN_HBM,
    )(place, *parts)[0]


def six_pair_body(integrals, coeffs, pair_blocks, pair_count, orbital_count):
    width = coeffs.shape[1] // CHUNKS
    total_aux = integrals.shape[0] * lax.axis_size("aux")
    table = pair_blocks.T

    half = width // 2
    parts = [lax.slice_in_dim(coeffs, 0, width, axis=1)]
    first, rest = lax.optimization_barrier((lead(), coeffs))
    parts.append(lax.slice_in_dim(rest, width, 2 * width, axis=1))
    mine = lax.dynamic_slice_in_dim(rest, width + lax.axis_index("aux") * half, half, axis=1)
    inner = [lax.ppermute(part, "ao", INSIDE) for part in (parts[0], mine)]
    outer = [lax.ppermute(part, "ao", OUTSIDE) for part in parts]
    wants = tables(first, orbital_count, table, width)

    pieces = list(transform(0, wants, integrals, parts[0], outer[0], inner[0]))
    blocks = [[piece] for piece in pieces]
    inner[1], blocks[0][0] = lax.optimization_barrier((inner[1], blocks[0][0]))
    swapped = lax.ppermute(inner[1], "aux", SWAP)
    pieces = shared_transform(
        width, wants, integrals, parts[1], outer[1], inner[1], swapped
    )
    for block, piece in zip(blocks, pieces):
        block.append(piece)

    def fetch(s):
        swap = [(j, j ^ s) for j in range(GROUPS)]
        return [lax.ppermute(piece, "ao", swap) for piece in blocks[s]]

    middle = fetch(2)
    got = [blocks[0], fetch(1), middle]
    got.append(fetch(3))
    near0, across0, place = early_pairs(pair_count, table, got)
    far0 = lax.ppermute(across0, "aux", SWAP)
    near1, give1 = late_pairs(got)
    got1 = lax.ppermute(give1, "orb", SWAP)
    far1 = lax.ppermute((near1[1] + got1[1]).astype(jnp.bfloat16), "aux", SWAP)
    got0 = lax.ppermute(near0[1] + far0[1].astype(jnp.float32), "orb", SWAP)
    factor = 1.0 / math.sqrt(total_aux * ORBS)
    return spread(factor, place, near0, far0, got0, near1, got1, far1)


def solution(mesh):
    sizes = dict(mesh.shape)
    body = general_body
    if sizes["ao"] == 4 and sizes["aux"] == 2 and sizes["orb"] == 2:
        body = six_pair_body
    return jax.shard_map(
        body,
        mesh=mesh,
        in_specs=(
            P(("grp", "aux"), "ao", None),
            P(("grp", "ao"), "orb"),
            P("grp", None),
            P("grp"),
            P("grp"),
        ),
        out_specs=P(("aux", "orb"), ("grp", "ao"), None),
        check_vma=False,
    )
```

```python
import functools
import math

import jax
import jax.numpy as jnp
from jax import lax
from jax.experimental import pallas as pl
from jax.experimental.pallas import tpu as pltpu
from jax.sharding import PartitionSpec as P

BLOCK = 256
AO_DEV = 2
WIN = 5
ORBS = 1024
CHUNKS = 2
SPREAD_STEPS = 4
SPREAD_STEPS = 4
SPREAD_STEPS = 4
SPREAD_STEPS = 4
SPREAD_STEPS = 4
SPREAD_STEPS = 4
VMEM_LIMIT = 40 * 1024 * 1024
LEAD_FLOPS = 1 << 32
CUT_LIMIT = 63 * 1024 * 1024


def with_halo(cells, sides, width):
    for axis, dim in sides:
        count = lax.axis_size(axis)
        ends = count - 1
        head = lax.slice_in_dim(cells, 0, width, axis=dim)
        tail = lax.slice_in_dim(cells, cells.shape[dim] - width, cells.shape[dim], axis=dim)
        cells = jnp.concatenate(
            [
                lax.ppermute(tail, axis, [(i, (i + 1) % count) for i in range(ends)]),
                cells,
                lax.ppermute(head, axis, [((i + 1) % count, i) for i in range(ends)]),
            ],
            axis=dim,
        )
    return cells


def general_body(integrals, coeffs, pair_blocks, pair_count, orbital_count):
    orb_local = coeffs.shape[1]
    aux_devices = lax.axis_size("aux")
    total_aux = integrals.shape[0] * aux_devices
    rim = WIN // 2 * BLOCK
    extended = with_halo(coeffs, (("ao", 0),), rim)
    ao_here = lax.axis_index("ao")
    orbital_ids = lax.axis_index("orb") * orb_local + jnp.arange(orb_local, dtype=jnp.int32)
    pieces = []
    for offset in range(AO_DEV):
        slab = integrals[:, offset * BLOCK : (offset + 1) * BLOCK, :]
        slot_range = extended[offset * BLOCK : offset * BLOCK + WIN * BLOCK]
        values = jnp.einsum("pml,li->pmi", slab, slot_range, preferred_element_type=jnp.float32)
        limit = orbital_count[ao_here * AO_DEV + offset]
        values = jnp.where((orbital_ids < limit)[None, None, :], values, 0.0)
        pieces.append(values.astype(jnp.bfloat16))
    transformed = jnp.stack(pieces)
    owners = lax.axis_size("ao")
    table = pair_blocks.reshape(owners, -1, 2)
    slots = table.shape[1]
    live = jnp.arange(slots, dtype=jnp.int32)[None, :] < pair_count[:, None]
    touched = live[:, :, None] & (table // AO_DEV == ao_here)
    wanted = jnp.max(jnp.where(touched, table % AO_DEV, 0), axis=(1, 2))
    outgoing = transformed[wanted]
    received = lax.all_to_all(outgoing, "ao", split_axis=0, concat_axis=0, tiled=True)
    owned = table[ao_here]
    factor = 1.0 / math.sqrt(total_aux * ORBS)
    weights = jnp.where(live[ao_here], factor, 0.0).astype(jnp.float32)
    left_source = owned[:, 0] // AO_DEV
    right_source = owned[:, 1] // AO_DEV
    right_factors = received[right_source]
    lefts = received[left_source]
    term = jnp.einsum("spmi,spni->msn", lefts, right_factors, preferred_element_type=jnp.float32)
    return lax.psum_scatter(
        term * weights[None, :, None], ("aux", "orb"), scatter_dimension=0, tiled=True
    )


EARLY_PAIRS = ((0, 1), (0, 2), (1, 2))
LATE_PAIRS = ((0, 3), (1, 3), (2, 3))
ALL_PAIRS = EARLY_PAIRS + LATE_PAIRS
GROUPS = 4
SWAP = [(0, 1), (1, 0)]
OUTSIDE = [(0, 1), (1, 0), (2, 3), (3, 2)]
INSIDE = [(1, 2), (2, 1)]

IN_HBM = pl.BlockSpec(memory_space=pltpu.HBM)
IN_VMEM = pl.BlockSpec(memory_space=pltpu.VMEM)


def like(shape, dtype):
    return jax.ShapeDtypeStruct(shape, dtype)


def local_call(kernel, name, out_shape, inputs, flops, scratch=(), out_spec=IN_VMEM):
    moved = sum(math.prod(o.shape) * o.dtype.itemsize for o in out_shape)
    return pl.pallas_call(
        kernel,
        out_shape=out_shape,
        in_specs=[IN_VMEM] * inputs,
        out_specs=[out_spec] * len(out_shape),
        scratch_shapes=list(scratch),
        compiler_params=pltpu.CompilerParams(vmem_limit_bytes=VMEM_LIMIT),
        cost_estimate=pl.CostEstimate(flops=flops, bytes_accessed=2 * moved, transcendentals=0),
        name=name,
    )


def dot(a, b):
    return jnp.dot(a, b, preferred_element_type=jnp.float32)


def cut_kernel(coeffs, direct, shared, mine, sems):
    width, half = direct.shape[1], mine.shape[1]
    start = pl.multiple_of(width + lax.axis_index("aux") * half, half)
    copies = [
        pltpu.make_async_copy(coeffs.at[:, columns], out, sems.at[i])
        for i, (columns, out) in enumerate(
            ((pl.ds(0, width), direct), (pl.ds(start, half), mine), (pl.ds(width, width), shared))
        )
    ]
    for copy in copies:
        copy.start()
    for copy in copies:
        copy.wait()


def cut(coeffs):
    rows, columns = coeffs.shape
    width = columns // CHUNKS
    return pl.pallas_call(
        cut_kernel,
        out_shape=[like((rows, n), coeffs.dtype) for n in (width, width, width // 2)],
        in_specs=[IN_HBM],
        out_specs=[IN_HBM] * 3,
        scratch_shapes=[pltpu.SemaphoreType.DMA((3,))],
        compiler_params=pltpu.CompilerParams(vmem_limit_bytes=CUT_LIMIT),
        cost_estimate=pl.CostEstimate(flops=LEAD_FLOPS, bytes_accessed=0, transcendentals=0),
        name="cut",
    )(coeffs)


def scalar_at(values, index):
    ids = lax.broadcasted_iota(jnp.int32, values.shape, 1)
    return jnp.sum(jnp.where(ids == index, values, 0).astype(jnp.float32))


def tables_kernel(counts, table, wants):
    here, orb = lax.axis_index("ao"), lax.axis_index("orb")
    slots = table.shape[1] // GROUPS
    named = jnp.where(table[...] // AO_DEV == here, table[...] % AO_DEV, 0).astype(jnp.float32)
    owner = lax.broadcasted_iota(jnp.int32, table.shape, 1) // slots
    rows = [jnp.max(jnp.where(owner == here ^ s, named, 0.0)) for s in range(GROUPS)]
    for offset in range(AO_DEV):
        count = scalar_at(counts[...], here * AO_DEV + offset)
        rows.append(count - (orb * (ORBS // 2)).astype(jnp.float32))
    row = lax.broadcasted_iota(jnp.int32, wants.shape, 0)
    out = jnp.zeros(wants.shape, jnp.float32)
    for k, value in enumerate(rows):
        out = jnp.where(row == k, value, out)
    wants[...] = out.astype(jnp.int32)


def tables(counts, table, width):
    return local_call(
        tables_kernel, "tables", [like((8, width), jnp.int32)], 2, LEAD_FLOPS
    )(counts.reshape(1, -1), table)[0]


def transform_kernel(start, wants, integrals, own, outer, inner, *outs):
    mid = AO_DEV * BLOCK

    def blocks(prev, following):
        ids = start + lax.broadcasted_iota(jnp.int32, (BLOCK, own.shape[1]), 1)
        for p in range(integrals.shape[0]):
            both = []
            for offset in range(AO_DEV):
                low = mid - offset * BLOCK
                slab = integrals[p, offset * BLOCK : (offset + 1) * BLOCK, :]
                values = dot(slab[:, low : low + mid], own[...])
                values += dot(slab[:, :low], prev[offset * BLOCK :, :])
                values += dot(slab[:, low + mid :], following[: (offset + 1) * BLOCK, :])
                live = ids < wants[GROUPS + offset : GROUPS + offset + 1, :]
                both.append(jnp.where(live, values, 0.0))
            for s, out in enumerate(outs):
                out[p] = jnp.where(wants[s : s + 1, :] == 0, *both).astype(jnp.bfloat16)

    odd = lax.axis_index("ao") & 1
    pl.when(odd == 0)(lambda: blocks(inner, outer))
    pl.when(odd == 1)(lambda: blocks(outer, inner))


def shared_kernel(start, wants, integrals, own, outer, inner, swapped, *refs):
    *outs, whole = refs
    aux = lax.axis_index("aux")
    width = inner.shape[1]
    whole[:, pl.ds(pl.multiple_of(aux * width, width), width)] = inner[...]
    whole[:, pl.ds(pl.multiple_of((1 - aux) * width, width), width)] = swapped[...]
    transform_kernel(start, wants, integrals, own, outer, whole, *outs)


def shared_transform(start, wants, integrals, own, outer, inner, swapped):
    shape = (integrals.shape[0], BLOCK, own.shape[1])
    return local_call(
        functools.partial(shared_kernel, start),
        "transform",
        [like(shape, jnp.bfloat16)] * GROUPS,
        6,
        2 * AO_DEV * math.prod(shape) * integrals.shape[2],
        [pltpu.VMEM(own.shape, jnp.bfloat16)],
    )(wants, integrals, own, outer, inner, swapped)


def transform(start, wants, integrals, own, outer, inner):
    shape = (integrals.shape[0], BLOCK, own.shape[1])
    return local_call(
        functools.partial(transform_kernel, start),
        "transform",
        [like(shape, jnp.bfloat16)] * GROUPS,
        5,
        2 * AO_DEV * math.prod(shape) * integrals.shape[2],
    )(wants, integrals, own, outer, inner)


def form_pairs(pairs, blocks, grams):
    here = lax.axis_index("ao")
    slices = [[(ref, p) for ref in block for p in range(ref.shape[0])] for block in blocks]

    def product(left, right):
        total = None
        for (a, i), (b, j) in zip(slices[left], slices[right]):
            part = lax.dot_general(
                a[i], b[j], (((1,), (1,)), ((), ())), preferred_element_type=jnp.float32
            )
            total = part if total is None else total + part
        return total.reshape(grams.shape[1:])

    for bit in (0, 1):
        mine = [(k, a, b) for k, (a, b) in enumerate(pairs) if (a ^ b) >> 1 == bit]
        upper = (here >> bit) & 1

        @pl.when(upper == 0)
        def _(mine=mine):
            for k, a, b in mine:
                grams[k] = product(a, b)

        @pl.when(upper == 1)
        def _(mine=mine):
            for k, a, b in mine:
                grams[k] = product(b, a)


def early_kernel(live, table, *refs):
    used = 3 * CHUNKS
    own, middle, next_to = [refs[i : i + CHUNKS] for i in range(0, used, CHUNKS)]
    blocks = own, next_to, middle
    near, far, place, grams = refs[used:]
    here, aux, orb = (lax.axis_index(axis) for axis in ("ao", "aux", "orb"))
    slots, width = place.shape
    slot = lax.broadcasted_iota(jnp.int32, (slots, table.shape[1]), 0)
    column = lax.broadcasted_iota(jnp.int32, (slots, table.shape[1]), 1)
    shown = column == here * slots + slot
    sides = []
    for side in (0, 1):
        group = (table[side : side + 1, :] // AO_DEV).astype(jnp.float32)
        group = jnp.sum(jnp.where(shown, group, 0.0), axis=1, keepdims=True)
        sides.append(group.astype(jnp.int32) ^ here)
    low, high = jnp.minimum(*sides), jnp.maximum(*sides)
    index = jnp.where(high == 3, low + 3, jnp.where(high == 2, low + 1, 0))
    slot = lax.broadcasted_iota(jnp.int32, (slots, width), 0)
    count = scalar_at(live[...], here).astype(jnp.int32)
    place[...] = jnp.where(slot < count, index, len(ALL_PAIRS))
    form_pairs(EARLY_PAIRS, blocks, grams)
    for k in range(len(EARLY_PAIRS)):
        for core in (0, 1):
            near[core, k] = grams[k, 2 * aux + (orb ^ core)]
            far[core, k] = grams[k, 2 * (1 - aux) + (orb ^ core)].astype(jnp.bfloat16)


def late_kernel(*refs):
    used = GROUPS * CHUNKS
    own, middle, next_to, last = [refs[i : i + CHUNKS] for i in range(0, used, CHUNKS)]
    blocks = own, next_to, middle, last
    keep, give, grams = refs[used:]
    aux, orb = lax.axis_index("aux"), lax.axis_index("orb")
    form_pairs(LATE_PAIRS, blocks, grams)
    for k in range(len(LATE_PAIRS)):
        for chip in (0, 1):
            row = 2 * (aux ^ chip)
            keep[chip, k] = grams[k, row + orb]
            give[chip, k] = grams[k, row + 1 - orb]


def pair_flops(pairs, blocks):
    return 2 * len(pairs) * BLOCK * CHUNKS * blocks[0][0].size


def quarters(pairs):
    rows = BLOCK // 4
    return (2, len(pairs), rows, BLOCK), pltpu.VMEM((len(pairs), 4, rows, BLOCK), jnp.float32)


def early_pairs(live, table, blocks):
    shape, grams = quarters(EARLY_PAIRS)
    return local_call(
        early_kernel,
        "early_pairs",
        [
            like(shape, jnp.float32),
            like(shape, jnp.bfloat16),
            like((table.shape[1] // GROUPS, BLOCK), jnp.int32),
        ],
        2 + 3 * CHUNKS,
        pair_flops(EARLY_PAIRS, blocks),
        [grams],
    )(live.reshape(1, -1), table, *blocks[0], *blocks[2], *blocks[1])


def late_pairs(blocks):
    shape, grams = quarters(LATE_PAIRS)
    return local_call(
        late_kernel,
        "late_pairs",
        [like(shape, jnp.float32)] * 2,
        GROUPS * CHUNKS,
        pair_flops(LATE_PAIRS, blocks),
        [grams],
    )(*blocks[0], *blocks[2], *blocks[1], *blocks[3])


def spread_kernel(factor, place, near0, far0, got0, near1, got1, far1, out, sums, rows, sems):
    early = near0.shape[1]
    sums[:early] = (near0[0] + far0[0].astype(jnp.float32) + got0[...]) * factor
    sums[early:] = (near1[0] + got1[0] + far1[...].astype(jnp.float32)) * factor
    total, slots, width = out.shape
    masks = [place[...] == k for k in range(sums.shape[0])]

    def one(m, carry):
        row = jnp.zeros((slots, width), jnp.float32)
        for k, mask in enumerate(masks):
            values = jnp.broadcast_to(sums[k, pl.ds(m, 1), :], (slots, width))
            row = jnp.where(mask, values, row)
        rows[m] = row
        return carry

    step = total // SPREAD_STEPS
    copies = []
    for i in range(SPREAD_STEPS):
        lax.fori_loop(i * step, (i + 1) * step, one, 0, unroll=8)
        part = pl.ds(i * step, step)
        copies.append(pltpu.make_async_copy(rows.at[part], out.at[part], sems.at[i]))
        copies[-1].start()
    for copy in copies:
        copy.wait()


def spread(factor, place, *parts):
    rows = BLOCK // 4
    shape = (rows, place.shape[0], BLOCK)
    return local_call(
        functools.partial(spread_kernel, factor),
        "spread",
        [like(shape, jnp.float32)],
        1 + len(parts),
        6 * math.prod(shape),
        [
            pltpu.VMEM((len(ALL_PAIRS), rows, BLOCK), jnp.float32),
            pltpu.VMEM(shape, jnp.float32),
            pltpu.SemaphoreType.DMA((SPREAD_STEPS,)),
        ],
        IN_HBM,
    )(place, *parts)[0]


def six_pair_body(integrals, coeffs, pair_blocks, pair_count, orbital_count):
    width = coeffs.shape[1] // CHUNKS
    total_aux = integrals.shape[0] * lax.axis_size("aux")
    table = pair_blocks.T

    *parts, mine = cut(coeffs)
    inner = [lax.ppermute(part, "ao", INSIDE) for part in (parts[0], mine)]
    outer = [lax.ppermute(part, "ao", OUTSIDE) for part in parts]
    wants = tables(orbital_count, table, width)

    pieces = list(transform(0, wants, integrals, parts[0], outer[0], inner[0]))
    blocks = [[piece] for piece in pieces]
    inner[1], blocks[0][0] = lax.optimization_barrier((inner[1], blocks[0][0]))
    swapped = lax.ppermute(inner[1], "aux", SWAP)
    pieces = shared_transform(
        width, wants, integrals, parts[1], outer[1], inner[1], swapped
    )
    for block, piece in zip(blocks, pieces):
        block.append(piece)

    def fetch(s):
        swap = [(j, j ^ s) for j in range(GROUPS)]
        return [lax.ppermute(piece, "ao", swap) for piece in blocks[s]]

    middle = fetch(2)
    got = [blocks[0], fetch(1), middle]
    near0, across0, place = early_pairs(pair_count, table, got)
    far0 = lax.ppermute(across0, "aux", SWAP)
    got.append(fetch(3))
    near1, give1 = late_pairs(got)
    got1 = lax.ppermute(give1, "orb", SWAP)
    far1 = lax.ppermute((near1[1] + got1[1]).astype(jnp.bfloat16), "aux", SWAP)
    got0 = lax.ppermute(near0[1] + far0[1].astype(jnp.float32), "orb", SWAP)
    factor = 1.0 / math.sqrt(total_aux * ORBS)
    return spread(factor, place, near0, far0, got0, near1, got1, far1)


def solution(mesh):
    sizes = dict(mesh.shape)
    body = general_body
    if sizes["ao"] == 4 and sizes["aux"] == 2 and sizes["orb"] == 2:
        body = six_pair_body
    return jax.shard_map(
        body,
        mesh=mesh,
        in_specs=(
            P(("grp", "aux"), "ao", None),
            P(("grp", "ao"), "orb"),
            P("grp", None),
            P("grp"),
            P("grp"),
        ),
        out_specs=P(("aux", "orb"), ("grp", "ao"), None),
        check_vma=False,
    )
```

```python
import functools
import math

import jax
import jax.numpy as jnp
from jax import lax
from jax.experimental import pallas as pl
from jax.experimental.pallas import tpu as pltpu
from jax.sharding import PartitionSpec as P

BLOCK = 256
AO_DEV = 2
WIN = 5
ORBS = 1024
CHUNKS = 2
SPREAD_STEPS = 4
SPREAD_STEPS = 4
SPREAD_STEPS = 4
SPREAD_STEPS = 4
SPREAD_STEPS = 4
SPREAD_STEPS = 4
VMEM_LIMIT = 40 * 1024 * 1024
LEAD_FLOPS = 1 << 32
CUT_LIMIT = 53 * 1024 * 1024 + 256 * 1024


def with_halo(cells, sides, width):
    for axis, dim in sides:
        count = lax.axis_size(axis)
        ends = count - 1
        head = lax.slice_in_dim(cells, 0, width, axis=dim)
        tail = lax.slice_in_dim(cells, cells.shape[dim] - width, cells.shape[dim], axis=dim)
        cells = jnp.concatenate(
            [
                lax.ppermute(tail, axis, [(i, (i + 1) % count) for i in range(ends)]),
                cells,
                lax.ppermute(head, axis, [((i + 1) % count, i) for i in range(ends)]),
            ],
            axis=dim,
        )
    return cells


def general_body(integrals, coeffs, pair_blocks, pair_count, orbital_count):
    orb_local = coeffs.shape[1]
    aux_devices = lax.axis_size("aux")
    total_aux = integrals.shape[0] * aux_devices
    rim = WIN // 2 * BLOCK
    extended = with_halo(coeffs, (("ao", 0),), rim)
    ao_here = lax.axis_index("ao")
    orbital_ids = lax.axis_index("orb") * orb_local + jnp.arange(orb_local, dtype=jnp.int32)
    pieces = []
    for offset in range(AO_DEV):
        slab = integrals[:, offset * BLOCK : (offset + 1) * BLOCK, :]
        slot_range = extended[offset * BLOCK : offset * BLOCK + WIN * BLOCK]
        values = jnp.einsum("pml,li->pmi", slab, slot_range, preferred_element_type=jnp.float32)
        limit = orbital_count[ao_here * AO_DEV + offset]
        values = jnp.where((orbital_ids < limit)[None, None, :], values, 0.0)
        pieces.append(values.astype(jnp.bfloat16))
    transformed = jnp.stack(pieces)
    owners = lax.axis_size("ao")
    table = pair_blocks.reshape(owners, -1, 2)
    slots = table.shape[1]
    live = jnp.arange(slots, dtype=jnp.int32)[None, :] < pair_count[:, None]
    touched = live[:, :, None] & (table // AO_DEV == ao_here)
    wanted = jnp.max(jnp.where(touched, table % AO_DEV, 0), axis=(1, 2))
    outgoing = transformed[wanted]
    received = lax.all_to_all(outgoing, "ao", split_axis=0, concat_axis=0, tiled=True)
    owned = table[ao_here]
    factor = 1.0 / math.sqrt(total_aux * ORBS)
    weights = jnp.where(live[ao_here], factor, 0.0).astype(jnp.float32)
    left_source = owned[:, 0] // AO_DEV
    right_source = owned[:, 1] // AO_DEV
    right_factors = received[right_source]
    lefts = received[left_source]
    term = jnp.einsum("spmi,spni->msn", lefts, right_factors, preferred_element_type=jnp.float32)
    return lax.psum_scatter(
        term * weights[None, :, None], ("aux", "orb"), scatter_dimension=0, tiled=True
    )


EARLY_PAIRS = ((0, 1), (0, 2), (1, 2))
LATE_PAIRS = ((0, 3), (1, 3), (2, 3))
ALL_PAIRS = EARLY_PAIRS + LATE_PAIRS
GROUPS = 4
SWAP = [(0, 1), (1, 0)]
OUTSIDE = [(0, 1), (1, 0), (2, 3), (3, 2)]
INSIDE = [(1, 2), (2, 1)]

IN_HBM = pl.BlockSpec(memory_space=pltpu.HBM)
IN_VMEM = pl.BlockSpec(memory_space=pltpu.VMEM)


def like(shape, dtype):
    return jax.ShapeDtypeStruct(shape, dtype)


def local_call(kernel, name, out_shape, inputs, flops, scratch=(), out_spec=IN_VMEM):
    moved = sum(math.prod(o.shape) * o.dtype.itemsize for o in out_shape)
    return pl.pallas_call(
        kernel,
        out_shape=out_shape,
        in_specs=[IN_VMEM] * inputs,
        out_specs=[out_spec] * len(out_shape),
        scratch_shapes=list(scratch),
        compiler_params=pltpu.CompilerParams(vmem_limit_bytes=VMEM_LIMIT),
        cost_estimate=pl.CostEstimate(flops=flops, bytes_accessed=2 * moved, transcendentals=0),
        name=name,
    )


def dot(a, b):
    return jnp.dot(a, b, preferred_element_type=jnp.float32)


def cut_kernel(coeffs, direct, shared, mine, sems):
    width, half = direct.shape[1], mine.shape[1]
    start = pl.multiple_of(width + lax.axis_index("aux") * half, half)
    copies = [
        pltpu.make_async_copy(coeffs.at[:, columns], out, sems.at[i])
        for i, (columns, out) in enumerate(
            ((pl.ds(0, width), direct), (pl.ds(start, half), mine), (pl.ds(width, width), shared))
        )
    ]
    for copy in copies:
        copy.start()
    for copy in copies:
        copy.wait()


def cut(coeffs):
    rows, columns = coeffs.shape
    width = columns // CHUNKS
    return pl.pallas_call(
        cut_kernel,
        out_shape=[like((rows, n), coeffs.dtype) for n in (width, width, width // 2)],
        in_specs=[IN_HBM],
        out_specs=[IN_VMEM] * 3,
        scratch_shapes=[pltpu.SemaphoreType.DMA((3,))],
        compiler_params=pltpu.CompilerParams(vmem_limit_bytes=CUT_LIMIT),
        cost_estimate=pl.CostEstimate(flops=LEAD_FLOPS, bytes_accessed=0, transcendentals=0),
        name="cut",
    )(coeffs)


def scalar_at(values, index):
    ids = lax.broadcasted_iota(jnp.int32, values.shape, 1)
    return jnp.sum(jnp.where(ids == index, values, 0).astype(jnp.float32))


def tables_kernel(counts, table, wants):
    here, orb = lax.axis_index("ao"), lax.axis_index("orb")
    slots = table.shape[1] // GROUPS
    named = jnp.where(table[...] // AO_DEV == here, table[...] % AO_DEV, 0).astype(jnp.float32)
    owner = lax.broadcasted_iota(jnp.int32, table.shape, 1) // slots
    rows = [jnp.max(jnp.where(owner == here ^ s, named, 0.0)) for s in range(GROUPS)]
    for offset in range(AO_DEV):
        count = scalar_at(counts[...], here * AO_DEV + offset)
        rows.append(count - (orb * (ORBS // 2)).astype(jnp.float32))
    row = lax.broadcasted_iota(jnp.int32, wants.shape, 0)
    out = jnp.zeros(wants.shape, jnp.float32)
    for k, value in enumerate(rows):
        out = jnp.where(row == k, value, out)
    wants[...] = out.astype(jnp.int32)


def tables(counts, table, width):
    return local_call(
        tables_kernel, "tables", [like((8, width), jnp.int32)], 2, LEAD_FLOPS
    )(counts.reshape(1, -1), table)[0]


def transform_kernel(start, wants, integrals, own, outer, inner, *outs):
    mid = AO_DEV * BLOCK

    def blocks(prev, following):
        ids = start + lax.broadcasted_iota(jnp.int32, (BLOCK, own.shape[1]), 1)
        for p in range(integrals.shape[0]):
            both = []
            for offset in range(AO_DEV):
                low = mid - offset * BLOCK
                slab = integrals[p, offset * BLOCK : (offset + 1) * BLOCK, :]
                values = dot(slab[:, low : low + mid], own[...])
                values += dot(slab[:, :low], prev[offset * BLOCK :, :])
                values += dot(slab[:, low + mid :], following[: (offset + 1) * BLOCK, :])
                live = ids < wants[GROUPS + offset : GROUPS + offset + 1, :]
                both.append(jnp.where(live, values, 0.0))
            for s, out in enumerate(outs):
                out[p] = jnp.where(wants[s : s + 1, :] == 0, *both).astype(jnp.bfloat16)

    odd = lax.axis_index("ao") & 1
    pl.when(odd == 0)(lambda: blocks(inner, outer))
    pl.when(odd == 1)(lambda: blocks(outer, inner))


def shared_kernel(start, wants, integrals, own, outer, inner, swapped, *refs):
    *outs, whole = refs
    aux = lax.axis_index("aux")
    width = inner.shape[1]
    whole[:, pl.ds(pl.multiple_of(aux * width, width), width)] = inner[...]
    whole[:, pl.ds(pl.multiple_of((1 - aux) * width, width), width)] = swapped[...]
    transform_kernel(start, wants, integrals, own, outer, whole, *outs)


def shared_transform(start, wants, integrals, own, outer, inner, swapped):
    shape = (integrals.shape[0], BLOCK, own.shape[1])
    return local_call(
        functools.partial(shared_kernel, start),
        "transform",
        [like(shape, jnp.bfloat16)] * GROUPS,
        6,
        2 * AO_DEV * math.prod(shape) * integrals.shape[2],
        [pltpu.VMEM(own.shape, jnp.bfloat16)],
    )(wants, integrals, own, outer, inner, swapped)


def transform(start, wants, integrals, own, outer, inner):
    shape = (integrals.shape[0], BLOCK, own.shape[1])
    return local_call(
        functools.partial(transform_kernel, start),
        "transform",
        [like(shape, jnp.bfloat16)] * GROUPS,
        5,
        2 * AO_DEV * math.prod(shape) * integrals.shape[2],
    )(wants, integrals, own, outer, inner)


def form_pairs(pairs, blocks, grams):
    here = lax.axis_index("ao")
    slices = [[(ref, p) for ref in block for p in range(ref.shape[0])] for block in blocks]

    def product(left, right):
        total = None
        for (a, i), (b, j) in zip(slices[left], slices[right]):
            part = lax.dot_general(
                a[i], b[j], (((1,), (1,)), ((), ())), preferred_element_type=jnp.float32
            )
            total = part if total is None else total + part
        return total.reshape(grams.shape[1:])

    for bit in (0, 1):
        mine = [(k, a, b) for k, (a, b) in enumerate(pairs) if (a ^ b) >> 1 == bit]
        upper = (here >> bit) & 1

        @pl.when(upper == 0)
        def _(mine=mine):
            for k, a, b in mine:
                grams[k] = product(a, b)

        @pl.when(upper == 1)
        def _(mine=mine):
            for k, a, b in mine:
                grams[k] = product(b, a)


def early_kernel(live, table, *refs):
    used = 3 * CHUNKS
    own, middle, next_to = [refs[i : i + CHUNKS] for i in range(0, used, CHUNKS)]
    blocks = own, next_to, middle
    near, far, place, grams = refs[used:]
    here, aux, orb = (lax.axis_index(axis) for axis in ("ao", "aux", "orb"))
    slots, width = place.shape
    slot = lax.broadcasted_iota(jnp.int32, (slots, table.shape[1]), 0)
    column = lax.broadcasted_iota(jnp.int32, (slots, table.shape[1]), 1)
    shown = column == here * slots + slot
    sides = []
    for side in (0, 1):
        group = (table[side : side + 1, :] // AO_DEV).astype(jnp.float32)
        group = jnp.sum(jnp.where(shown, group, 0.0), axis=1, keepdims=True)
        sides.append(group.astype(jnp.int32) ^ here)
    low, high = jnp.minimum(*sides), jnp.maximum(*sides)
    index = jnp.where(high == 3, low + 3, jnp.where(high == 2, low + 1, 0))
    slot = lax.broadcasted_iota(jnp.int32, (slots, width), 0)
    count = scalar_at(live[...], here).astype(jnp.int32)
    place[...] = jnp.where(slot < count, index, len(ALL_PAIRS))
    form_pairs(EARLY_PAIRS, blocks, grams)
    for k in range(len(EARLY_PAIRS)):
        for core in (0, 1):
            near[core, k] = grams[k, 2 * aux + (orb ^ core)]
            far[core, k] = grams[k, 2 * (1 - aux) + (orb ^ core)].astype(jnp.bfloat16)


def late_kernel(*refs):
    used = GROUPS * CHUNKS
    own, middle, next_to, last = [refs[i : i + CHUNKS] for i in range(0, used, CHUNKS)]
    blocks = own, next_to, middle, last
    keep, give, grams = refs[used:]
    aux, orb = lax.axis_index("aux"), lax.axis_index("orb")
    form_pairs(LATE_PAIRS, blocks, grams)
    for k in range(len(LATE_PAIRS)):
        for chip in (0, 1):
            row = 2 * (aux ^ chip)
            keep[chip, k] = grams[k, row + orb]
            give[chip, k] = grams[k, row + 1 - orb]


def pair_flops(pairs, blocks):
    return 2 * len(pairs) * BLOCK * CHUNKS * blocks[0][0].size


def quarters(pairs):
    rows = BLOCK // 4
    return (2, len(pairs), rows, BLOCK), pltpu.VMEM((len(pairs), 4, rows, BLOCK), jnp.float32)


def early_pairs(live, table, blocks):
    shape, grams = quarters(EARLY_PAIRS)
    return local_call(
        early_kernel,
        "early_pairs",
        [
            like(shape, jnp.float32),
            like(shape, jnp.bfloat16),
            like((table.shape[1] // GROUPS, BLOCK), jnp.int32),
        ],
        2 + 3 * CHUNKS,
        pair_flops(EARLY_PAIRS, blocks),
        [grams],
    )(live.reshape(1, -1), table, *blocks[0], *blocks[2], *blocks[1])


def late_pairs(blocks):
    shape, grams = quarters(LATE_PAIRS)
    return local_call(
        late_kernel,
        "late_pairs",
        [like(shape, jnp.float32)] * 2,
        GROUPS * CHUNKS,
        pair_flops(LATE_PAIRS, blocks),
        [grams],
    )(*blocks[0], *blocks[2], *blocks[1], *blocks[3])


def spread_kernel(factor, place, near0, far0, got0, near1, got1, far1, out, sums, rows, sems):
    early = near0.shape[1]
    sums[:early] = (near0[0] + far0[0].astype(jnp.float32) + got0[...]) * factor
    sums[early:] = (near1[0] + got1[0] + far1[...].astype(jnp.float32)) * factor
    total, slots, width = out.shape
    masks = [place[...] == k for k in range(sums.shape[0])]

    def one(m, carry):
        row = jnp.zeros((slots, width), jnp.float32)
        for k, mask in enumerate(masks):
            values = jnp.broadcast_to(sums[k, pl.ds(m, 1), :], (slots, width))
            row = jnp.where(mask, values, row)
        rows[m] = row
        return carry

    step = total // SPREAD_STEPS
    copies = []
    for i in range(SPREAD_STEPS):
        lax.fori_loop(i * step, (i + 1) * step, one, 0, unroll=8)
        part = pl.ds(i * step, step)
        copies.append(pltpu.make_async_copy(rows.at[part], out.at[part], sems.at[i]))
        copies[-1].start()
    for copy in copies:
        copy.wait()


def spread(factor, place, *parts):
    rows = BLOCK // 4
    shape = (rows, place.shape[0], BLOCK)
    return local_call(
        functools.partial(spread_kernel, factor),
        "spread",
        [like(shape, jnp.float32)],
        1 + len(parts),
        6 * math.prod(shape),
        [
            pltpu.VMEM((len(ALL_PAIRS), rows, BLOCK), jnp.float32),
            pltpu.VMEM(shape, jnp.float32),
            pltpu.SemaphoreType.DMA((SPREAD_STEPS,)),
        ],
        IN_HBM,
    )(place, *parts)[0]


def six_pair_body(integrals, coeffs, pair_blocks, pair_count, orbital_count):
    width = coeffs.shape[1] // CHUNKS
    total_aux = integrals.shape[0] * lax.axis_size("aux")
    table = pair_blocks.T

    *parts, mine = cut(coeffs)
    inner = [lax.ppermute(part, "ao", INSIDE) for part in (parts[0], mine)]
    outer = [lax.ppermute(part, "ao", OUTSIDE) for part in parts]
    wants = tables(orbital_count, table, width)

    pieces = list(transform(0, wants, integrals, parts[0], outer[0], inner[0]))
    blocks = [[piece] for piece in pieces]
    inner[1], blocks[0][0] = lax.optimization_barrier((inner[1], blocks[0][0]))
    swapped = lax.ppermute(inner[1], "aux", SWAP)
    pieces = shared_transform(
        width, wants, integrals, parts[1], outer[1], inner[1], swapped
    )
    for block, piece in zip(blocks, pieces):
        block.append(piece)

    def fetch(s):
        swap = [(j, j ^ s) for j in range(GROUPS)]
        return [lax.ppermute(piece, "ao", swap) for piece in blocks[s]]

    middle = fetch(2)
    got = [blocks[0], fetch(1), middle]
    near0, across0, place = early_pairs(pair_count, table, got)
    far0 = lax.ppermute(across0, "aux", SWAP)
    got.append(fetch(3))
    near1, give1 = late_pairs(got)
    got1 = lax.ppermute(give1, "orb", SWAP)
    far1 = lax.ppermute((near1[1] + got1[1]).astype(jnp.bfloat16), "aux", SWAP)
    got0 = lax.ppermute(near0[1] + far0[1].astype(jnp.float32), "orb", SWAP)
    factor = 1.0 / math.sqrt(total_aux * ORBS)
    return spread(factor, place, near0, far0, got0, near1, got1, far1)


def solution(mesh):
    sizes = dict(mesh.shape)
    body = general_body
    if sizes["ao"] == 4 and sizes["aux"] == 2 and sizes["orb"] == 2:
        body = six_pair_body
    return jax.shard_map(
        body,
        mesh=mesh,
        in_specs=(
            P(("grp", "aux"), "ao", None),
            P(("grp", "ao"), "orb"),
            P("grp", None),
            P("grp"),
            P("grp"),
        ),
        out_specs=P(("aux", "orb"), ("grp", "ao"), None),
        check_vma=False,
    )
```

```python
import functools
import math

import jax
import jax.numpy as jnp
from jax import lax
from jax.experimental import pallas as pl
from jax.experimental.pallas import tpu as pltpu
from jax.sharding import PartitionSpec as P

BLOCK = 256
AO_DEV = 2
WIN = 5
ORBS = 1024
CHUNKS = 2
SPREAD_STEPS = 4
SPREAD_STEPS = 4
SPREAD_STEPS = 4
SPREAD_STEPS = 4
SPREAD_STEPS = 4
SPREAD_STEPS = 4
VMEM_LIMIT = 40 * 1024 * 1024
LEAD_FLOPS = 1 << 32
CUT_LIMIT = 53 * 1024 * 1024 + 256 * 1024


def with_halo(cells, sides, width):
    for axis, dim in sides:
        count = lax.axis_size(axis)
        ends = count - 1
        head = lax.slice_in_dim(cells, 0, width, axis=dim)
        tail = lax.slice_in_dim(cells, cells.shape[dim] - width, cells.shape[dim], axis=dim)
        cells = jnp.concatenate(
            [
                lax.ppermute(tail, axis, [(i, (i + 1) % count) for i in range(ends)]),
                cells,
                lax.ppermute(head, axis, [((i + 1) % count, i) for i in range(ends)]),
            ],
            axis=dim,
        )
    return cells


def general_body(integrals, coeffs, pair_blocks, pair_count, orbital_count):
    orb_local = coeffs.shape[1]
    aux_devices = lax.axis_size("aux")
    total_aux = integrals.shape[0] * aux_devices
    rim = WIN // 2 * BLOCK
    extended = with_halo(coeffs, (("ao", 0),), rim)
    ao_here = lax.axis_index("ao")
    orbital_ids = lax.axis_index("orb") * orb_local + jnp.arange(orb_local, dtype=jnp.int32)
    pieces = []
    for offset in range(AO_DEV):
        slab = integrals[:, offset * BLOCK : (offset + 1) * BLOCK, :]
        slot_range = extended[offset * BLOCK : offset * BLOCK + WIN * BLOCK]
        values = jnp.einsum("pml,li->pmi", slab, slot_range, preferred_element_type=jnp.float32)
        limit = orbital_count[ao_here * AO_DEV + offset]
        values = jnp.where((orbital_ids < limit)[None, None, :], values, 0.0)
        pieces.append(values.astype(jnp.bfloat16))
    transformed = jnp.stack(pieces)
    owners = lax.axis_size("ao")
    table = pair_blocks.reshape(owners, -1, 2)
    slots = table.shape[1]
    live = jnp.arange(slots, dtype=jnp.int32)[None, :] < pair_count[:, None]
    touched = live[:, :, None] & (table // AO_DEV == ao_here)
    wanted = jnp.max(jnp.where(touched, table % AO_DEV, 0), axis=(1, 2))
    outgoing = transformed[wanted]
    received = lax.all_to_all(outgoing, "ao", split_axis=0, concat_axis=0, tiled=True)
    owned = table[ao_here]
    factor = 1.0 / math.sqrt(total_aux * ORBS)
    weights = jnp.where(live[ao_here], factor, 0.0).astype(jnp.float32)
    left_source = owned[:, 0] // AO_DEV
    right_source = owned[:, 1] // AO_DEV
    right_factors = received[right_source]
    lefts = received[left_source]
    term = jnp.einsum("spmi,spni->msn", lefts, right_factors, preferred_element_type=jnp.float32)
    return lax.psum_scatter(
        term * weights[None, :, None], ("aux", "orb"), scatter_dimension=0, tiled=True
    )


EARLY_PAIRS = ((0, 1), (0, 2), (1, 2))
LATE_PAIRS = ((0, 3), (1, 3), (2, 3))
ALL_PAIRS = EARLY_PAIRS + LATE_PAIRS
GROUPS = 4
SWAP = [(0, 1), (1, 0)]
OUTSIDE = [(0, 1), (1, 0), (2, 3), (3, 2)]
INSIDE = [(1, 2), (2, 1)]

IN_HBM = pl.BlockSpec(memory_space=pltpu.HBM)
IN_VMEM = pl.BlockSpec(memory_space=pltpu.VMEM)


def like(shape, dtype):
    return jax.ShapeDtypeStruct(shape, dtype)


def local_call(kernel, name, out_shape, inputs, flops, scratch=(), out_spec=IN_VMEM):
    moved = sum(math.prod(o.shape) * o.dtype.itemsize for o in out_shape)
    return pl.pallas_call(
        kernel,
        out_shape=out_shape,
        in_specs=[IN_VMEM] * inputs,
        out_specs=[out_spec] * len(out_shape),
        scratch_shapes=list(scratch),
        compiler_params=pltpu.CompilerParams(vmem_limit_bytes=VMEM_LIMIT),
        cost_estimate=pl.CostEstimate(flops=flops, bytes_accessed=2 * moved, transcendentals=0),
        name=name,
    )


def dot(a, b):
    return jnp.dot(a, b, preferred_element_type=jnp.float32)


def cut_kernel(coeffs, direct, shared, mine, sems):
    width, half = direct.shape[1], mine.shape[1]
    start = pl.multiple_of(width + lax.axis_index("aux") * half, half)
    copies = [
        pltpu.make_async_copy(coeffs.at[:, columns], out, sems.at[i])
        for i, (columns, out) in enumerate(
            ((pl.ds(0, width), direct), (pl.ds(start, half), mine), (pl.ds(width, width), shared))
        )
    ]
    for copy in copies:
        copy.start()
    for copy in copies:
        copy.wait()


def cut(coeffs):
    rows, columns = coeffs.shape
    width = columns // CHUNKS
    return pl.pallas_call(
        cut_kernel,
        out_shape=[like((rows, n), coeffs.dtype) for n in (width, width, width // 2)],
        in_specs=[IN_HBM],
        out_specs=[IN_VMEM] * 3,
        scratch_shapes=[pltpu.SemaphoreType.DMA((3,))],
        compiler_params=pltpu.CompilerParams(vmem_limit_bytes=CUT_LIMIT),
        cost_estimate=pl.CostEstimate(flops=LEAD_FLOPS, bytes_accessed=0, transcendentals=0),
        name="cut",
    )(coeffs)


def scalar_at(values, index):
    ids = lax.broadcasted_iota(jnp.int32, values.shape, 1)
    return jnp.sum(jnp.where(ids == index, values, 0).astype(jnp.float32))


def tables_kernel(counts, table, wants):
    here, orb = lax.axis_index("ao"), lax.axis_index("orb")
    slots = table.shape[1] // GROUPS
    named = jnp.where(table[...] // AO_DEV == here, table[...] % AO_DEV, 0).astype(jnp.float32)
    owner = lax.broadcasted_iota(jnp.int32, table.shape, 1) // slots
    rows = [jnp.max(jnp.where(owner == here ^ s, named, 0.0)) for s in range(GROUPS)]
    for offset in range(AO_DEV):
        count = scalar_at(counts[...], here * AO_DEV + offset)
        rows.append(count - (orb * (ORBS // 2)).astype(jnp.float32))
    row = lax.broadcasted_iota(jnp.int32, wants.shape, 0)
    out = jnp.zeros(wants.shape, jnp.float32)
    for k, value in enumerate(rows):
        out = jnp.where(row == k, value, out)
    wants[...] = out.astype(jnp.int32)


def tables(counts, table, width):
    return local_call(
        tables_kernel, "tables", [like((8, width), jnp.int32)], 2, LEAD_FLOPS
    )(counts.reshape(1, -1), table)[0]


def transform_kernel(start, wants, integrals, own, outer, inner, *outs):
    mid = AO_DEV * BLOCK

    def blocks(prev, following):
        ids = start + lax.broadcasted_iota(jnp.int32, (BLOCK, own.shape[1]), 1)
        for p in range(integrals.shape[0]):
            both = []
            for offset in range(AO_DEV):
                low = mid - offset * BLOCK
                slab = integrals[p, offset * BLOCK : (offset + 1) * BLOCK, :]
                values = dot(slab[:, low : low + mid], own[...])
                values += dot(slab[:, :low], prev[offset * BLOCK :, :])
                values += dot(slab[:, low + mid :], following[: (offset + 1) * BLOCK, :])
                live = ids < wants[GROUPS + offset : GROUPS + offset + 1, :]
                both.append(jnp.where(live, values, 0.0))
            for s, out in enumerate(outs):
                out[p] = jnp.where(wants[s : s + 1, :] == 0, *both).astype(jnp.bfloat16)

    odd = lax.axis_index("ao") & 1
    pl.when(odd == 0)(lambda: blocks(inner, outer))
    pl.when(odd == 1)(lambda: blocks(outer, inner))


def shared_kernel(start, wants, integrals, own, outer, inner, swapped, *refs):
    *outs, whole = refs
    aux = lax.axis_index("aux")
    width = inner.shape[1]
    whole[:, pl.ds(pl.multiple_of(aux * width, width), width)] = inner[...]
    whole[:, pl.ds(pl.multiple_of((1 - aux) * width, width), width)] = swapped[...]
    transform_kernel(start, wants, integrals, own, outer, whole, *outs)


def shared_transform(start, wants, integrals, own, outer, inner, swapped):
    shape = (integrals.shape[0], BLOCK, own.shape[1])
    return local_call(
        functools.partial(shared_kernel, start),
        "transform",
        [like(shape, jnp.bfloat16)] * GROUPS,
        6,
        2 * AO_DEV * math.prod(shape) * integrals.shape[2],
        [pltpu.VMEM(own.shape, jnp.bfloat16)],
    )(wants, integrals, own, outer, inner, swapped)


def transform(start, wants, integrals, own, outer, inner):
    shape = (integrals.shape[0], BLOCK, own.shape[1])
    return local_call(
        functools.partial(transform_kernel, start),
        "transform",
        [like(shape, jnp.bfloat16)] * GROUPS,
        5,
        2 * AO_DEV * math.prod(shape) * integrals.shape[2],
    )(wants, integrals, own, outer, inner)


def form_pairs(pairs, blocks, grams, before=None):
    here = lax.axis_index("ao")
    slices = [[(ref, p) for ref in block for p in range(ref.shape[0])] for block in blocks]

    def product(left, right):
        total = None
        for (a, i), (b, j) in zip(slices[left], slices[right]):
            part = lax.dot_general(
                a[i], b[j], (((1,), (1,)), ((), ())), preferred_element_type=jnp.float32
            )
            total = part if total is None else total + part
        return total.reshape(grams.shape[1:])

    def formed(k, left, right):
        gram = product(left, right)
        return gram if before is None else gram + before[k]

    for bit in (0, 1):
        mine = [(k, a, b) for k, (a, b) in enumerate(pairs) if (a ^ b) >> 1 == bit]
        upper = (here >> bit) & 1

        @pl.when(upper == 0)
        def _(mine=mine):
            for k, a, b in mine:
                grams[k] = formed(k, a, b)

        @pl.when(upper == 1)
        def _(mine=mine):
            for k, a, b in mine:
                grams[k] = formed(k, b, a)


def early_kernel(live, table, *refs):
    used = 3 * CHUNKS
    own, middle, next_to = [refs[i : i + CHUNKS] for i in range(0, used, CHUNKS)]
    blocks = own, next_to, middle
    near, far, place, grams = refs[used:]
    here, aux, orb = (lax.axis_index(axis) for axis in ("ao", "aux", "orb"))
    slots, width = place.shape
    slot = lax.broadcasted_iota(jnp.int32, (slots, table.shape[1]), 0)
    column = lax.broadcasted_iota(jnp.int32, (slots, table.shape[1]), 1)
    shown = column == here * slots + slot
    sides = []
    for side in (0, 1):
        group = (table[side : side + 1, :] // AO_DEV).astype(jnp.float32)
        group = jnp.sum(jnp.where(shown, group, 0.0), axis=1, keepdims=True)
        sides.append(group.astype(jnp.int32) ^ here)
    low, high = jnp.minimum(*sides), jnp.maximum(*sides)
    index = jnp.where(high == 3, low + 3, jnp.where(high == 2, low + 1, 0))
    slot = lax.broadcasted_iota(jnp.int32, (slots, width), 0)
    count = scalar_at(live[...], here).astype(jnp.int32)
    place[...] = jnp.where(slot < count, index, len(ALL_PAIRS))
    form_pairs(EARLY_PAIRS, blocks, grams)
    for k in range(len(EARLY_PAIRS)):
        for core in (0, 1):
            near[core, k] = grams[k, 2 * aux + (orb ^ core)]
            far[core, k] = grams[k, 2 * (1 - aux) + (orb ^ core)].astype(jnp.bfloat16)


def begin_kernel(own, middle, next_to, last, grams):
    form_pairs(LATE_PAIRS, ([own], [next_to], [middle], [last]), grams)


def late_kernel(own, middle, next_to, last, before, *refs):
    keep, give, grams = refs
    blocks = [own], [next_to], [middle], [last]
    aux, orb = lax.axis_index("aux"), lax.axis_index("orb")
    form_pairs(LATE_PAIRS, blocks, grams, before)
    for k in range(len(LATE_PAIRS)):
        for chip in (0, 1):
            row = 2 * (aux ^ chip)
            keep[chip, k] = grams[k, row + orb]
            give[chip, k] = grams[k, row + 1 - orb]


def pair_flops(pairs, blocks):
    return 2 * len(pairs) * BLOCK * CHUNKS * blocks[0][0].size


def quarters(pairs):
    rows = BLOCK // 4
    return (2, len(pairs), rows, BLOCK), pltpu.VMEM((len(pairs), 4, rows, BLOCK), jnp.float32)


def early_pairs(live, table, blocks):
    shape, grams = quarters(EARLY_PAIRS)
    return local_call(
        early_kernel,
        "early_pairs",
        [
            like(shape, jnp.float32),
            like(shape, jnp.bfloat16),
            like((table.shape[1] // GROUPS, BLOCK), jnp.int32),
        ],
        2 + 3 * CHUNKS,
        pair_flops(EARLY_PAIRS, blocks),
        [grams],
    )(live.reshape(1, -1), table, *blocks[0], *blocks[2], *blocks[1])


def late_pairs(blocks):
    shape, grams = quarters(LATE_PAIRS)
    own, next_to, middle, last = blocks
    begun = local_call(
        begin_kernel,
        "begin_pairs",
        [like(grams.shape, jnp.float32)],
        GROUPS,
        pair_flops(LATE_PAIRS, blocks) // CHUNKS,
    )(own[0], middle[0], next_to[0], last[0])
    return local_call(
        late_kernel,
        "late_pairs",
        [like(shape, jnp.float32)] * 2,
        GROUPS + 1,
        pair_flops(LATE_PAIRS, blocks) // CHUNKS,
        [grams],
    )(own[1], middle[1], next_to[1], last[1], *begun)


def spread_kernel(factor, place, near0, far0, got0, near1, got1, far1, out, sums, rows, sems):
    early = near0.shape[1]
    sums[:early] = (near0[0] + far0[0].astype(jnp.float32) + got0[...]) * factor
    sums[early:] = (near1[0] + got1[0] + far1[...].astype(jnp.float32)) * factor
    total, slots, width = out.shape
    masks = [place[...] == k for k in range(sums.shape[0])]

    def one(m, carry):
        row = jnp.zeros((slots, width), jnp.float32)
        for k, mask in enumerate(masks):
            values = jnp.broadcast_to(sums[k, pl.ds(m, 1), :], (slots, width))
            row = jnp.where(mask, values, row)
        rows[m] = row
        return carry

    step = total // SPREAD_STEPS
    copies = []
    for i in range(SPREAD_STEPS):
        lax.fori_loop(i * step, (i + 1) * step, one, 0, unroll=8)
        part = pl.ds(i * step, step)
        copies.append(pltpu.make_async_copy(rows.at[part], out.at[part], sems.at[i]))
        copies[-1].start()
    for copy in copies:
        copy.wait()


def spread(factor, place, *parts):
    rows = BLOCK // 4
    shape = (rows, place.shape[0], BLOCK)
    return local_call(
        functools.partial(spread_kernel, factor),
        "spread",
        [like(shape, jnp.float32)],
        1 + len(parts),
        6 * math.prod(shape),
        [
            pltpu.VMEM((len(ALL_PAIRS), rows, BLOCK), jnp.float32),
            pltpu.VMEM(shape, jnp.float32),
            pltpu.SemaphoreType.DMA((SPREAD_STEPS,)),
        ],
        IN_HBM,
    )(place, *parts)[0]


def six_pair_body(integrals, coeffs, pair_blocks, pair_count, orbital_count):
    width = coeffs.shape[1] // CHUNKS
    total_aux = integrals.shape[0] * lax.axis_size("aux")
    table = pair_blocks.T

    *parts, mine = cut(coeffs)
    inner = [lax.ppermute(part, "ao", INSIDE) for part in (parts[0], mine)]
    outer = [lax.ppermute(part, "ao", OUTSIDE) for part in parts]
    wants = tables(orbital_count, table, width)

    pieces = list(transform(0, wants, integrals, parts[0], outer[0], inner[0]))
    blocks = [[piece] for piece in pieces]
    inner[1], blocks[0][0] = lax.optimization_barrier((inner[1], blocks[0][0]))
    swapped = lax.ppermute(inner[1], "aux", SWAP)
    pieces = shared_transform(
        width, wants, integrals, parts[1], outer[1], inner[1], swapped
    )
    for block, piece in zip(blocks, pieces):
        block.append(piece)

    def fetch(s):
        swap = [(j, j ^ s) for j in range(GROUPS)]
        return [lax.ppermute(piece, "ao", swap) for piece in blocks[s]]

    middle = fetch(2)
    got = [blocks[0], fetch(1), middle]
    near0, across0, place = early_pairs(pair_count, table, got)
    far0 = lax.ppermute(across0, "aux", SWAP)
    got.append(fetch(3))
    near1, give1 = late_pairs(got)
    got1 = lax.ppermute(give1, "orb", SWAP)
    far1 = lax.ppermute((near1[1] + got1[1]).astype(jnp.bfloat16), "aux", SWAP)
    got0 = lax.ppermute(near0[1] + far0[1].astype(jnp.float32), "orb", SWAP)
    factor = 1.0 / math.sqrt(total_aux * ORBS)
    return spread(factor, place, near0, far0, got0, near1, got1, far1)


def solution(mesh):
    sizes = dict(mesh.shape)
    body = general_body
    if sizes["ao"] == 4 and sizes["aux"] == 2 and sizes["orb"] == 2:
        body = six_pair_body
    return jax.shard_map(
        body,
        mesh=mesh,
        in_specs=(
            P(("grp", "aux"), "ao", None),
            P(("grp", "ao"), "orb"),
            P("grp", None),
            P("grp"),
            P("grp"),
        ),
        out_specs=P(("aux", "orb"), ("grp", "ao"), None),
        check_vma=False,
    )
```

```python
import functools
import math

import jax
import jax.numpy as jnp
from jax import lax
from jax.experimental import pallas as pl
from jax.experimental.pallas import tpu as pltpu
from jax.sharding import PartitionSpec as P

BLOCK = 256
AO_DEV = 2
WIN = 5
ORBS = 1024
CHUNKS = 2
SPREAD_STEPS = 4
SPREAD_STEPS = 4
SPREAD_STEPS = 4
SPREAD_STEPS = 4
SPREAD_STEPS = 4
SPREAD_STEPS = 4
VMEM_LIMIT = 40 * 1024 * 1024
LEAD_FLOPS = 1 << 32


def with_halo(cells, sides, width):
    for axis, dim in sides:
        count = lax.axis_size(axis)
        ends = count - 1
        head = lax.slice_in_dim(cells, 0, width, axis=dim)
        tail = lax.slice_in_dim(cells, cells.shape[dim] - width, cells.shape[dim], axis=dim)
        cells = jnp.concatenate(
            [
                lax.ppermute(tail, axis, [(i, (i + 1) % count) for i in range(ends)]),
                cells,
                lax.ppermute(head, axis, [((i + 1) % count, i) for i in range(ends)]),
            ],
            axis=dim,
        )
    return cells


def general_body(integrals, coeffs, pair_blocks, pair_count, orbital_count):
    orb_local = coeffs.shape[1]
    aux_devices = lax.axis_size("aux")
    total_aux = integrals.shape[0] * aux_devices
    rim = WIN // 2 * BLOCK
    extended = with_halo(coeffs, (("ao", 0),), rim)
    ao_here = lax.axis_index("ao")
    orbital_ids = lax.axis_index("orb") * orb_local + jnp.arange(orb_local, dtype=jnp.int32)
    pieces = []
    for offset in range(AO_DEV):
        slab = integrals[:, offset * BLOCK : (offset + 1) * BLOCK, :]
        slot_range = extended[offset * BLOCK : offset * BLOCK + WIN * BLOCK]
        values = jnp.einsum("pml,li->pmi", slab, slot_range, preferred_element_type=jnp.float32)
        limit = orbital_count[ao_here * AO_DEV + offset]
        values = jnp.where((orbital_ids < limit)[None, None, :], values, 0.0)
        pieces.append(values.astype(jnp.bfloat16))
    transformed = jnp.stack(pieces)
    owners = lax.axis_size("ao")
    table = pair_blocks.reshape(owners, -1, 2)
    slots = table.shape[1]
    live = jnp.arange(slots, dtype=jnp.int32)[None, :] < pair_count[:, None]
    touched = live[:, :, None] & (table // AO_DEV == ao_here)
    wanted = jnp.max(jnp.where(touched, table % AO_DEV, 0), axis=(1, 2))
    outgoing = transformed[wanted]
    received = lax.all_to_all(outgoing, "ao", split_axis=0, concat_axis=0, tiled=True)
    owned = table[ao_here]
    factor = 1.0 / math.sqrt(total_aux * ORBS)
    weights = jnp.where(live[ao_here], factor, 0.0).astype(jnp.float32)
    left_source = owned[:, 0] // AO_DEV
    right_source = owned[:, 1] // AO_DEV
    right_factors = received[right_source]
    lefts = received[left_source]
    term = jnp.einsum("spmi,spni->msn", lefts, right_factors, preferred_element_type=jnp.float32)
    return lax.psum_scatter(
        term * weights[None, :, None], ("aux", "orb"), scatter_dimension=0, tiled=True
    )


EARLY_PAIRS = ((0, 1), (0, 2), (1, 2))
LATE_PAIRS = ((0, 3), (1, 3), (2, 3))
LATE_GROUPS = 2, 1
ALL_PAIRS = EARLY_PAIRS + LATE_PAIRS
GROUPS = 4
SWAP = [(0, 1), (1, 0)]
OUTSIDE = [(0, 1), (1, 0), (2, 3), (3, 2)]
INSIDE = [(1, 2), (2, 1)]

IN_HBM = pl.BlockSpec(memory_space=pltpu.HBM)
IN_VMEM = pl.BlockSpec(memory_space=pltpu.VMEM)


def like(shape, dtype):
    return jax.ShapeDtypeStruct(shape, dtype)


def local_call(kernel, name, out_shape, inputs, flops, scratch=(), out_spec=IN_VMEM):
    moved = sum(math.prod(o.shape) * o.dtype.itemsize for o in out_shape)
    return pl.pallas_call(
        kernel,
        out_shape=out_shape,
        in_specs=[IN_VMEM] * inputs,
        out_specs=[out_spec] * len(out_shape),
        scratch_shapes=list(scratch),
        compiler_params=pltpu.CompilerParams(vmem_limit_bytes=VMEM_LIMIT),
        cost_estimate=pl.CostEstimate(flops=flops, bytes_accessed=2 * moved, transcendentals=0),
        name=name,
    )


def dot(a, b):
    return jnp.dot(a, b, preferred_element_type=jnp.float32)


def lead_kernel(out):
    out[...] = jnp.zeros_like(out)


def lead():
    return local_call(lead_kernel, "lead", [like((8, 128), jnp.int32)], 0, LEAD_FLOPS)()[0]


def scalar_at(values, index):
    ids = lax.broadcasted_iota(jnp.int32, values.shape, 1)
    return jnp.sum(jnp.where(ids == index, values, 0).astype(jnp.float32))


def tables_kernel(first, counts, table, wants):
    here, orb = lax.axis_index("ao"), lax.axis_index("orb")
    slots = table.shape[1] // GROUPS
    named = jnp.where(table[...] // AO_DEV == here, table[...] % AO_DEV, 0).astype(jnp.float32)
    owner = lax.broadcasted_iota(jnp.int32, table.shape, 1) // slots
    rows = [jnp.max(jnp.where(owner == here ^ s, named, 0.0)) for s in range(GROUPS)]
    for offset in range(AO_DEV):
        count = scalar_at(counts[...], here * AO_DEV + offset)
        rows.append(count - (orb * (ORBS // 2)).astype(jnp.float32))
    row = lax.broadcasted_iota(jnp.int32, wants.shape, 0)
    out = first[0, 0:1].astype(jnp.float32).reshape(1, 1) + jnp.zeros(wants.shape, jnp.float32)
    for k, value in enumerate(rows):
        out = jnp.where(row == k, value, out)
    wants[...] = out.astype(jnp.int32)


def tables(first, counts, table, width):
    return local_call(
        tables_kernel, "tables", [like((8, width), jnp.int32)], 3, table.size
    )(first, counts.reshape(1, -1), table)[0]


def transform_kernel(start, wants, integrals, own, outer, inner, *outs):
    mid = AO_DEV * BLOCK

    def blocks(prev, following):
        ids = start + lax.broadcasted_iota(jnp.int32, (BLOCK, own.shape[1]), 1)
        for p in range(integrals.shape[0]):
            both = []
            for offset in range(AO_DEV):
                low = mid - offset * BLOCK
                slab = integrals[p, offset * BLOCK : (offset + 1) * BLOCK, :]
                values = dot(slab[:, low : low + mid], own[...])
                values += dot(slab[:, :low], prev[offset * BLOCK :, :])
                values += dot(slab[:, low + mid :], following[: (offset + 1) * BLOCK, :])
                live = ids < wants[GROUPS + offset : GROUPS + offset + 1, :]
                both.append(jnp.where(live, values, 0.0))
            for s, out in enumerate(outs):
                out[p] = jnp.where(wants[s : s + 1, :] == 0, *both).astype(jnp.bfloat16)

    odd = lax.axis_index("ao") & 1
    pl.when(odd == 0)(lambda: blocks(inner, outer))
    pl.when(odd == 1)(lambda: blocks(outer, inner))


def shared_kernel(start, wants, integrals, own, outer, inner, swapped, *refs):
    *outs, whole = refs
    aux = lax.axis_index("aux")
    width = inner.shape[1]
    whole[:, pl.ds(pl.multiple_of(aux * width, width), width)] = inner[...]
    whole[:, pl.ds(pl.multiple_of((1 - aux) * width, width), width)] = swapped[...]
    transform_kernel(start, wants, integrals, own, outer, whole, *outs)


def shared_transform(start, wants, integrals, own, outer, inner, swapped):
    shape = (integrals.shape[0], BLOCK, own.shape[1])
    return local_call(
        functools.partial(shared_kernel, start),
        "transform",
        [like(shape, jnp.bfloat16)] * GROUPS,
        6,
        2 * AO_DEV * math.prod(shape) * integrals.shape[2],
        [pltpu.VMEM(own.shape, jnp.bfloat16)],
    )(wants, integrals, own, outer, inner, swapped)


def transform(start, wants, integrals, own, outer, inner):
    shape = (integrals.shape[0], BLOCK, own.shape[1])
    return local_call(
        functools.partial(transform_kernel, start),
        "transform",
        [like(shape, jnp.bfloat16)] * GROUPS,
        5,
        2 * AO_DEV * math.prod(shape) * integrals.shape[2],
    )(wants, integrals, own, outer, inner)


def form_pairs(pairs, blocks, grams, before=None):
    here = lax.axis_index("ao")
    slices = [[(ref, p) for ref in block for p in range(ref.shape[0])] for block in blocks]

    def product(left, right):
        total = None
        for (a, i), (b, j) in zip(slices[left], slices[right]):
            part = lax.dot_general(
                a[i], b[j], (((1,), (1,)), ((), ())), preferred_element_type=jnp.float32
            )
            total = part if total is None else total + part
        return total.reshape(grams.shape[1:])

    def formed(k, left, right):
        gram = product(left, right)
        return gram if before is None else gram + before[k]

    for bit in (0, 1):
        mine = [(k, a, b) for k, (a, b) in enumerate(pairs) if (a ^ b) >> 1 == bit]
        upper = (here >> bit) & 1

        @pl.when(upper == 0)
        def _(mine=mine):
            for k, a, b in mine:
                grams[k] = formed(k, a, b)

        @pl.when(upper == 1)
        def _(mine=mine):
            for k, a, b in mine:
                grams[k] = formed(k, b, a)


def early_kernel(live, table, *refs):
    used = 3 * CHUNKS
    own, middle, next_to = [refs[i : i + CHUNKS] for i in range(0, used, CHUNKS)]
    blocks = own, next_to, middle
    near, far, place, grams = refs[used:]
    here, aux, orb = (lax.axis_index(axis) for axis in ("ao", "aux", "orb"))
    slots, width = place.shape
    slot = lax.broadcasted_iota(jnp.int32, (slots, table.shape[1]), 0)
    column = lax.broadcasted_iota(jnp.int32, (slots, table.shape[1]), 1)
    shown = column == here * slots + slot
    sides = []
    for side in (0, 1):
        group = (table[side : side + 1, :] // AO_DEV).astype(jnp.float32)
        group = jnp.sum(jnp.where(shown, group, 0.0), axis=1, keepdims=True)
        sides.append(group.astype(jnp.int32) ^ here)
    low, high = jnp.minimum(*sides), jnp.maximum(*sides)
    index = jnp.where(high == 3, low + 3, jnp.where(high == 2, low + 1, 0))
    slot = lax.broadcasted_iota(jnp.int32, (slots, width), 0)
    count = scalar_at(live[...], here).astype(jnp.int32)
    place[...] = jnp.where(slot < count, index, len(ALL_PAIRS))
    form_pairs(EARLY_PAIRS, blocks, grams)
    for k in range(len(EARLY_PAIRS)):
        for core in (0, 1):
            near[core, k] = grams[k, 2 * aux + (orb ^ core)]
            far[core, k] = grams[k, 2 * (1 - aux) + (orb ^ core)].astype(jnp.bfloat16)


def begin_kernel(own, middle, next_to, last, grams):
    form_pairs(LATE_PAIRS, ([own], [next_to], [middle], [last]), grams)


def late_kernel(own, middle, next_to, last, before, *refs):
    *shares, grams = refs
    blocks = [own], [next_to], [middle], [last]
    aux, orb = lax.axis_index("aux"), lax.axis_index("orb")
    form_pairs(LATE_PAIRS, blocks, grams, before)
    done = 0
    for keep, give in zip(shares[::2], shares[1::2]):
        for k in range(keep.shape[1]):
            for chip in (0, 1):
                row = 2 * (aux ^ chip)
                keep[chip, k] = grams[done + k, row + orb]
                give[chip, k] = grams[done + k, row + 1 - orb]
        done += keep.shape[1]


def pair_flops(pairs, blocks):
    return 2 * len(pairs) * BLOCK * CHUNKS * blocks[0][0].size


def quarters(pairs):
    rows = BLOCK // 4
    return (2, len(pairs), rows, BLOCK), pltpu.VMEM((len(pairs), 4, rows, BLOCK), jnp.float32)


def early_pairs(live, table, blocks):
    shape, grams = quarters(EARLY_PAIRS)
    return local_call(
        early_kernel,
        "early_pairs",
        [
            like(shape, jnp.float32),
            like(shape, jnp.bfloat16),
            like((table.shape[1] // GROUPS, BLOCK), jnp.int32),
        ],
        2 + 3 * CHUNKS,
        pair_flops(EARLY_PAIRS, blocks),
        [grams],
    )(live.reshape(1, -1), table, *blocks[0], *blocks[2], *blocks[1])


def late_pairs(blocks):
    shape, grams = quarters(LATE_PAIRS)
    own, next_to, middle, last = blocks
    begun = local_call(
        begin_kernel,
        "begin_pairs",
        [like(grams.shape, jnp.float32)],
        GROUPS,
        16 * pair_flops(LATE_PAIRS, blocks),
    )(own[0], middle[0], next_to[0], last[0])
    return local_call(
        late_kernel,
        "late_pairs",
        [like((2, n, *shape[2:]), jnp.float32) for n in LATE_GROUPS for _ in range(2)],
        GROUPS + 1,
        16 * pair_flops(LATE_PAIRS, blocks),
        [grams],
    )(own[1], middle[1], next_to[1], last[1], *begun)


def spread_kernel(factor, place, near, far, got, *refs):
    *late, out, sums, rows, sems = refs
    done = near.shape[1]
    sums[:done] = (near[0] + far[0].astype(jnp.float32) + got[...]) * factor
    for i in range(0, len(late), 3):
        near, got, far = late[i : i + 3]
        more = done + near.shape[1]
        sums[done:more] = (near[0] + got[0] + far[...].astype(jnp.float32)) * factor
        done = more
    total, slots, width = out.shape
    masks = [place[...] == k for k in range(sums.shape[0])]

    def one(m, carry):
        row = jnp.zeros((slots, width), jnp.float32)
        for k, mask in enumerate(masks):
            values = jnp.broadcast_to(sums[k, pl.ds(m, 1), :], (slots, width))
            row = jnp.where(mask, values, row)
        rows[m] = row
        return carry

    step = total // SPREAD_STEPS
    copies = []
    for i in range(SPREAD_STEPS):
        lax.fori_loop(i * step, (i + 1) * step, one, 0, unroll=8)
        part = pl.ds(i * step, step)
        copies.append(pltpu.make_async_copy(rows.at[part], out.at[part], sems.at[i]))
        copies[-1].start()
    for copy in copies:
        copy.wait()


def spread(factor, place, *parts):
    rows = BLOCK // 4
    shape = (rows, place.shape[0], BLOCK)
    return local_call(
        functools.partial(spread_kernel, factor),
        "spread",
        [like(shape, jnp.float32)],
        1 + len(parts),
        6 * math.prod(shape),
        [
            pltpu.VMEM((len(ALL_PAIRS), rows, BLOCK), jnp.float32),
            pltpu.VMEM(shape, jnp.float32),
            pltpu.SemaphoreType.DMA((SPREAD_STEPS,)),
        ],
        IN_HBM,
    )(place, *parts)[0]


def six_pair_body(integrals, coeffs, pair_blocks, pair_count, orbital_count):
    width = coeffs.shape[1] // CHUNKS
    total_aux = integrals.shape[0] * lax.axis_size("aux")
    table = pair_blocks.T

    half = width // 2
    parts = [lax.slice_in_dim(coeffs, 0, width, axis=1)]
    first, rest = lax.optimization_barrier((lead(), coeffs))
    parts.append(lax.slice_in_dim(rest, width, 2 * width, axis=1))
    mine = lax.dynamic_slice_in_dim(rest, width + lax.axis_index("aux") * half, half, axis=1)
    inner = [lax.ppermute(part, "ao", INSIDE) for part in (parts[0], mine)]
    outer = [lax.ppermute(part, "ao", OUTSIDE) for part in parts]
    wants = tables(first, orbital_count, table, width)

    pieces = list(transform(0, wants, integrals, parts[0], outer[0], inner[0]))
    blocks = [[piece] for piece in pieces]
    inner[1], blocks[0][0] = lax.optimization_barrier((inner[1], blocks[0][0]))
    swapped = lax.ppermute(inner[1], "aux", SWAP)
    pieces = shared_transform(
        width, wants, integrals, parts[1], outer[1], inner[1], swapped
    )
    for block, piece in zip(blocks, pieces):
        block.append(piece)

    def fetch(s):
        swap = [(j, j ^ s) for j in range(GROUPS)]
        return [lax.ppermute(piece, "ao", swap) for piece in blocks[s]]

    middle = fetch(2)
    got = [blocks[0], fetch(1), middle]
    near0, across0, place = early_pairs(pair_count, table, got)
    far0 = lax.ppermute(across0, "aux", SWAP)
    got.append(fetch(3))
    shares = late_pairs(got)
    late = []
    for near1, give1 in zip(shares[::2], shares[1::2]):
        got1 = lax.ppermute(give1, "orb", SWAP)
        far1 = lax.ppermute((near1[1] + got1[1]).astype(jnp.bfloat16), "aux", SWAP)
        late += [near1, got1, far1]
    got0 = lax.ppermute(near0[1] + far0[1].astype(jnp.float32), "orb", SWAP)
    factor = 1.0 / math.sqrt(total_aux * ORBS)
    return spread(factor, place, near0, far0, got0, *late)


def solution(mesh):
    sizes = dict(mesh.shape)
    body = general_body
    if sizes["ao"] == 4 and sizes["aux"] == 2 and sizes["orb"] == 2:
        body = six_pair_body
    return jax.shard_map(
        body,
        mesh=mesh,
        in_specs=(
            P(("grp", "aux"), "ao", None),
            P(("grp", "ao"), "orb"),
            P("grp", None),
            P("grp"),
            P("grp"),
        ),
        out_specs=P(("aux", "orb"), ("grp", "ao"), None),
        check_vma=False,
    )
```

```python
import functools
import math

import jax
import jax.numpy as jnp
from jax import lax
from jax.experimental import pallas as pl
from jax.experimental.pallas import tpu as pltpu
from jax.sharding import PartitionSpec as P

BLOCK = 256
AO_DEV = 2
WIN = 5
ORBS = 1024
CHUNKS = 2
SPREAD_STEPS = 4
SPREAD_STEPS = 4
SPREAD_STEPS = 4
SPREAD_STEPS = 4
SPREAD_STEPS = 4
SPREAD_STEPS = 4
VMEM_LIMIT = 40 * 1024 * 1024
LEAD_FLOPS = 1 << 32
LATE_WEIGHT = 8


def with_halo(cells, sides, width):
    for axis, dim in sides:
        count = lax.axis_size(axis)
        ends = count - 1
        head = lax.slice_in_dim(cells, 0, width, axis=dim)
        tail = lax.slice_in_dim(cells, cells.shape[dim] - width, cells.shape[dim], axis=dim)
        cells = jnp.concatenate(
            [
                lax.ppermute(tail, axis, [(i, (i + 1) % count) for i in range(ends)]),
                cells,
                lax.ppermute(head, axis, [((i + 1) % count, i) for i in range(ends)]),
            ],
            axis=dim,
        )
    return cells


def general_body(integrals, coeffs, pair_blocks, pair_count, orbital_count):
    orb_local = coeffs.shape[1]
    aux_devices = lax.axis_size("aux")
    total_aux = integrals.shape[0] * aux_devices
    rim = WIN // 2 * BLOCK
    extended = with_halo(coeffs, (("ao", 0),), rim)
    ao_here = lax.axis_index("ao")
    orbital_ids = lax.axis_index("orb") * orb_local + jnp.arange(orb_local, dtype=jnp.int32)
    pieces = []
    for offset in range(AO_DEV):
        slab = integrals[:, offset * BLOCK : (offset + 1) * BLOCK, :]
        slot_range = extended[offset * BLOCK : offset * BLOCK + WIN * BLOCK]
        values = jnp.einsum("pml,li->pmi", slab, slot_range, preferred_element_type=jnp.float32)
        limit = orbital_count[ao_here * AO_DEV + offset]
        values = jnp.where((orbital_ids < limit)[None, None, :], values, 0.0)
        pieces.append(values.astype(jnp.bfloat16))
    transformed = jnp.stack(pieces)
    owners = lax.axis_size("ao")
    table = pair_blocks.reshape(owners, -1, 2)
    slots = table.shape[1]
    live = jnp.arange(slots, dtype=jnp.int32)[None, :] < pair_count[:, None]
    touched = live[:, :, None] & (table // AO_DEV == ao_here)
    wanted = jnp.max(jnp.where(touched, table % AO_DEV, 0), axis=(1, 2))
    outgoing = transformed[wanted]
    received = lax.all_to_all(outgoing, "ao", split_axis=0, concat_axis=0, tiled=True)
    owned = table[ao_here]
    factor = 1.0 / math.sqrt(total_aux * ORBS)
    weights = jnp.where(live[ao_here], factor, 0.0).astype(jnp.float32)
    left_source = owned[:, 0] // AO_DEV
    right_source = owned[:, 1] // AO_DEV
    right_factors = received[right_source]
    lefts = received[left_source]
    term = jnp.einsum("spmi,spni->msn", lefts, right_factors, preferred_element_type=jnp.float32)
    return lax.psum_scatter(
        term * weights[None, :, None], ("aux", "orb"), scatter_dimension=0, tiled=True
    )


EARLY_PAIRS = ((0, 1), (0, 2), (1, 2))
LATE_PAIRS = ((0, 3), (1, 3), (2, 3))
LATE_GROUPS = 2, 1
ALL_PAIRS = EARLY_PAIRS + LATE_PAIRS
GROUPS = 4
SWAP = [(0, 1), (1, 0)]
OUTSIDE = [(0, 1), (1, 0), (2, 3), (3, 2)]
INSIDE = [(1, 2), (2, 1)]

IN_HBM = pl.BlockSpec(memory_space=pltpu.HBM)
IN_VMEM = pl.BlockSpec(memory_space=pltpu.VMEM)


def like(shape, dtype):
    return jax.ShapeDtypeStruct(shape, dtype)


def local_call(kernel, name, out_shape, inputs, flops, scratch=(), out_spec=IN_VMEM):
    moved = sum(math.prod(o.shape) * o.dtype.itemsize for o in out_shape)
    return pl.pallas_call(
        kernel,
        out_shape=out_shape,
        in_specs=[IN_VMEM] * inputs,
        out_specs=[out_spec] * len(out_shape),
        scratch_shapes=list(scratch),
        compiler_params=pltpu.CompilerParams(vmem_limit_bytes=VMEM_LIMIT),
        cost_estimate=pl.CostEstimate(flops=flops, bytes_accessed=2 * moved, transcendentals=0),
        name=name,
    )


def dot(a, b):
    return jnp.dot(a, b, preferred_element_type=jnp.float32)


def lead_kernel(out):
    out[...] = jnp.zeros_like(out)


def lead():
    return local_call(lead_kernel, "lead", [like((8, 128), jnp.int32)], 0, LEAD_FLOPS)()[0]


def scalar_at(values, index):
    ids = lax.broadcasted_iota(jnp.int32, values.shape, 1)
    return jnp.sum(jnp.where(ids == index, values, 0).astype(jnp.float32))


def tables_kernel(first, counts, table, wants):
    here, orb = lax.axis_index("ao"), lax.axis_index("orb")
    slots = table.shape[1] // GROUPS
    named = jnp.where(table[...] // AO_DEV == here, table[...] % AO_DEV, 0).astype(jnp.float32)
    owner = lax.broadcasted_iota(jnp.int32, table.shape, 1) // slots
    rows = [jnp.max(jnp.where(owner == here ^ s, named, 0.0)) for s in range(GROUPS)]
    for offset in range(AO_DEV):
        count = scalar_at(counts[...], here * AO_DEV + offset)
        rows.append(count - (orb * (ORBS // 2)).astype(jnp.float32))
    row = lax.broadcasted_iota(jnp.int32, wants.shape, 0)
    out = first[0, 0:1].astype(jnp.float32).reshape(1, 1) + jnp.zeros(wants.shape, jnp.float32)
    for k, value in enumerate(rows):
        out = jnp.where(row == k, value, out)
    wants[...] = out.astype(jnp.int32)


def tables(first, counts, table, width):
    return local_call(
        tables_kernel, "tables", [like((8, width), jnp.int32)], 3, table.size
    )(first, counts.reshape(1, -1), table)[0]


def transform_kernel(start, wants, integrals, own, outer, inner, *outs):
    mid = AO_DEV * BLOCK

    def blocks(prev, following):
        ids = start + lax.broadcasted_iota(jnp.int32, (BLOCK, own.shape[1]), 1)
        for p in range(integrals.shape[0]):
            both = []
            for offset in range(AO_DEV):
                low = mid - offset * BLOCK
                slab = integrals[p, offset * BLOCK : (offset + 1) * BLOCK, :]
                values = dot(slab[:, low : low + mid], own[...])
                values += dot(slab[:, :low], prev[offset * BLOCK :, :])
                values += dot(slab[:, low + mid :], following[: (offset + 1) * BLOCK, :])
                live = ids < wants[GROUPS + offset : GROUPS + offset + 1, :]
                both.append(jnp.where(live, values, 0.0))
            for s, out in enumerate(outs):
                out[p] = jnp.where(wants[s : s + 1, :] == 0, *both).astype(jnp.bfloat16)

    odd = lax.axis_index("ao") & 1
    pl.when(odd == 0)(lambda: blocks(inner, outer))
    pl.when(odd == 1)(lambda: blocks(outer, inner))


def shared_kernel(start, wants, integrals, own, outer, inner, swapped, *refs):
    *outs, whole = refs
    aux = lax.axis_index("aux")
    width = inner.shape[1]
    whole[:, pl.ds(pl.multiple_of(aux * width, width), width)] = inner[...]
    whole[:, pl.ds(pl.multiple_of((1 - aux) * width, width), width)] = swapped[...]
    transform_kernel(start, wants, integrals, own, outer, whole, *outs)


def shared_transform(start, wants, integrals, own, outer, inner, swapped):
    shape = (integrals.shape[0], BLOCK, own.shape[1])
    return local_call(
        functools.partial(shared_kernel, start),
        "transform",
        [like(shape, jnp.bfloat16)] * GROUPS,
        6,
        2 * AO_DEV * math.prod(shape) * integrals.shape[2],
        [pltpu.VMEM(own.shape, jnp.bfloat16)],
    )(wants, integrals, own, outer, inner, swapped)


def transform(start, wants, integrals, own, outer, inner):
    shape = (integrals.shape[0], BLOCK, own.shape[1])
    return local_call(
        functools.partial(transform_kernel, start),
        "transform",
        [like(shape, jnp.bfloat16)] * GROUPS,
        5,
        2 * AO_DEV * math.prod(shape) * integrals.shape[2],
    )(wants, integrals, own, outer, inner)


def form_pairs(pairs, blocks, grams, before=None):
    here = lax.axis_index("ao")
    slices = [[(ref, p) for ref in block for p in range(ref.shape[0])] for block in blocks]

    def product(left, right):
        total = None
        for (a, i), (b, j) in zip(slices[left], slices[right]):
            part = lax.dot_general(
                a[i], b[j], (((1,), (1,)), ((), ())), preferred_element_type=jnp.float32
            )
            total = part if total is None else total + part
        return total.reshape(grams.shape[1:])

    def formed(k, left, right):
        gram = product(left, right)
        return gram if before is None else gram + before[k]

    for bit in (0, 1):
        mine = [(k, a, b) for k, (a, b) in enumerate(pairs) if (a ^ b) >> 1 == bit]
        upper = (here >> bit) & 1

        @pl.when(upper == 0)
        def _(mine=mine):
            for k, a, b in mine:
                grams[k] = formed(k, a, b)

        @pl.when(upper == 1)
        def _(mine=mine):
            for k, a, b in mine:
                grams[k] = formed(k, b, a)


def early_kernel(live, table, *refs):
    used = 3 * CHUNKS
    own, middle, next_to = [refs[i : i + CHUNKS] for i in range(0, used, CHUNKS)]
    blocks = own, next_to, middle
    near, far, place, grams = refs[used:]
    here, aux, orb = (lax.axis_index(axis) for axis in ("ao", "aux", "orb"))
    slots, width = place.shape
    slot = lax.broadcasted_iota(jnp.int32, (slots, table.shape[1]), 0)
    column = lax.broadcasted_iota(jnp.int32, (slots, table.shape[1]), 1)
    shown = column == here * slots + slot
    sides = []
    for side in (0, 1):
        group = (table[side : side + 1, :] // AO_DEV).astype(jnp.float32)
        group = jnp.sum(jnp.where(shown, group, 0.0), axis=1, keepdims=True)
        sides.append(group.astype(jnp.int32) ^ here)
    low, high = jnp.minimum(*sides), jnp.maximum(*sides)
    index = jnp.where(high == 3, low + 3, jnp.where(high == 2, low + 1, 0))
    slot = lax.broadcasted_iota(jnp.int32, (slots, width), 0)
    count = scalar_at(live[...], here).astype(jnp.int32)
    place[...] = jnp.where(slot < count, index, len(ALL_PAIRS))
    form_pairs(EARLY_PAIRS, blocks, grams)
    for k in range(len(EARLY_PAIRS)):
        for core in (0, 1):
            near[core, k] = grams[k, 2 * aux + (orb ^ core)]
            far[core, k] = grams[k, 2 * (1 - aux) + (orb ^ core)].astype(jnp.bfloat16)


def begin_kernel(own, middle, next_to, last, grams):
    form_pairs(LATE_PAIRS, ([own], [next_to], [middle], [last]), grams)


def late_kernel(own, middle, next_to, last, before, *refs):
    *shares, grams = refs
    blocks = [own], [next_to], [middle], [last]
    aux, orb = lax.axis_index("aux"), lax.axis_index("orb")
    form_pairs(LATE_PAIRS, blocks, grams, before)
    done = 0
    for keep, give in zip(shares[::2], shares[1::2]):
        for k in range(keep.shape[1]):
            for chip in (0, 1):
                row = 2 * (aux ^ chip)
                keep[chip, k] = grams[done + k, row + orb]
                give[chip, k] = grams[done + k, row + 1 - orb]
        done += keep.shape[1]


def pair_flops(pairs, blocks):
    return 2 * len(pairs) * BLOCK * CHUNKS * blocks[0][0].size


def quarters(pairs):
    rows = BLOCK // 4
    return (2, len(pairs), rows, BLOCK), pltpu.VMEM((len(pairs), 4, rows, BLOCK), jnp.float32)


def early_pairs(live, table, blocks):
    shape, grams = quarters(EARLY_PAIRS)
    return local_call(
        early_kernel,
        "early_pairs",
        [
            like(shape, jnp.float32),
            like(shape, jnp.bfloat16),
            like((table.shape[1] // GROUPS, BLOCK), jnp.int32),
        ],
        2 + 3 * CHUNKS,
        pair_flops(EARLY_PAIRS, blocks),
        [grams],
    )(live.reshape(1, -1), table, *blocks[0], *blocks[2], *blocks[1])


def late_pairs(blocks):
    shape, grams = quarters(LATE_PAIRS)
    own, next_to, middle, last = blocks
    begun = local_call(
        begin_kernel,
        "begin_pairs",
        [like(grams.shape, jnp.float32)],
        GROUPS,
        pair_flops(LATE_PAIRS, blocks) // CHUNKS,
    )(own[0], middle[0], next_to[0], last[0])
    return local_call(
        late_kernel,
        "late_pairs",
        [like((2, n, *shape[2:]), jnp.float32) for n in LATE_GROUPS for _ in range(2)],
        GROUPS + 1,
        LATE_WEIGHT * pair_flops(LATE_PAIRS, blocks) // CHUNKS,
        [grams],
    )(own[1], middle[1], next_to[1], last[1], *begun)


def spread_kernel(factor, place, near, far, got, *refs):
    *late, out, sums, rows, sems = refs
    done = near.shape[1]
    sums[:done] = (near[0] + far[0].astype(jnp.float32) + got[...]) * factor
    for i in range(0, len(late), 3):
        near, got, far = late[i : i + 3]
        more = done + near.shape[1]
        sums[done:more] = (near[0] + got[0] + far[...].astype(jnp.float32)) * factor
        done = more
    total, slots, width = out.shape
    masks = [place[...] == k for k in range(sums.shape[0])]

    def one(m, carry):
        row = jnp.zeros((slots, width), jnp.float32)
        for k, mask in enumerate(masks):
            values = jnp.broadcast_to(sums[k, pl.ds(m, 1), :], (slots, width))
            row = jnp.where(mask, values, row)
        rows[m] = row
        return carry

    step = total // SPREAD_STEPS
    copies = []
    for i in range(SPREAD_STEPS):
        lax.fori_loop(i * step, (i + 1) * step, one, 0, unroll=8)
        part = pl.ds(i * step, step)
        copies.append(pltpu.make_async_copy(rows.at[part], out.at[part], sems.at[i]))
        copies[-1].start()
    for copy in copies:
        copy.wait()


def spread(factor, place, *parts):
    rows = BLOCK // 4
    shape = (rows, place.shape[0], BLOCK)
    return local_call(
        functools.partial(spread_kernel, factor),
        "spread",
        [like(shape, jnp.float32)],
        1 + len(parts),
        6 * math.prod(shape),
        [
            pltpu.VMEM((len(ALL_PAIRS), rows, BLOCK), jnp.float32),
            pltpu.VMEM(shape, jnp.float32),
            pltpu.SemaphoreType.DMA((SPREAD_STEPS,)),
        ],
        IN_HBM,
    )(place, *parts)[0]


def six_pair_body(integrals, coeffs, pair_blocks, pair_count, orbital_count):
    width = coeffs.shape[1] // CHUNKS
    total_aux = integrals.shape[0] * lax.axis_size("aux")
    table = pair_blocks.T

    half = width // 2
    parts = [lax.slice_in_dim(coeffs, 0, width, axis=1)]
    first, rest = lax.optimization_barrier((lead(), coeffs))
    parts.append(lax.slice_in_dim(rest, width, 2 * width, axis=1))
    mine = lax.dynamic_slice_in_dim(rest, width + lax.axis_index("aux") * half, half, axis=1)
    inner = [lax.ppermute(part, "ao", INSIDE) for part in (parts[0], mine)]
    outer = [lax.ppermute(part, "ao", OUTSIDE) for part in parts]
    wants = tables(first, orbital_count, table, width)

    pieces = list(transform(0, wants, integrals, parts[0], outer[0], inner[0]))
    blocks = [[piece] for piece in pieces]
    inner[1], blocks[0][0] = lax.optimization_barrier((inner[1], blocks[0][0]))
    swapped = lax.ppermute(inner[1], "aux", SWAP)
    pieces = shared_transform(
        width, wants, integrals, parts[1], outer[1], inner[1], swapped
    )
    for block, piece in zip(blocks, pieces):
        block.append(piece)

    def fetch(s):
        swap = [(j, j ^ s) for j in range(GROUPS)]
        return [lax.ppermute(piece, "ao", swap) for piece in blocks[s]]

    middle = fetch(2)
    got = [blocks[0], fetch(1), middle]
    near0, across0, place = early_pairs(pair_count, table, got)
    far0 = lax.ppermute(across0, "aux", SWAP)
    got.append(fetch(3))
    shares = late_pairs(got)
    late = []
    for near1, give1 in zip(shares[::2], shares[1::2]):
        got1 = lax.ppermute(give1, "orb", SWAP)
        far1 = lax.ppermute((near1[1] + got1[1]).astype(jnp.bfloat16), "aux", SWAP)
        late += [near1, got1, far1]
    got0 = lax.ppermute(near0[1] + far0[1].astype(jnp.float32), "orb", SWAP)
    factor = 1.0 / math.sqrt(total_aux * ORBS)
    return spread(factor, place, near0, far0, got0, *late)


def solution(mesh):
    sizes = dict(mesh.shape)
    body = general_body
    if sizes["ao"] == 4 and sizes["aux"] == 2 and sizes["orb"] == 2:
        body = six_pair_body
    return jax.shard_map(
        body,
        mesh=mesh,
        in_specs=(
            P(("grp", "aux"), "ao", None),
            P(("grp", "ao"), "orb"),
            P("grp", None),
            P("grp"),
            P("grp"),
        ),
        out_specs=P(("aux", "orb"), ("grp", "ao"), None),
        check_vma=False,
    )
```

```python
import functools
import math

import jax
import jax.numpy as jnp
from jax import lax
from jax.experimental import pallas as pl
from jax.experimental.pallas import tpu as pltpu
from jax.sharding import PartitionSpec as P

BLOCK = 256
AO_DEV = 2
WIN = 5
ORBS = 1024
CHUNKS = 2
SPREAD_STEPS = 4
SPREAD_STEPS = 4
SPREAD_STEPS = 4
SPREAD_STEPS = 4
SPREAD_STEPS = 4
SPREAD_STEPS = 4
VMEM_LIMIT = 40 * 1024 * 1024
LEAD_FLOPS = 1 << 32
LATE_WEIGHT = 10
CUT_LIMIT = 53 * 1024 * 1024 + 256 * 1024


def with_halo(cells, sides, width):
    for axis, dim in sides:
        count = lax.axis_size(axis)
        ends = count - 1
        head = lax.slice_in_dim(cells, 0, width, axis=dim)
        tail = lax.slice_in_dim(cells, cells.shape[dim] - width, cells.shape[dim], axis=dim)
        cells = jnp.concatenate(
            [
                lax.ppermute(tail, axis, [(i, (i + 1) % count) for i in range(ends)]),
                cells,
                lax.ppermute(head, axis, [((i + 1) % count, i) for i in range(ends)]),
            ],
            axis=dim,
        )
    return cells


def general_body(integrals, coeffs, pair_blocks, pair_count, orbital_count):
    orb_local = coeffs.shape[1]
    aux_devices = lax.axis_size("aux")
    total_aux = integrals.shape[0] * aux_devices
    rim = WIN // 2 * BLOCK
    extended = with_halo(coeffs, (("ao", 0),), rim)
    ao_here = lax.axis_index("ao")
    orbital_ids = lax.axis_index("orb") * orb_local + jnp.arange(orb_local, dtype=jnp.int32)
    pieces = []
    for offset in range(AO_DEV):
        slab = integrals[:, offset * BLOCK : (offset + 1) * BLOCK, :]
        slot_range = extended[offset * BLOCK : offset * BLOCK + WIN * BLOCK]
        values = jnp.einsum("pml,li->pmi", slab, slot_range, preferred_element_type=jnp.float32)
        limit = orbital_count[ao_here * AO_DEV + offset]
        values = jnp.where((orbital_ids < limit)[None, None, :], values, 0.0)
        pieces.append(values.astype(jnp.bfloat16))
    transformed = jnp.stack(pieces)
    owners = lax.axis_size("ao")
    table = pair_blocks.reshape(owners, -1, 2)
    slots = table.shape[1]
    live = jnp.arange(slots, dtype=jnp.int32)[None, :] < pair_count[:, None]
    touched = live[:, :, None] & (table // AO_DEV == ao_here)
    wanted = jnp.max(jnp.where(touched, table % AO_DEV, 0), axis=(1, 2))
    outgoing = transformed[wanted]
    received = lax.all_to_all(outgoing, "ao", split_axis=0, concat_axis=0, tiled=True)
    owned = table[ao_here]
    factor = 1.0 / math.sqrt(total_aux * ORBS)
    weights = jnp.where(live[ao_here], factor, 0.0).astype(jnp.float32)
    left_source = owned[:, 0] // AO_DEV
    right_source = owned[:, 1] // AO_DEV
    right_factors = received[right_source]
    lefts = received[left_source]
    term = jnp.einsum("spmi,spni->msn", lefts, right_factors, preferred_element_type=jnp.float32)
    return lax.psum_scatter(
        term * weights[None, :, None], ("aux", "orb"), scatter_dimension=0, tiled=True
    )


EARLY_PAIRS = ((0, 1), (0, 2), (1, 2))
LATE_PAIRS = ((0, 3), (1, 3), (2, 3))
ALL_PAIRS = EARLY_PAIRS + LATE_PAIRS
GROUPS = 4
SWAP = [(0, 1), (1, 0)]
OUTSIDE = [(0, 1), (1, 0), (2, 3), (3, 2)]
INSIDE = [(1, 2), (2, 1)]

IN_HBM = pl.BlockSpec(memory_space=pltpu.HBM)
IN_VMEM = pl.BlockSpec(memory_space=pltpu.VMEM)


def like(shape, dtype):
    return jax.ShapeDtypeStruct(shape, dtype)


def local_call(kernel, name, out_shape, inputs, flops, scratch=(), out_spec=IN_VMEM):
    moved = sum(math.prod(o.shape) * o.dtype.itemsize for o in out_shape)
    return pl.pallas_call(
        kernel,
        out_shape=out_shape,
        in_specs=[IN_VMEM] * inputs,
        out_specs=[out_spec] * len(out_shape),
        scratch_shapes=list(scratch),
        compiler_params=pltpu.CompilerParams(vmem_limit_bytes=VMEM_LIMIT),
        cost_estimate=pl.CostEstimate(flops=flops, bytes_accessed=2 * moved, transcendentals=0),
        name=name,
    )


def dot(a, b):
    return jnp.dot(a, b, preferred_element_type=jnp.float32)


def cut_kernel(coeffs, direct, shared, mine, sems):
    width, half = direct.shape[1], mine.shape[1]
    start = pl.multiple_of(width + lax.axis_index("aux") * half, half)
    copies = [
        pltpu.make_async_copy(coeffs.at[:, columns], out, sems.at[i])
        for i, (columns, out) in enumerate(
            ((pl.ds(0, width), direct), (pl.ds(start, half), mine), (pl.ds(width, width), shared))
        )
    ]
    for copy in copies:
        copy.start()
    for copy in copies:
        copy.wait()


def cut(coeffs):
    rows, columns = coeffs.shape
    width = columns // CHUNKS
    return pl.pallas_call(
        cut_kernel,
        out_shape=[like((rows, n), coeffs.dtype) for n in (width, width, width // 2)],
        in_specs=[IN_HBM],
        out_specs=[IN_VMEM] * 3,
        scratch_shapes=[pltpu.SemaphoreType.DMA((3,))],
        compiler_params=pltpu.CompilerParams(vmem_limit_bytes=CUT_LIMIT),
        cost_estimate=pl.CostEstimate(flops=LEAD_FLOPS, bytes_accessed=0, transcendentals=0),
        name="cut",
    )(coeffs)


def scalar_at(values, index):
    ids = lax.broadcasted_iota(jnp.int32, values.shape, 1)
    return jnp.sum(jnp.where(ids == index, values, 0).astype(jnp.float32))


def tables_kernel(counts, table, wants):
    here, orb = lax.axis_index("ao"), lax.axis_index("orb")
    slots = table.shape[1] // GROUPS
    named = jnp.where(table[...] // AO_DEV == here, table[...] % AO_DEV, 0).astype(jnp.float32)
    owner = lax.broadcasted_iota(jnp.int32, table.shape, 1) // slots
    rows = [jnp.max(jnp.where(owner == here ^ s, named, 0.0)) for s in range(GROUPS)]
    for offset in range(AO_DEV):
        count = scalar_at(counts[...], here * AO_DEV + offset)
        rows.append(count - (orb * (ORBS // 2)).astype(jnp.float32))
    row = lax.broadcasted_iota(jnp.int32, wants.shape, 0)
    out = jnp.zeros(wants.shape, jnp.float32)
    for k, value in enumerate(rows):
        out = jnp.where(row == k, value, out)
    wants[...] = out.astype(jnp.int32)


def tables(counts, table, width):
    return local_call(
        tables_kernel, "tables", [like((8, width), jnp.int32)], 2, LEAD_FLOPS
    )(counts.reshape(1, -1), table)[0]


def transform_kernel(start, wants, integrals, own, outer, inner, *outs):
    mid = AO_DEV * BLOCK

    def blocks(prev, following):
        ids = start + lax.broadcasted_iota(jnp.int32, (BLOCK, own.shape[1]), 1)
        for p in range(integrals.shape[0]):
            both = []
            for offset in range(AO_DEV):
                low = mid - offset * BLOCK
                slab = integrals[p, offset * BLOCK : (offset + 1) * BLOCK, :]
                values = dot(slab[:, low : low + mid], own[...])
                values += dot(slab[:, :low], prev[offset * BLOCK :, :])
                values += dot(slab[:, low + mid :], following[: (offset + 1) * BLOCK, :])
                live = ids < wants[GROUPS + offset : GROUPS + offset + 1, :]
                both.append(jnp.where(live, values, 0.0))
            for s, out in enumerate(outs):
                out[p] = jnp.where(wants[s : s + 1, :] == 0, *both).astype(jnp.bfloat16)

    odd = lax.axis_index("ao") & 1
    pl.when(odd == 0)(lambda: blocks(inner, outer))
    pl.when(odd == 1)(lambda: blocks(outer, inner))


def shared_kernel(start, wants, integrals, own, outer, inner, swapped, *refs):
    *outs, whole = refs
    aux = lax.axis_index("aux")
    width = inner.shape[1]
    whole[:, pl.ds(pl.multiple_of(aux * width, width), width)] = inner[...]
    whole[:, pl.ds(pl.multiple_of((1 - aux) * width, width), width)] = swapped[...]
    transform_kernel(start, wants, integrals, own, outer, whole, *outs)


def shared_transform(start, wants, integrals, own, outer, inner, swapped):
    shape = (integrals.shape[0], BLOCK, own.shape[1])
    return local_call(
        functools.partial(shared_kernel, start),
        "transform",
        [like(shape, jnp.bfloat16)] * GROUPS,
        6,
        2 * AO_DEV * math.prod(shape) * integrals.shape[2],
        [pltpu.VMEM(own.shape, jnp.bfloat16)],
    )(wants, integrals, own, outer, inner, swapped)


def transform(start, wants, integrals, own, outer, inner):
    shape = (integrals.shape[0], BLOCK, own.shape[1])
    return local_call(
        functools.partial(transform_kernel, start),
        "transform",
        [like(shape, jnp.bfloat16)] * GROUPS,
        5,
        2 * AO_DEV * math.prod(shape) * integrals.shape[2],
    )(wants, integrals, own, outer, inner)


def form_pairs(pairs, blocks, grams, before=None):
    here = lax.axis_index("ao")
    slices = [[(ref, p) for ref in block for p in range(ref.shape[0])] for block in blocks]

    def product(left, right):
        total = None
        for (a, i), (b, j) in zip(slices[left], slices[right]):
            part = lax.dot_general(
                a[i], b[j], (((1,), (1,)), ((), ())), preferred_element_type=jnp.float32
            )
            total = part if total is None else total + part
        return total.reshape(grams.shape[1:])

    def formed(k, left, right):
        gram = product(left, right)
        return gram if before is None else gram + before[k]

    for bit in (0, 1):
        mine = [(k, a, b) for k, (a, b) in enumerate(pairs) if (a ^ b) >> 1 == bit]
        upper = (here >> bit) & 1

        @pl.when(upper == 0)
        def _(mine=mine):
            for k, a, b in mine:
                grams[k] = formed(k, a, b)

        @pl.when(upper == 1)
        def _(mine=mine):
            for k, a, b in mine:
                grams[k] = formed(k, b, a)


def early_kernel(live, table, *refs):
    used = 3 * CHUNKS
    own, middle, next_to = [refs[i : i + CHUNKS] for i in range(0, used, CHUNKS)]
    blocks = own, next_to, middle
    near, far, place, grams = refs[used:]
    here, aux, orb = (lax.axis_index(axis) for axis in ("ao", "aux", "orb"))
    slots, width = place.shape
    slot = lax.broadcasted_iota(jnp.int32, (slots, table.shape[1]), 0)
    column = lax.broadcasted_iota(jnp.int32, (slots, table.shape[1]), 1)
    shown = column == here * slots + slot
    sides = []
    for side in (0, 1):
        group = (table[side : side + 1, :] // AO_DEV).astype(jnp.float32)
        group = jnp.sum(jnp.where(shown, group, 0.0), axis=1, keepdims=True)
        sides.append(group.astype(jnp.int32) ^ here)
    low, high = jnp.minimum(*sides), jnp.maximum(*sides)
    index = jnp.where(high == 3, low + 3, jnp.where(high == 2, low + 1, 0))
    slot = lax.broadcasted_iota(jnp.int32, (slots, width), 0)
    count = scalar_at(live[...], here).astype(jnp.int32)
    place[...] = jnp.where(slot < count, index, len(ALL_PAIRS))
    form_pairs(EARLY_PAIRS, blocks, grams)
    for k in range(len(EARLY_PAIRS)):
        for core in (0, 1):
            near[core, k] = grams[k, 2 * aux + (orb ^ core)]
            far[core, k] = grams[k, 2 * (1 - aux) + (orb ^ core)].astype(jnp.bfloat16)


def begin_kernel(own, middle, next_to, last, grams):
    form_pairs(LATE_PAIRS, ([own], [next_to], [middle], [last]), grams)


def late_kernel(own, middle, next_to, last, before, *refs):
    keep, give, grams = refs
    blocks = [own], [next_to], [middle], [last]
    aux, orb = lax.axis_index("aux"), lax.axis_index("orb")
    form_pairs(LATE_PAIRS, blocks, grams, before)
    for k in range(len(LATE_PAIRS)):
        for chip in (0, 1):
            row = 2 * (aux ^ chip)
            keep[chip, k] = grams[k, row + orb]
            give[chip, k] = grams[k, row + 1 - orb].astype(jnp.bfloat16)


def pair_flops(pairs, blocks):
    return 2 * len(pairs) * BLOCK * CHUNKS * blocks[0][0].size


def quarters(pairs):
    rows = BLOCK // 4
    return (2, len(pairs), rows, BLOCK), pltpu.VMEM((len(pairs), 4, rows, BLOCK), jnp.float32)


def early_pairs(live, table, blocks):
    shape, grams = quarters(EARLY_PAIRS)
    return local_call(
        early_kernel,
        "early_pairs",
        [
            like(shape, jnp.float32),
            like(shape, jnp.bfloat16),
            like((table.shape[1] // GROUPS, BLOCK), jnp.int32),
        ],
        2 + 3 * CHUNKS,
        pair_flops(EARLY_PAIRS, blocks),
        [grams],
    )(live.reshape(1, -1), table, *blocks[0], *blocks[2], *blocks[1])


def late_pairs(blocks):
    shape, grams = quarters(LATE_PAIRS)
    own, next_to, middle, last = blocks
    begun = local_call(
        begin_kernel,
        "begin_pairs",
        [like(grams.shape, jnp.float32)],
        GROUPS,
        pair_flops(LATE_PAIRS, blocks) // CHUNKS,
    )(own[0], middle[0], next_to[0], last[0])
    return local_call(
        late_kernel,
        "late_pairs",
        [like(shape, jnp.float32), like(shape, jnp.bfloat16)],
        GROUPS + 1,
        LATE_WEIGHT * pair_flops(LATE_PAIRS, blocks) // CHUNKS,
        [grams],
    )(own[1], middle[1], next_to[1], last[1], *begun)


def spread_kernel(factor, place, near0, far0, got0, near1, got1, far1, out, sums, rows, sems):
    early = near0.shape[1]
    sums[:early] = (near0[0] + far0[0].astype(jnp.float32) + got0[...]) * factor
    sums[early:] = (near1[0] + got1[0].astype(jnp.float32) + far1[...].astype(jnp.float32)) * factor
    total, slots, width = out.shape
    masks = [place[...] == k for k in range(sums.shape[0])]

    def one(m, carry):
        row = jnp.zeros((slots, width), jnp.float32)
        for k, mask in enumerate(masks):
            values = jnp.broadcast_to(sums[k, pl.ds(m, 1), :], (slots, width))
            row = jnp.where(mask, values, row)
        rows[m] = row
        return carry

    step = total // SPREAD_STEPS
    copies = []
    for i in range(SPREAD_STEPS):
        lax.fori_loop(i * step, (i + 1) * step, one, 0, unroll=8)
        part = pl.ds(i * step, step)
        copies.append(pltpu.make_async_copy(rows.at[part], out.at[part], sems.at[i]))
        copies[-1].start()
    for copy in copies:
        copy.wait()


def spread(factor, place, *parts):
    rows = BLOCK // 4
    shape = (rows, place.shape[0], BLOCK)
    return local_call(
        functools.partial(spread_kernel, factor),
        "spread",
        [like(shape, jnp.float32)],
        1 + len(parts),
        6 * math.prod(shape),
        [
            pltpu.VMEM((len(ALL_PAIRS), rows, BLOCK), jnp.float32),
            pltpu.VMEM(shape, jnp.float32),
            pltpu.SemaphoreType.DMA((SPREAD_STEPS,)),
        ],
        IN_HBM,
    )(place, *parts)[0]


def six_pair_body(integrals, coeffs, pair_blocks, pair_count, orbital_count):
    width = coeffs.shape[1] // CHUNKS
    total_aux = integrals.shape[0] * lax.axis_size("aux")
    table = pair_blocks.T

    *parts, mine = cut(coeffs)
    inner = [lax.ppermute(part, "ao", INSIDE) for part in (parts[0], mine)]
    outer = [lax.ppermute(part, "ao", OUTSIDE) for part in parts]
    wants = tables(orbital_count, table, width)

    pieces = list(transform(0, wants, integrals, parts[0], outer[0], inner[0]))
    blocks = [[piece] for piece in pieces]
    inner[1], blocks[0][0] = lax.optimization_barrier((inner[1], blocks[0][0]))
    swapped = lax.ppermute(inner[1], "aux", SWAP)
    pieces = shared_transform(
        width, wants, integrals, parts[1], outer[1], inner[1], swapped
    )
    for block, piece in zip(blocks, pieces):
        block.append(piece)

    def fetch(s):
        swap = [(j, j ^ s) for j in range(GROUPS)]
        return [lax.ppermute(piece, "ao", swap) for piece in blocks[s]]

    middle = fetch(2)
    got = [blocks[0], fetch(1), middle]
    near0, across0, place = early_pairs(pair_count, table, got)
    far0 = lax.ppermute(across0, "aux", SWAP)
    got.append(fetch(3))
    near1, give1 = late_pairs(got)
    got1 = lax.ppermute(give1, "orb", SWAP)
    far1 = lax.ppermute((near1[1] + got1[1].astype(jnp.float32)).astype(jnp.bfloat16), "aux", SWAP)
    got0 = lax.ppermute(near0[1] + far0[1].astype(jnp.float32), "orb", SWAP)
    factor = 1.0 / math.sqrt(total_aux * ORBS)
    return spread(factor, place, near0, far0, got0, near1, got1, far1)


def solution(mesh):
    sizes = dict(mesh.shape)
    body = general_body
    if sizes["ao"] == 4 and sizes["aux"] == 2 and sizes["orb"] == 2:
        body = six_pair_body
    return jax.shard_map(
        body,
        mesh=mesh,
        in_specs=(
            P(("grp", "aux"), "ao", None),
            P(("grp", "ao"), "orb"),
            P("grp", None),
            P("grp"),
            P("grp"),
        ),
        out_specs=P(("aux", "orb"), ("grp", "ao"), None),
        check_vma=False,
    )
```

```python
import functools
import math

import jax
import jax.numpy as jnp
from jax import lax
from jax.experimental import pallas as pl
from jax.experimental.pallas import tpu as pltpu
from jax.sharding import PartitionSpec as P

BLOCK = 256
AO_DEV = 2
WIN = 5
ORBS = 1024
CHUNKS = 2
SPREAD_STEPS = 4
SPREAD_STEPS = 4
SPREAD_STEPS = 4
SPREAD_STEPS = 4
SPREAD_STEPS = 4
SPREAD_STEPS = 4
VMEM_LIMIT = 40 * 1024 * 1024
LEAD_FLOPS = 1 << 32


def with_halo(cells, sides, width):
    for axis, dim in sides:
        count = lax.axis_size(axis)
        ends = count - 1
        head = lax.slice_in_dim(cells, 0, width, axis=dim)
        tail = lax.slice_in_dim(cells, cells.shape[dim] - width, cells.shape[dim], axis=dim)
        cells = jnp.concatenate(
            [
                lax.ppermute(tail, axis, [(i, (i + 1) % count) for i in range(ends)]),
                cells,
                lax.ppermute(head, axis, [((i + 1) % count, i) for i in range(ends)]),
            ],
            axis=dim,
        )
    return cells


def general_body(integrals, coeffs, pair_blocks, pair_count, orbital_count):
    orb_local = coeffs.shape[1]
    aux_devices = lax.axis_size("aux")
    total_aux = integrals.shape[0] * aux_devices
    rim = WIN // 2 * BLOCK
    extended = with_halo(coeffs, (("ao", 0),), rim)
    ao_here = lax.axis_index("ao")
    orbital_ids = lax.axis_index("orb") * orb_local + jnp.arange(orb_local, dtype=jnp.int32)
    pieces = []
    for offset in range(AO_DEV):
        slab = integrals[:, offset * BLOCK : (offset + 1) * BLOCK, :]
        slot_range = extended[offset * BLOCK : offset * BLOCK + WIN * BLOCK]
        values = jnp.einsum("pml,li->pmi", slab, slot_range, preferred_element_type=jnp.float32)
        limit = orbital_count[ao_here * AO_DEV + offset]
        values = jnp.where((orbital_ids < limit)[None, None, :], values, 0.0)
        pieces.append(values.astype(jnp.bfloat16))
    transformed = jnp.stack(pieces)
    owners = lax.axis_size("ao")
    table = pair_blocks.reshape(owners, -1, 2)
    slots = table.shape[1]
    live = jnp.arange(slots, dtype=jnp.int32)[None, :] < pair_count[:, None]
    touched = live[:, :, None] & (table // AO_DEV == ao_here)
    wanted = jnp.max(jnp.where(touched, table % AO_DEV, 0), axis=(1, 2))
    outgoing = transformed[wanted]
    received = lax.all_to_all(outgoing, "ao", split_axis=0, concat_axis=0, tiled=True)
    owned = table[ao_here]
    factor = 1.0 / math.sqrt(total_aux * ORBS)
    weights = jnp.where(live[ao_here], factor, 0.0).astype(jnp.float32)
    left_source = owned[:, 0] // AO_DEV
    right_source = owned[:, 1] // AO_DEV
    right_factors = received[right_source]
    lefts = received[left_source]
    term = jnp.einsum("spmi,spni->msn", lefts, right_factors, preferred_element_type=jnp.float32)
    return lax.psum_scatter(
        term * weights[None, :, None], ("aux", "orb"), scatter_dimension=0, tiled=True
    )


EARLY_PAIRS = ((0, 1), (0, 2), (1, 2))
LATE_PAIRS = ((0, 3), (1, 3), (2, 3))
ALL_PAIRS = EARLY_PAIRS + LATE_PAIRS
GROUPS = 4
SWAP = [(0, 1), (1, 0)]
OUTSIDE = [(0, 1), (1, 0), (2, 3), (3, 2)]
INSIDE = [(1, 2), (2, 1)]

IN_HBM = pl.BlockSpec(memory_space=pltpu.HBM)
IN_VMEM = pl.BlockSpec(memory_space=pltpu.VMEM)


def like(shape, dtype):
    return jax.ShapeDtypeStruct(shape, dtype)


def local_call(kernel, name, out_shape, inputs, flops, scratch=(), out_spec=IN_VMEM):
    moved = sum(math.prod(o.shape) * o.dtype.itemsize for o in out_shape)
    return pl.pallas_call(
        kernel,
        out_shape=out_shape,
        in_specs=[IN_VMEM] * inputs,
        out_specs=[out_spec] * len(out_shape),
        scratch_shapes=list(scratch),
        compiler_params=pltpu.CompilerParams(vmem_limit_bytes=VMEM_LIMIT),
        cost_estimate=pl.CostEstimate(flops=flops, bytes_accessed=2 * moved, transcendentals=0),
        name=name,
    )


def dot(a, b):
    return jnp.dot(a, b, preferred_element_type=jnp.float32)


def lead_kernel(out):
    out[...] = jnp.zeros_like(out)


def lead():
    return local_call(lead_kernel, "lead", [like((8, 128), jnp.int32)], 0, LEAD_FLOPS)()[0]


def scalar_at(values, index):
    ids = lax.broadcasted_iota(jnp.int32, values.shape, 1)
    return jnp.sum(jnp.where(ids == index, values, 0).astype(jnp.float32))


def tables_kernel(first, counts, table, wants):
    here, orb = lax.axis_index("ao"), lax.axis_index("orb")
    slots = table.shape[1] // GROUPS
    named = jnp.where(table[...] // AO_DEV == here, table[...] % AO_DEV, 0).astype(jnp.float32)
    owner = lax.broadcasted_iota(jnp.int32, table.shape, 1) // slots
    rows = [jnp.max(jnp.where(owner == here ^ s, named, 0.0)) for s in range(GROUPS)]
    for offset in range(AO_DEV):
        count = scalar_at(counts[...], here * AO_DEV + offset)
        rows.append(count - (orb * (ORBS // 2)).astype(jnp.float32))
    row = lax.broadcasted_iota(jnp.int32, wants.shape, 0)
    out = first[0, 0:1].astype(jnp.float32).reshape(1, 1) + jnp.zeros(wants.shape, jnp.float32)
    for k, value in enumerate(rows):
        out = jnp.where(row == k, value, out)
    wants[...] = out.astype(jnp.int32)


def tables(first, counts, table, width):
    return local_call(
        tables_kernel, "tables", [like((8, width), jnp.int32)], 3, table.size
    )(first, counts.reshape(1, -1), table)[0]


def transform_kernel(start, wants, integrals, own, outer, inner, *outs):
    mid = AO_DEV * BLOCK

    def blocks(prev, following):
        ids = start + lax.broadcasted_iota(jnp.int32, (BLOCK, own.shape[1]), 1)
        for p in range(integrals.shape[0]):
            both = []
            for offset in range(AO_DEV):
                low = mid - offset * BLOCK
                slab = integrals[p, offset * BLOCK : (offset + 1) * BLOCK, :]
                values = dot(slab[:, low : low + mid], own[...])
                values += dot(slab[:, :low], prev[offset * BLOCK :, :])
                values += dot(slab[:, low + mid :], following[: (offset + 1) * BLOCK, :])
                live = ids < wants[GROUPS + offset : GROUPS + offset + 1, :]
                both.append(jnp.where(live, values, 0.0))
            for s, out in enumerate(outs):
                out[p] = jnp.where(wants[s : s + 1, :] == 0, *both).astype(jnp.bfloat16)

    odd = lax.axis_index("ao") & 1
    pl.when(odd == 0)(lambda: blocks(inner, outer))
    pl.when(odd == 1)(lambda: blocks(outer, inner))


def shared_kernel(start, wants, integrals, own, outer, inner, swapped, *refs):
    *outs, whole = refs
    aux = lax.axis_index("aux")
    width = inner.shape[1]
    whole[:, pl.ds(pl.multiple_of(aux * width, width), width)] = inner[...]
    whole[:, pl.ds(pl.multiple_of((1 - aux) * width, width), width)] = swapped[...]
    transform_kernel(start, wants, integrals, own, outer, whole, *outs)


def shared_transform(start, wants, integrals, own, outer, inner, swapped):
    shape = (integrals.shape[0], BLOCK, own.shape[1])
    return local_call(
        functools.partial(shared_kernel, start),
        "transform",
        [like(shape, jnp.bfloat16)] * GROUPS,
        6,
        2 * AO_DEV * math.prod(shape) * integrals.shape[2],
        [pltpu.VMEM(own.shape, jnp.bfloat16)],
    )(wants, integrals, own, outer, inner, swapped)


def transform(start, wants, integrals, own, outer, inner):
    shape = (integrals.shape[0], BLOCK, own.shape[1])
    return local_call(
        functools.partial(transform_kernel, start),
        "transform",
        [like(shape, jnp.bfloat16)] * GROUPS,
        5,
        2 * AO_DEV * math.prod(shape) * integrals.shape[2],
    )(wants, integrals, own, outer, inner)


def form_pairs(pairs, blocks, grams, before=None):
    here = lax.axis_index("ao")
    slices = [[(ref, p) for ref in block for p in range(ref.shape[0])] for block in blocks]

    def product(left, right):
        total = None
        for (a, i), (b, j) in zip(slices[left], slices[right]):
            part = lax.dot_general(
                a[i], b[j], (((1,), (1,)), ((), ())), preferred_element_type=jnp.float32
            )
            total = part if total is None else total + part
        return total.reshape(grams.shape[1:])

    def formed(k, left, right):
        gram = product(left, right)
        return gram if before is None else gram + before[k]

    for bit in (0, 1):
        mine = [(k, a, b) for k, (a, b) in enumerate(pairs) if (a ^ b) >> 1 == bit]
        upper = (here >> bit) & 1

        @pl.when(upper == 0)
        def _(mine=mine):
            for k, a, b in mine:
                grams[k] = formed(k, a, b)

        @pl.when(upper == 1)
        def _(mine=mine):
            for k, a, b in mine:
                grams[k] = formed(k, b, a)


def early_kernel(live, table, *refs):
    used = 3 * CHUNKS
    own, middle, next_to = [refs[i : i + CHUNKS] for i in range(0, used, CHUNKS)]
    blocks = own, next_to, middle
    near, far, place, grams = refs[used:]
    here, aux, orb = (lax.axis_index(axis) for axis in ("ao", "aux", "orb"))
    slots, width = place.shape
    slot = lax.broadcasted_iota(jnp.int32, (slots, table.shape[1]), 0)
    column = lax.broadcasted_iota(jnp.int32, (slots, table.shape[1]), 1)
    shown = column == here * slots + slot
    sides = []
    for side in (0, 1):
        group = (table[side : side + 1, :] // AO_DEV).astype(jnp.float32)
        group = jnp.sum(jnp.where(shown, group, 0.0), axis=1, keepdims=True)
        sides.append(group.astype(jnp.int32) ^ here)
    low, high = jnp.minimum(*sides), jnp.maximum(*sides)
    index = jnp.where(high == 3, low + 3, jnp.where(high == 2, low + 1, 0))
    slot = lax.broadcasted_iota(jnp.int32, (slots, width), 0)
    count = scalar_at(live[...], here).astype(jnp.int32)
    place[...] = jnp.where(slot < count, index, len(ALL_PAIRS))
    form_pairs(EARLY_PAIRS, blocks, grams)
    for k in range(len(EARLY_PAIRS)):
        for core in (0, 1):
            near[core, k] = grams[k, 2 * aux + (orb ^ core)]
            far[core, k] = grams[k, 2 * (1 - aux) + (orb ^ core)].astype(jnp.bfloat16)


def begin_kernel(own, middle, next_to, last, grams):
    form_pairs(LATE_PAIRS, ([own], [next_to], [middle], [last]), grams)


def late_kernel(own, middle, next_to, last, before, *refs):
    keep, give, grams = refs
    blocks = [own], [next_to], [middle], [last]
    aux, orb = lax.axis_index("aux"), lax.axis_index("orb")
    form_pairs(LATE_PAIRS, blocks, grams, before)
    for k in range(len(LATE_PAIRS)):
        for chip in (0, 1):
            row = 2 * (aux ^ chip)
            keep[chip, k] = grams[k, row + orb]
            give[chip, k] = grams[k, row + 1 - orb]


def pair_flops(pairs, blocks):
    return 2 * len(pairs) * BLOCK * CHUNKS * blocks[0][0].size


def quarters(pairs):
    rows = BLOCK // 4
    return (2, len(pairs), rows, BLOCK), pltpu.VMEM((len(pairs), 4, rows, BLOCK), jnp.float32)


def early_pairs(live, table, blocks):
    shape, grams = quarters(EARLY_PAIRS)
    return local_call(
        early_kernel,
        "early_pairs",
        [
            like(shape, jnp.float32),
            like(shape, jnp.bfloat16),
            like((table.shape[1] // GROUPS, BLOCK), jnp.int32),
        ],
        2 + 3 * CHUNKS,
        pair_flops(EARLY_PAIRS, blocks),
        [grams],
    )(live.reshape(1, -1), table, *blocks[0], *blocks[2], *blocks[1])


def late_pairs(blocks):
    shape, grams = quarters(LATE_PAIRS)
    own, next_to, middle, last = blocks
    begun = local_call(
        begin_kernel,
        "begin_pairs",
        [like(grams.shape, jnp.float32)],
        GROUPS,
        pair_flops(LATE_PAIRS, blocks) // CHUNKS,
    )(own[0], middle[0], next_to[0], last[0])
    return local_call(
        late_kernel,
        "late_pairs",
        [like(shape, jnp.float32)] * 2,
        GROUPS + 1,
        pair_flops(LATE_PAIRS, blocks) // CHUNKS,
        [grams],
    )(own[1], middle[1], next_to[1], last[1], *begun)


def spread_kernel(factor, place, near0, far0, got0, near1, got1, far1, out, sums, rows, sems):
    early = near0.shape[1]
    sums[:early] = (near0[0] + far0[0].astype(jnp.float32) + got0[...]) * factor
    sums[early:] = (near1[0] + got1[0] + far1[...].astype(jnp.float32)) * factor
    total, slots, width = out.shape
    masks = [place[...] == k for k in range(sums.shape[0])]

    def one(m, carry):
        row = jnp.zeros((slots, width), jnp.float32)
        for k, mask in enumerate(masks):
            values = jnp.broadcast_to(sums[k, pl.ds(m, 1), :], (slots, width))
            row = jnp.where(mask, values, row)
        rows[m] = row
        return carry

    step = total // SPREAD_STEPS
    copies = []
    for i in range(SPREAD_STEPS):
        lax.fori_loop(i * step, (i + 1) * step, one, 0, unroll=8)
        part = pl.ds(i * step, step)
        copies.append(pltpu.make_async_copy(rows.at[part], out.at[part], sems.at[i]))
        copies[-1].start()
    for copy in copies:
        copy.wait()


def spread(factor, place, *parts):
    rows = BLOCK // 4
    shape = (rows, place.shape[0], BLOCK)
    return local_call(
        functools.partial(spread_kernel, factor),
        "spread",
        [like(shape, jnp.float32)],
        1 + len(parts),
        6 * math.prod(shape),
        [
            pltpu.VMEM((len(ALL_PAIRS), rows, BLOCK), jnp.float32),
            pltpu.VMEM(shape, jnp.float32),
            pltpu.SemaphoreType.DMA((SPREAD_STEPS,)),
        ],
        IN_HBM,
    )(place, *parts)[0]


def six_pair_body(integrals, coeffs, pair_blocks, pair_count, orbital_count):
    width = coeffs.shape[1] // CHUNKS
    total_aux = integrals.shape[0] * lax.axis_size("aux")
    table = pair_blocks.T

    half = width // 2
    parts = [lax.slice_in_dim(coeffs, 0, width, axis=1)]
    first, rest = lax.optimization_barrier((lead(), coeffs))
    parts.append(lax.slice_in_dim(rest, width, 2 * width, axis=1))
    mine = lax.dynamic_slice_in_dim(rest, width + lax.axis_index("aux") * half, half, axis=1)
    inner = [lax.ppermute(part, "ao", INSIDE) for part in (parts[0], mine)]
    outer = [lax.ppermute(part, "ao", OUTSIDE) for part in parts]
    wants = tables(first, orbital_count, table, width)

    pieces = list(transform(0, wants, integrals, parts[0], outer[0], inner[0]))
    blocks = [[piece] for piece in pieces]
    inner[1], blocks[0][0] = lax.optimization_barrier((inner[1], blocks[0][0]))
    swapped = lax.ppermute(inner[1], "aux", SWAP)
    pieces = shared_transform(
        width, wants, integrals, parts[1], outer[1], inner[1], swapped
    )
    for block, piece in zip(blocks, pieces):
        block.append(piece)

    def fetch(s):
        swap = [(j, j ^ s) for j in range(GROUPS)]
        return [lax.ppermute(piece, "ao", swap) for piece in blocks[s]]

    middle = fetch(2)
    got = [blocks[0], fetch(1), middle]
    near0, across0, place = early_pairs(pair_count, table, got)
    far0 = lax.ppermute(across0, "aux", SWAP)
    got.append(fetch(3))
    near1, give1 = late_pairs(got)
    got1 = lax.ppermute(give1, "orb", SWAP)
    far1 = lax.ppermute((near1[1] + got1[1]).astype(jnp.bfloat16), "aux", SWAP)
    got0 = lax.ppermute(near0[1] + far0[1].astype(jnp.float32), "orb", SWAP)
    factor = 1.0 / math.sqrt(total_aux * ORBS)
    return spread(factor, place, near0, far0, got0, near1, got1, far1)


def solution(mesh):
    sizes = dict(mesh.shape)
    body = general_body
    if sizes["ao"] == 4 and sizes["aux"] == 2 and sizes["orb"] == 2:
        body = six_pair_body
    return jax.shard_map(
        body,
        mesh=mesh,
        in_specs=(
            P(("grp", "aux"), "ao", None),
            P(("grp", "ao"), "orb"),
            P("grp", None),
            P("grp"),
            P("grp"),
        ),
        out_specs=P(("aux", "orb"), ("grp", "ao"), None),
        check_vma=False,
    )
```

```python
import functools
import math

import jax
import jax.numpy as jnp
from jax import lax
from jax.experimental import pallas as pl
from jax.experimental.pallas import tpu as pltpu
from jax.sharding import PartitionSpec as P

BLOCK = 256
AO_DEV = 2
WIN = 5
ORBS = 1024
CHUNKS = 2
SPREAD_STEPS = 4
SPREAD_STEPS = 4
SPREAD_STEPS = 4
SPREAD_STEPS = 4
SPREAD_STEPS = 4
SPREAD_STEPS = 4
VMEM_LIMIT = 40 * 1024 * 1024
LEAD_FLOPS = 1 << 32
CUT_LIMIT = 53 * 1024 * 1024 + 256 * 1024


def with_halo(cells, sides, width):
    for axis, dim in sides:
        count = lax.axis_size(axis)
        ends = count - 1
        head = lax.slice_in_dim(cells, 0, width, axis=dim)
        tail = lax.slice_in_dim(cells, cells.shape[dim] - width, cells.shape[dim], axis=dim)
        cells = jnp.concatenate(
            [
                lax.ppermute(tail, axis, [(i, (i + 1) % count) for i in range(ends)]),
                cells,
                lax.ppermute(head, axis, [((i + 1) % count, i) for i in range(ends)]),
            ],
            axis=dim,
        )
    return cells


def general_body(integrals, coeffs, pair_blocks, pair_count, orbital_count):
    orb_local = coeffs.shape[1]
    aux_devices = lax.axis_size("aux")
    total_aux = integrals.shape[0] * aux_devices
    rim = WIN // 2 * BLOCK
    extended = with_halo(coeffs, (("ao", 0),), rim)
    ao_here = lax.axis_index("ao")
    orbital_ids = lax.axis_index("orb") * orb_local + jnp.arange(orb_local, dtype=jnp.int32)
    pieces = []
    for offset in range(AO_DEV):
        slab = integrals[:, offset * BLOCK : (offset + 1) * BLOCK, :]
        slot_range = extended[offset * BLOCK : offset * BLOCK + WIN * BLOCK]
        values = jnp.einsum("pml,li->pmi", slab, slot_range, preferred_element_type=jnp.float32)
        limit = orbital_count[ao_here * AO_DEV + offset]
        values = jnp.where((orbital_ids < limit)[None, None, :], values, 0.0)
        pieces.append(values.astype(jnp.bfloat16))
    transformed = jnp.stack(pieces)
    owners = lax.axis_size("ao")
    table = pair_blocks.reshape(owners, -1, 2)
    slots = table.shape[1]
    live = jnp.arange(slots, dtype=jnp.int32)[None, :] < pair_count[:, None]
    touched = live[:, :, None] & (table // AO_DEV == ao_here)
    wanted = jnp.max(jnp.where(touched, table % AO_DEV, 0), axis=(1, 2))
    outgoing = transformed[wanted]
    received = lax.all_to_all(outgoing, "ao", split_axis=0, concat_axis=0, tiled=True)
    owned = table[ao_here]
    factor = 1.0 / math.sqrt(total_aux * ORBS)
    weights = jnp.where(live[ao_here], factor, 0.0).astype(jnp.float32)
    left_source = owned[:, 0] // AO_DEV
    right_source = owned[:, 1] // AO_DEV
    right_factors = received[right_source]
    lefts = received[left_source]
    term = jnp.einsum("spmi,spni->msn", lefts, right_factors, preferred_element_type=jnp.float32)
    return lax.psum_scatter(
        term * weights[None, :, None], ("aux", "orb"), scatter_dimension=0, tiled=True
    )


EARLY_PAIRS = ((0, 1), (0, 2), (1, 2))
LATE_PAIRS = ((0, 3), (1, 3), (2, 3))
ALL_PAIRS = EARLY_PAIRS + LATE_PAIRS
GROUPS = 4
SWAP = [(0, 1), (1, 0)]
OUTSIDE = [(0, 1), (1, 0), (2, 3), (3, 2)]
INSIDE = [(1, 2), (2, 1)]

IN_HBM = pl.BlockSpec(memory_space=pltpu.HBM)
IN_VMEM = pl.BlockSpec(memory_space=pltpu.VMEM)


def like(shape, dtype):
    return jax.ShapeDtypeStruct(shape, dtype)


def local_call(kernel, name, out_shape, inputs, flops, scratch=(), out_spec=IN_VMEM):
    moved = sum(math.prod(o.shape) * o.dtype.itemsize for o in out_shape)
    return pl.pallas_call(
        kernel,
        out_shape=out_shape,
        in_specs=[IN_VMEM] * inputs,
        out_specs=[out_spec] * len(out_shape),
        scratch_shapes=list(scratch),
        compiler_params=pltpu.CompilerParams(vmem_limit_bytes=VMEM_LIMIT),
        cost_estimate=pl.CostEstimate(flops=flops, bytes_accessed=2 * moved, transcendentals=0),
        name=name,
    )


def dot(a, b):
    return jnp.dot(a, b, preferred_element_type=jnp.float32)


def cut_kernel(coeffs, direct, sem):
    copy = pltpu.make_async_copy(coeffs.at[:, pl.ds(0, direct.shape[1])], direct, sem)
    copy.start()
    copy.wait()


def cut(coeffs):
    rows, columns = coeffs.shape
    return pl.pallas_call(
        cut_kernel,
        out_shape=like((rows, columns // CHUNKS), coeffs.dtype),
        in_specs=[IN_HBM],
        out_specs=IN_VMEM,
        scratch_shapes=[pltpu.SemaphoreType.DMA],
        compiler_params=pltpu.CompilerParams(vmem_limit_bytes=CUT_LIMIT),
        cost_estimate=pl.CostEstimate(flops=LEAD_FLOPS, bytes_accessed=0, transcendentals=0),
        name="cut",
    )(coeffs)


def rest_kernel(coeffs, first, shared, mine):
    width, half = shared.shape[1], mine.shape[1]
    shared[...] = coeffs[:, width:]
    start = pl.multiple_of(width + lax.axis_index("aux") * half, half)
    mine[...] = coeffs[:, pl.ds(start, half)]


def cut_rest(coeffs, first):
    rows, columns = coeffs.shape
    width = columns // CHUNKS
    return local_call(
        rest_kernel, "cut_rest", [like((rows, n), coeffs.dtype) for n in (width, width // 2)], 2, LEAD_FLOPS
    )(coeffs, first)


def scalar_at(values, index):
    ids = lax.broadcasted_iota(jnp.int32, values.shape, 1)
    return jnp.sum(jnp.where(ids == index, values, 0).astype(jnp.float32))


def tables_kernel(counts, table, wants):
    here, orb = lax.axis_index("ao"), lax.axis_index("orb")
    slots = table.shape[1] // GROUPS
    named = jnp.where(table[...] // AO_DEV == here, table[...] % AO_DEV, 0).astype(jnp.float32)
    owner = lax.broadcasted_iota(jnp.int32, table.shape, 1) // slots
    rows = [jnp.max(jnp.where(owner == here ^ s, named, 0.0)) for s in range(GROUPS)]
    for offset in range(AO_DEV):
        count = scalar_at(counts[...], here * AO_DEV + offset)
        rows.append(count - (orb * (ORBS // 2)).astype(jnp.float32))
    row = lax.broadcasted_iota(jnp.int32, wants.shape, 0)
    out = jnp.zeros(wants.shape, jnp.float32)
    for k, value in enumerate(rows):
        out = jnp.where(row == k, value, out)
    wants[...] = out.astype(jnp.int32)


def tables(counts, table, width):
    return local_call(
        tables_kernel, "tables", [like((8, width), jnp.int32)], 2, LEAD_FLOPS
    )(counts.reshape(1, -1), table)[0]


def transform_kernel(start, wants, integrals, own, outer, inner, *outs):
    mid = AO_DEV * BLOCK

    def blocks(prev, following):
        ids = start + lax.broadcasted_iota(jnp.int32, (BLOCK, own.shape[1]), 1)
        for p in range(integrals.shape[0]):
            both = []
            for offset in range(AO_DEV):
                low = mid - offset * BLOCK
                slab = integrals[p, offset * BLOCK : (offset + 1) * BLOCK, :]
                values = dot(slab[:, low : low + mid], own[...])
                values += dot(slab[:, :low], prev[offset * BLOCK :, :])
                values += dot(slab[:, low + mid :], following[: (offset + 1) * BLOCK, :])
                live = ids < wants[GROUPS + offset : GROUPS + offset + 1, :]
                both.append(jnp.where(live, values, 0.0))
            for s, out in enumerate(outs):
                out[p] = jnp.where(wants[s : s + 1, :] == 0, *both).astype(jnp.bfloat16)

    odd = lax.axis_index("ao") & 1
    pl.when(odd == 0)(lambda: blocks(inner, outer))
    pl.when(odd == 1)(lambda: blocks(outer, inner))


def shared_kernel(start, wants, integrals, own, outer, inner, swapped, *refs):
    *outs, whole = refs
    aux = lax.axis_index("aux")
    width = inner.shape[1]
    whole[:, pl.ds(pl.multiple_of(aux * width, width), width)] = inner[...]
    whole[:, pl.ds(pl.multiple_of((1 - aux) * width, width), width)] = swapped[...]
    transform_kernel(start, wants, integrals, own, outer, whole, *outs)


def shared_transform(start, wants, integrals, own, outer, inner, swapped):
    shape = (integrals.shape[0], BLOCK, own.shape[1])
    return local_call(
        functools.partial(shared_kernel, start),
        "transform",
        [like(shape, jnp.bfloat16)] * GROUPS,
        6,
        2 * AO_DEV * math.prod(shape) * integrals.shape[2],
        [pltpu.VMEM(own.shape, jnp.bfloat16)],
    )(wants, integrals, own, outer, inner, swapped)


def transform(start, wants, integrals, own, outer, inner):
    shape = (integrals.shape[0], BLOCK, own.shape[1])
    return local_call(
        functools.partial(transform_kernel, start),
        "transform",
        [like(shape, jnp.bfloat16)] * GROUPS,
        5,
        2 * AO_DEV * math.prod(shape) * integrals.shape[2],
    )(wants, integrals, own, outer, inner)


def form_pairs(pairs, blocks, grams, before=None):
    here = lax.axis_index("ao")
    slices = [[(ref, p) for ref in block for p in range(ref.shape[0])] for block in blocks]

    def product(left, right):
        total = None
        for (a, i), (b, j) in zip(slices[left], slices[right]):
            part = lax.dot_general(
                a[i], b[j], (((1,), (1,)), ((), ())), preferred_element_type=jnp.float32
            )
            total = part if total is None else total + part
        return total.reshape(grams.shape[1:])

    def formed(k, left, right):
        gram = product(left, right)
        return gram if before is None else gram + before[k]

    for bit in (0, 1):
        mine = [(k, a, b) for k, (a, b) in enumerate(pairs) if (a ^ b) >> 1 == bit]
        upper = (here >> bit) & 1

        @pl.when(upper == 0)
        def _(mine=mine):
            for k, a, b in mine:
                grams[k] = formed(k, a, b)

        @pl.when(upper == 1)
        def _(mine=mine):
            for k, a, b in mine:
                grams[k] = formed(k, b, a)


def early_kernel(live, table, *refs):
    used = 3 * CHUNKS
    own, middle, next_to = [refs[i : i + CHUNKS] for i in range(0, used, CHUNKS)]
    blocks = own, next_to, middle
    near, far, place, grams = refs[used:]
    here, aux, orb = (lax.axis_index(axis) for axis in ("ao", "aux", "orb"))
    slots, width = place.shape
    slot = lax.broadcasted_iota(jnp.int32, (slots, table.shape[1]), 0)
    column = lax.broadcasted_iota(jnp.int32, (slots, table.shape[1]), 1)
    shown = column == here * slots + slot
    sides = []
    for side in (0, 1):
        group = (table[side : side + 1, :] // AO_DEV).astype(jnp.float32)
        group = jnp.sum(jnp.where(shown, group, 0.0), axis=1, keepdims=True)
        sides.append(group.astype(jnp.int32) ^ here)
    low, high = jnp.minimum(*sides), jnp.maximum(*sides)
    index = jnp.where(high == 3, low + 3, jnp.where(high == 2, low + 1, 0))
    slot = lax.broadcasted_iota(jnp.int32, (slots, width), 0)
    count = scalar_at(live[...], here).astype(jnp.int32)
    place[...] = jnp.where(slot < count, index, len(ALL_PAIRS))
    form_pairs(EARLY_PAIRS, blocks, grams)
    for k in range(len(EARLY_PAIRS)):
        for core in (0, 1):
            near[core, k] = grams[k, 2 * aux + (orb ^ core)]
            far[core, k] = grams[k, 2 * (1 - aux) + (orb ^ core)].astype(jnp.bfloat16)


def begin_kernel(own, middle, next_to, last, grams):
    form_pairs(LATE_PAIRS, ([own], [next_to], [middle], [last]), grams)


def late_kernel(own, middle, next_to, last, before, *refs):
    keep, give, grams = refs
    blocks = [own], [next_to], [middle], [last]
    aux, orb = lax.axis_index("aux"), lax.axis_index("orb")
    form_pairs(LATE_PAIRS, blocks, grams, before)
    for k in range(len(LATE_PAIRS)):
        for chip in (0, 1):
            row = 2 * (aux ^ chip)
            keep[chip, k] = grams[k, row + orb]
            give[chip, k] = grams[k, row + 1 - orb]


def pair_flops(pairs, blocks):
    return 2 * len(pairs) * BLOCK * CHUNKS * blocks[0][0].size


def quarters(pairs):
    rows = BLOCK // 4
    return (2, len(pairs), rows, BLOCK), pltpu.VMEM((len(pairs), 4, rows, BLOCK), jnp.float32)


def early_pairs(live, table, blocks):
    shape, grams = quarters(EARLY_PAIRS)
    return local_call(
        early_kernel,
        "early_pairs",
        [
            like(shape, jnp.float32),
            like(shape, jnp.bfloat16),
            like((table.shape[1] // GROUPS, BLOCK), jnp.int32),
        ],
        2 + 3 * CHUNKS,
        pair_flops(EARLY_PAIRS, blocks),
        [grams],
    )(live.reshape(1, -1), table, *blocks[0], *blocks[2], *blocks[1])


def late_pairs(blocks):
    shape, grams = quarters(LATE_PAIRS)
    own, next_to, middle, last = blocks
    begun = local_call(
        begin_kernel,
        "begin_pairs",
        [like(grams.shape, jnp.float32)],
        GROUPS,
        pair_flops(LATE_PAIRS, blocks) // CHUNKS,
    )(own[0], middle[0], next_to[0], last[0])
    return local_call(
        late_kernel,
        "late_pairs",
        [like(shape, jnp.float32)] * 2,
        GROUPS + 1,
        pair_flops(LATE_PAIRS, blocks) // CHUNKS,
        [grams],
    )(own[1], middle[1], next_to[1], last[1], *begun)


def spread_kernel(factor, place, near0, far0, got0, near1, got1, far1, out, sums, rows, sems):
    early = near0.shape[1]
    sums[:early] = (near0[0] + far0[0].astype(jnp.float32) + got0[...]) * factor
    sums[early:] = (near1[0] + got1[0] + far1[...].astype(jnp.float32)) * factor
    total, slots, width = out.shape
    masks = [place[...] == k for k in range(sums.shape[0])]

    def one(m, carry):
        row = jnp.zeros((slots, width), jnp.float32)
        for k, mask in enumerate(masks):
            values = jnp.broadcast_to(sums[k, pl.ds(m, 1), :], (slots, width))
            row = jnp.where(mask, values, row)
        rows[m] = row
        return carry

    step = total // SPREAD_STEPS
    copies = []
    for i in range(SPREAD_STEPS):
        lax.fori_loop(i * step, (i + 1) * step, one, 0, unroll=8)
        part = pl.ds(i * step, step)
        copies.append(pltpu.make_async_copy(rows.at[part], out.at[part], sems.at[i]))
        copies[-1].start()
    for copy in copies:
        copy.wait()


def spread(factor, place, *parts):
    rows = BLOCK // 4
    shape = (rows, place.shape[0], BLOCK)
    return local_call(
        functools.partial(spread_kernel, factor),
        "spread",
        [like(shape, jnp.float32)],
        1 + len(parts),
        6 * math.prod(shape),
        [
            pltpu.VMEM((len(ALL_PAIRS), rows, BLOCK), jnp.float32),
            pltpu.VMEM(shape, jnp.float32),
            pltpu.SemaphoreType.DMA((SPREAD_STEPS,)),
        ],
        IN_HBM,
    )(place, *parts)[0]


def six_pair_body(integrals, coeffs, pair_blocks, pair_count, orbital_count):
    width = coeffs.shape[1] // CHUNKS
    total_aux = integrals.shape[0] * lax.axis_size("aux")
    table = pair_blocks.T

    direct = cut(coeffs)
    shared, mine = cut_rest(coeffs, direct)
    parts = [direct, shared]
    inner = [lax.ppermute(part, "ao", INSIDE) for part in (parts[0], mine)]
    outer = [lax.ppermute(part, "ao", OUTSIDE) for part in parts]
    wants = tables(orbital_count, table, width)

    pieces = list(transform(0, wants, integrals, parts[0], outer[0], inner[0]))
    blocks = [[piece] for piece in pieces]
    inner[1], blocks[0][0] = lax.optimization_barrier((inner[1], blocks[0][0]))
    swapped = lax.ppermute(inner[1], "aux", SWAP)
    pieces = shared_transform(
        width, wants, integrals, parts[1], outer[1], inner[1], swapped
    )
    for block, piece in zip(blocks, pieces):
        block.append(piece)

    def fetch(s):
        swap = [(j, j ^ s) for j in range(GROUPS)]
        return [lax.ppermute(piece, "ao", swap) for piece in blocks[s]]

    middle = fetch(2)
    got = [blocks[0], fetch(1), middle]
    near0, across0, place = early_pairs(pair_count, table, got)
    far0 = lax.ppermute(across0, "aux", SWAP)
    got.append(fetch(3))
    near1, give1 = late_pairs(got)
    got1 = lax.ppermute(give1, "orb", SWAP)
    far1 = lax.ppermute((near1[1] + got1[1]).astype(jnp.bfloat16), "aux", SWAP)
    got0 = lax.ppermute(near0[1] + far0[1].astype(jnp.float32), "orb", SWAP)
    factor = 1.0 / math.sqrt(total_aux * ORBS)
    return spread(factor, place, near0, far0, got0, near1, got1, far1)


def solution(mesh):
    sizes = dict(mesh.shape)
    body = general_body
    if sizes["ao"] == 4 and sizes["aux"] == 2 and sizes["orb"] == 2:
        body = six_pair_body
    return jax.shard_map(
        body,
        mesh=mesh,
        in_specs=(
            P(("grp", "aux"), "ao", None),
            P(("grp", "ao"), "orb"),
            P("grp", None),
            P("grp"),
            P("grp"),
        ),
        out_specs=P(("aux", "orb"), ("grp", "ao"), None),
        check_vma=False,
    )
```

```python
import functools
import math

import jax
import jax.numpy as jnp
from jax import lax
from jax.experimental import pallas as pl
from jax.experimental.pallas import tpu as pltpu
from jax.sharding import PartitionSpec as P

BLOCK = 256
AO_DEV = 2
WIN = 5
ORBS = 1024
CHUNKS = 2
SPREAD_STEPS = 4
SPREAD_STEPS = 4
SPREAD_STEPS = 4
SPREAD_STEPS = 4
SPREAD_STEPS = 4
SPREAD_STEPS = 4
VMEM_LIMIT = 40 * 1024 * 1024
LEAD_FLOPS = 1 << 32
LATE_WEIGHT = 10
CUT_LIMIT = 53 * 1024 * 1024 + 256 * 1024


def with_halo(cells, sides, width):
    for axis, dim in sides:
        count = lax.axis_size(axis)
        ends = count - 1
        head = lax.slice_in_dim(cells, 0, width, axis=dim)
        tail = lax.slice_in_dim(cells, cells.shape[dim] - width, cells.shape[dim], axis=dim)
        cells = jnp.concatenate(
            [
                lax.ppermute(tail, axis, [(i, (i + 1) % count) for i in range(ends)]),
                cells,
                lax.ppermute(head, axis, [((i + 1) % count, i) for i in range(ends)]),
            ],
            axis=dim,
        )
    return cells


def general_body(integrals, coeffs, pair_blocks, pair_count, orbital_count):
    orb_local = coeffs.shape[1]
    aux_devices = lax.axis_size("aux")
    total_aux = integrals.shape[0] * aux_devices
    rim = WIN // 2 * BLOCK
    extended = with_halo(coeffs, (("ao", 0),), rim)
    ao_here = lax.axis_index("ao")
    orbital_ids = lax.axis_index("orb") * orb_local + jnp.arange(orb_local, dtype=jnp.int32)
    pieces = []
    for offset in range(AO_DEV):
        slab = integrals[:, offset * BLOCK : (offset + 1) * BLOCK, :]
        slot_range = extended[offset * BLOCK : offset * BLOCK + WIN * BLOCK]
        values = jnp.einsum("pml,li->pmi", slab, slot_range, preferred_element_type=jnp.float32)
        limit = orbital_count[ao_here * AO_DEV + offset]
        values = jnp.where((orbital_ids < limit)[None, None, :], values, 0.0)
        pieces.append(values.astype(jnp.bfloat16))
    transformed = jnp.stack(pieces)
    owners = lax.axis_size("ao")
    table = pair_blocks.reshape(owners, -1, 2)
    slots = table.shape[1]
    live = jnp.arange(slots, dtype=jnp.int32)[None, :] < pair_count[:, None]
    touched = live[:, :, None] & (table // AO_DEV == ao_here)
    wanted = jnp.max(jnp.where(touched, table % AO_DEV, 0), axis=(1, 2))
    outgoing = transformed[wanted]
    received = lax.all_to_all(outgoing, "ao", split_axis=0, concat_axis=0, tiled=True)
    owned = table[ao_here]
    factor = 1.0 / math.sqrt(total_aux * ORBS)
    weights = jnp.where(live[ao_here], factor, 0.0).astype(jnp.float32)
    left_source = owned[:, 0] // AO_DEV
    right_source = owned[:, 1] // AO_DEV
    right_factors = received[right_source]
    lefts = received[left_source]
    term = jnp.einsum("spmi,spni->msn", lefts, right_factors, preferred_element_type=jnp.float32)
    return lax.psum_scatter(
        term * weights[None, :, None], ("aux", "orb"), scatter_dimension=0, tiled=True
    )


EARLY_PAIRS = ((0, 1), (0, 2), (1, 2))
LATE_PAIRS = ((0, 3), (1, 3), (2, 3))
ALL_PAIRS = EARLY_PAIRS + LATE_PAIRS
GROUPS = 4
SWAP = [(0, 1), (1, 0)]
OUTSIDE = [(0, 1), (1, 0), (2, 3), (3, 2)]
INSIDE = [(1, 2), (2, 1)]

IN_HBM = pl.BlockSpec(memory_space=pltpu.HBM)
IN_VMEM = pl.BlockSpec(memory_space=pltpu.VMEM)


def like(shape, dtype):
    return jax.ShapeDtypeStruct(shape, dtype)


def local_call(kernel, name, out_shape, inputs, flops, scratch=(), out_spec=IN_VMEM):
    moved = sum(math.prod(o.shape) * o.dtype.itemsize for o in out_shape)
    return pl.pallas_call(
        kernel,
        out_shape=out_shape,
        in_specs=[IN_VMEM] * inputs,
        out_specs=[out_spec] * len(out_shape),
        scratch_shapes=list(scratch),
        compiler_params=pltpu.CompilerParams(vmem_limit_bytes=VMEM_LIMIT),
        cost_estimate=pl.CostEstimate(flops=flops, bytes_accessed=2 * moved, transcendentals=0),
        name=name,
    )


def dot(a, b):
    return jnp.dot(a, b, preferred_element_type=jnp.float32)


def cut_kernel(coeffs, direct, sem):
    copy = pltpu.make_async_copy(coeffs.at[:, pl.ds(0, direct.shape[1])], direct, sem)
    copy.start()
    copy.wait()


def cut(coeffs):
    rows, columns = coeffs.shape
    return pl.pallas_call(
        cut_kernel,
        out_shape=like((rows, columns // CHUNKS), coeffs.dtype),
        in_specs=[IN_HBM],
        out_specs=IN_VMEM,
        scratch_shapes=[pltpu.SemaphoreType.DMA],
        compiler_params=pltpu.CompilerParams(vmem_limit_bytes=CUT_LIMIT),
        cost_estimate=pl.CostEstimate(flops=LEAD_FLOPS, bytes_accessed=0, transcendentals=0),
        name="cut",
    )(coeffs)


def rest_kernel(coeffs, first, shared, mine):
    width, half = shared.shape[1], mine.shape[1]
    shared[...] = coeffs[:, width:]
    start = pl.multiple_of(width + lax.axis_index("aux") * half, half)
    mine[...] = coeffs[:, pl.ds(start, half)]


def cut_rest(coeffs, first):
    rows, columns = coeffs.shape
    width = columns // CHUNKS
    return local_call(
        rest_kernel, "cut_rest", [like((rows, n), coeffs.dtype) for n in (width, width // 2)], 2, LEAD_FLOPS
    )(coeffs, first)


def scalar_at(values, index):
    ids = lax.broadcasted_iota(jnp.int32, values.shape, 1)
    return jnp.sum(jnp.where(ids == index, values, 0).astype(jnp.float32))


def tables_kernel(counts, table, wants):
    here, orb = lax.axis_index("ao"), lax.axis_index("orb")
    slots = table.shape[1] // GROUPS
    named = jnp.where(table[...] // AO_DEV == here, table[...] % AO_DEV, 0).astype(jnp.float32)
    owner = lax.broadcasted_iota(jnp.int32, table.shape, 1) // slots
    rows = [jnp.max(jnp.where(owner == here ^ s, named, 0.0)) for s in range(GROUPS)]
    for offset in range(AO_DEV):
        count = scalar_at(counts[...], here * AO_DEV + offset)
        rows.append(count - (orb * (ORBS // 2)).astype(jnp.float32))
    row = lax.broadcasted_iota(jnp.int32, wants.shape, 0)
    out = jnp.zeros(wants.shape, jnp.float32)
    for k, value in enumerate(rows):
        out = jnp.where(row == k, value, out)
    wants[...] = out.astype(jnp.int32)


def tables(counts, table, width):
    return local_call(
        tables_kernel, "tables", [like((8, width), jnp.int32)], 2, LEAD_FLOPS
    )(counts.reshape(1, -1), table)[0]


def transform_kernel(start, wants, integrals, own, outer, inner, *outs):
    mid = AO_DEV * BLOCK

    def blocks(prev, following):
        ids = start + lax.broadcasted_iota(jnp.int32, (BLOCK, own.shape[1]), 1)
        for p in range(integrals.shape[0]):
            both = []
            for offset in range(AO_DEV):
                low = mid - offset * BLOCK
                slab = integrals[p, offset * BLOCK : (offset + 1) * BLOCK, :]
                values = dot(slab[:, low : low + mid], own[...])
                values += dot(slab[:, :low], prev[offset * BLOCK :, :])
                values += dot(slab[:, low + mid :], following[: (offset + 1) * BLOCK, :])
                live = ids < wants[GROUPS + offset : GROUPS + offset + 1, :]
                both.append(jnp.where(live, values, 0.0))
            for s, out in enumerate(outs):
                out[p] = jnp.where(wants[s : s + 1, :] == 0, *both).astype(jnp.bfloat16)

    odd = lax.axis_index("ao") & 1
    pl.when(odd == 0)(lambda: blocks(inner, outer))
    pl.when(odd == 1)(lambda: blocks(outer, inner))


def shared_kernel(start, wants, integrals, own, outer, inner, swapped, *refs):
    *outs, whole = refs
    aux = lax.axis_index("aux")
    width = inner.shape[1]
    whole[:, pl.ds(pl.multiple_of(aux * width, width), width)] = inner[...]
    whole[:, pl.ds(pl.multiple_of((1 - aux) * width, width), width)] = swapped[...]
    transform_kernel(start, wants, integrals, own, outer, whole, *outs)


def shared_transform(start, wants, integrals, own, outer, inner, swapped):
    shape = (integrals.shape[0], BLOCK, own.shape[1])
    return local_call(
        functools.partial(shared_kernel, start),
        "transform",
        [like(shape, jnp.bfloat16)] * GROUPS,
        6,
        2 * AO_DEV * math.prod(shape) * integrals.shape[2],
        [pltpu.VMEM(own.shape, jnp.bfloat16)],
    )(wants, integrals, own, outer, inner, swapped)


def transform(start, wants, integrals, own, outer, inner):
    shape = (integrals.shape[0], BLOCK, own.shape[1])
    return local_call(
        functools.partial(transform_kernel, start),
        "transform",
        [like(shape, jnp.bfloat16)] * GROUPS,
        5,
        2 * AO_DEV * math.prod(shape) * integrals.shape[2],
    )(wants, integrals, own, outer, inner)


def form_pairs(pairs, blocks, grams, before=None):
    here = lax.axis_index("ao")
    slices = [[(ref, p) for ref in block for p in range(ref.shape[0])] for block in blocks]

    def product(left, right):
        total = None
        for (a, i), (b, j) in zip(slices[left], slices[right]):
            part = lax.dot_general(
                a[i], b[j], (((1,), (1,)), ((), ())), preferred_element_type=jnp.float32
            )
            total = part if total is None else total + part
        return total.reshape(grams.shape[1:])

    def formed(k, left, right):
        gram = product(left, right)
        return gram if before is None else gram + before[k]

    for bit in (0, 1):
        mine = [(k, a, b) for k, (a, b) in enumerate(pairs) if (a ^ b) >> 1 == bit]
        upper = (here >> bit) & 1

        @pl.when(upper == 0)
        def _(mine=mine):
            for k, a, b in mine:
                grams[k] = formed(k, a, b)

        @pl.when(upper == 1)
        def _(mine=mine):
            for k, a, b in mine:
                grams[k] = formed(k, b, a)


def early_kernel(live, table, *refs):
    used = 3 * CHUNKS
    own, middle, next_to = [refs[i : i + CHUNKS] for i in range(0, used, CHUNKS)]
    blocks = own, next_to, middle
    near, far, place, grams = refs[used:]
    here, aux, orb = (lax.axis_index(axis) for axis in ("ao", "aux", "orb"))
    slots, width = place.shape
    slot = lax.broadcasted_iota(jnp.int32, (slots, table.shape[1]), 0)
    column = lax.broadcasted_iota(jnp.int32, (slots, table.shape[1]), 1)
    shown = column == here * slots + slot
    sides = []
    for side in (0, 1):
        group = (table[side : side + 1, :] // AO_DEV).astype(jnp.float32)
        group = jnp.sum(jnp.where(shown, group, 0.0), axis=1, keepdims=True)
        sides.append(group.astype(jnp.int32) ^ here)
    low, high = jnp.minimum(*sides), jnp.maximum(*sides)
    index = jnp.where(high == 3, low + 3, jnp.where(high == 2, low + 1, 0))
    slot = lax.broadcasted_iota(jnp.int32, (slots, width), 0)
    count = scalar_at(live[...], here).astype(jnp.int32)
    place[...] = jnp.where(slot < count, index, len(ALL_PAIRS))
    form_pairs(EARLY_PAIRS, blocks, grams)
    for k in range(len(EARLY_PAIRS)):
        for core in (0, 1):
            near[core, k] = grams[k, 2 * aux + (orb ^ core)]
            far[core, k] = grams[k, 2 * (1 - aux) + (orb ^ core)].astype(jnp.bfloat16)


def begin_kernel(own, middle, next_to, last, grams):
    form_pairs(LATE_PAIRS, ([own], [next_to], [middle], [last]), grams)


def late_kernel(own, middle, next_to, last, before, *refs):
    keep, give, grams = refs
    blocks = [own], [next_to], [middle], [last]
    aux, orb = lax.axis_index("aux"), lax.axis_index("orb")
    form_pairs(LATE_PAIRS, blocks, grams, before)
    for k in range(len(LATE_PAIRS)):
        for chip in (0, 1):
            row = 2 * (aux ^ chip)
            keep[chip, k] = grams[k, row + orb]
            give[chip, k] = grams[k, row + 1 - orb].astype(jnp.bfloat16)


def pair_flops(pairs, blocks):
    return 2 * len(pairs) * BLOCK * CHUNKS * blocks[0][0].size


def quarters(pairs):
    rows = BLOCK // 4
    return (2, len(pairs), rows, BLOCK), pltpu.VMEM((len(pairs), 4, rows, BLOCK), jnp.float32)


def early_pairs(live, table, blocks):
    shape, grams = quarters(EARLY_PAIRS)
    return local_call(
        early_kernel,
        "early_pairs",
        [
            like(shape, jnp.float32),
            like(shape, jnp.bfloat16),
            like((table.shape[1] // GROUPS, BLOCK), jnp.int32),
        ],
        2 + 3 * CHUNKS,
        pair_flops(EARLY_PAIRS, blocks),
        [grams],
    )(live.reshape(1, -1), table, *blocks[0], *blocks[2], *blocks[1])


def late_pairs(blocks):
    shape, grams = quarters(LATE_PAIRS)
    own, next_to, middle, last = blocks
    begun = local_call(
        begin_kernel,
        "begin_pairs",
        [like(grams.shape, jnp.float32)],
        GROUPS,
        pair_flops(LATE_PAIRS, blocks) // CHUNKS,
    )(own[0], middle[0], next_to[0], last[0])
    return local_call(
        late_kernel,
        "late_pairs",
        [like(shape, jnp.float32), like(shape, jnp.bfloat16)],
        GROUPS + 1,
        LATE_WEIGHT * pair_flops(LATE_PAIRS, blocks) // CHUNKS,
        [grams],
    )(own[1], middle[1], next_to[1], last[1], *begun)


def spread_kernel(factor, place, near0, far0, got0, near1, got1, far1, out, sums, rows, sems):
    early = near0.shape[1]
    sums[:early] = (near0[0] + far0[0].astype(jnp.float32) + got0[...]) * factor
    sums[early:] = (near1[0] + got1[0].astype(jnp.float32) + far1[...].astype(jnp.float32)) * factor
    total, slots, width = out.shape
    masks = [place[...] == k for k in range(sums.shape[0])]

    def one(m, carry):
        row = jnp.zeros((slots, width), jnp.float32)
        for k, mask in enumerate(masks):
            values = jnp.broadcast_to(sums[k, pl.ds(m, 1), :], (slots, width))
            row = jnp.where(mask, values, row)
        rows[m] = row
        return carry

    step = total // SPREAD_STEPS
    copies = []
    for i in range(SPREAD_STEPS):
        lax.fori_loop(i * step, (i + 1) * step, one, 0, unroll=8)
        part = pl.ds(i * step, step)
        copies.append(pltpu.make_async_copy(rows.at[part], out.at[part], sems.at[i]))
        copies[-1].start()
    for copy in copies:
        copy.wait()


def spread(factor, place, *parts):
    rows = BLOCK // 4
    shape = (rows, place.shape[0], BLOCK)
    return local_call(
        functools.partial(spread_kernel, factor),
        "spread",
        [like(shape, jnp.float32)],
        1 + len(parts),
        6 * math.prod(shape),
        [
            pltpu.VMEM((len(ALL_PAIRS), rows, BLOCK), jnp.float32),
            pltpu.VMEM(shape, jnp.float32),
            pltpu.SemaphoreType.DMA((SPREAD_STEPS,)),
        ],
        IN_HBM,
    )(place, *parts)[0]


def six_pair_body(integrals, coeffs, pair_blocks, pair_count, orbital_count):
    width = coeffs.shape[1] // CHUNKS
    total_aux = integrals.shape[0] * lax.axis_size("aux")
    table = pair_blocks.T

    direct = cut(coeffs)
    shared, mine = cut_rest(coeffs, direct)
    parts = [direct, shared]
    inner = [lax.ppermute(part, "ao", INSIDE) for part in (parts[0], mine)]
    outer = [lax.ppermute(part, "ao", OUTSIDE) for part in parts]
    wants = tables(orbital_count, table, width)

    pieces = list(transform(0, wants, integrals, parts[0], outer[0], inner[0]))
    blocks = [[piece] for piece in pieces]
    inner[1], blocks[0][0] = lax.optimization_barrier((inner[1], blocks[0][0]))
    swapped = lax.ppermute(inner[1], "aux", SWAP)
    pieces = shared_transform(
        width, wants, integrals, parts[1], outer[1], inner[1], swapped
    )
    for block, piece in zip(blocks, pieces):
        block.append(piece)

    def fetch(s):
        swap = [(j, j ^ s) for j in range(GROUPS)]
        return [lax.ppermute(piece, "ao", swap) for piece in blocks[s]]

    middle = fetch(2)
    got = [blocks[0], fetch(1), middle]
    near0, across0, place = early_pairs(pair_count, table, got)
    far0 = lax.ppermute(across0, "aux", SWAP)
    got.append(fetch(3))
    near1, give1 = late_pairs(got)
    got1 = lax.ppermute(give1, "orb", SWAP)
    far1 = lax.ppermute((near1[1] + got1[1].astype(jnp.float32)).astype(jnp.bfloat16), "aux", SWAP)
    got0 = lax.ppermute(near0[1] + far0[1].astype(jnp.float32), "orb", SWAP)
    factor = 1.0 / math.sqrt(total_aux * ORBS)
    return spread(factor, place, near0, far0, got0, near1, got1, far1)


def solution(mesh):
    sizes = dict(mesh.shape)
    body = general_body
    if sizes["ao"] == 4 and sizes["aux"] == 2 and sizes["orb"] == 2:
        body = six_pair_body
    return jax.shard_map(
        body,
        mesh=mesh,
        in_specs=(
            P(("grp", "aux"), "ao", None),
            P(("grp", "ao"), "orb"),
            P("grp", None),
            P("grp"),
            P("grp"),
        ),
        out_specs=P(("aux", "orb"), ("grp", "ao"), None),
        check_vma=False,
    )
```

```python
import functools
import math

import jax
import jax.numpy as jnp
from jax import lax
from jax.experimental import pallas as pl
from jax.experimental.pallas import tpu as pltpu
from jax.sharding import PartitionSpec as P

BLOCK = 256
AO_DEV = 2
WIN = 5
ORBS = 1024
CHUNKS = 2
SPREAD_STEPS = 4
SPREAD_STEPS = 4
SPREAD_STEPS = 4
SPREAD_STEPS = 4
SPREAD_STEPS = 4
SPREAD_STEPS = 4
VMEM_LIMIT = 40 * 1024 * 1024
LEAD_FLOPS = 1 << 32
CUT_COPIES = 4
CUT_LIMIT = 53 * 1024 * 1024 + 256 * 1024


def with_halo(cells, sides, width):
    for axis, dim in sides:
        count = lax.axis_size(axis)
        ends = count - 1
        head = lax.slice_in_dim(cells, 0, width, axis=dim)
        tail = lax.slice_in_dim(cells, cells.shape[dim] - width, cells.shape[dim], axis=dim)
        cells = jnp.concatenate(
            [
                lax.ppermute(tail, axis, [(i, (i + 1) % count) for i in range(ends)]),
                cells,
                lax.ppermute(head, axis, [((i + 1) % count, i) for i in range(ends)]),
            ],
            axis=dim,
        )
    return cells


def general_body(integrals, coeffs, pair_blocks, pair_count, orbital_count):
    orb_local = coeffs.shape[1]
    aux_devices = lax.axis_size("aux")
    total_aux = integrals.shape[0] * aux_devices
    rim = WIN // 2 * BLOCK
    extended = with_halo(coeffs, (("ao", 0),), rim)
    ao_here = lax.axis_index("ao")
    orbital_ids = lax.axis_index("orb") * orb_local + jnp.arange(orb_local, dtype=jnp.int32)
    pieces = []
    for offset in range(AO_DEV):
        slab = integrals[:, offset * BLOCK : (offset + 1) * BLOCK, :]
        slot_range = extended[offset * BLOCK : offset * BLOCK + WIN * BLOCK]
        values = jnp.einsum("pml,li->pmi", slab, slot_range, preferred_element_type=jnp.float32)
        limit = orbital_count[ao_here * AO_DEV + offset]
        values = jnp.where((orbital_ids < limit)[None, None, :], values, 0.0)
        pieces.append(values.astype(jnp.bfloat16))
    transformed = jnp.stack(pieces)
    owners = lax.axis_size("ao")
    table = pair_blocks.reshape(owners, -1, 2)
    slots = table.shape[1]
    live = jnp.arange(slots, dtype=jnp.int32)[None, :] < pair_count[:, None]
    touched = live[:, :, None] & (table // AO_DEV == ao_here)
    wanted = jnp.max(jnp.where(touched, table % AO_DEV, 0), axis=(1, 2))
    outgoing = transformed[wanted]
    received = lax.all_to_all(outgoing, "ao", split_axis=0, concat_axis=0, tiled=True)
    owned = table[ao_here]
    factor = 1.0 / math.sqrt(total_aux * ORBS)
    weights = jnp.where(live[ao_here], factor, 0.0).astype(jnp.float32)
    left_source = owned[:, 0] // AO_DEV
    right_source = owned[:, 1] // AO_DEV
    right_factors = received[right_source]
    lefts = received[left_source]
    term = jnp.einsum("spmi,spni->msn", lefts, right_factors, preferred_element_type=jnp.float32)
    return lax.psum_scatter(
        term * weights[None, :, None], ("aux", "orb"), scatter_dimension=0, tiled=True
    )


EARLY_PAIRS = ((0, 1), (0, 2), (1, 2))
LATE_PAIRS = ((0, 3), (1, 3), (2, 3))
ALL_PAIRS = EARLY_PAIRS + LATE_PAIRS
GROUPS = 4
SWAP = [(0, 1), (1, 0)]
OUTSIDE = [(0, 1), (1, 0), (2, 3), (3, 2)]
INSIDE = [(1, 2), (2, 1)]

IN_HBM = pl.BlockSpec(memory_space=pltpu.HBM)
IN_VMEM = pl.BlockSpec(memory_space=pltpu.VMEM)


def like(shape, dtype):
    return jax.ShapeDtypeStruct(shape, dtype)


def local_call(kernel, name, out_shape, inputs, flops, scratch=(), out_spec=IN_VMEM):
    moved = sum(math.prod(o.shape) * o.dtype.itemsize for o in out_shape)
    return pl.pallas_call(
        kernel,
        out_shape=out_shape,
        in_specs=[IN_VMEM] * inputs,
        out_specs=[out_spec] * len(out_shape),
        scratch_shapes=list(scratch),
        compiler_params=pltpu.CompilerParams(vmem_limit_bytes=VMEM_LIMIT),
        cost_estimate=pl.CostEstimate(flops=flops, bytes_accessed=2 * moved, transcendentals=0),
        name=name,
    )


def dot(a, b):
    return jnp.dot(a, b, preferred_element_type=jnp.float32)


def cut_kernel(coeffs, direct, sem):
    rows, width = direct.shape
    step = rows // CUT_COPIES
    copies = []
    for i in range(CUT_COPIES):
        part = pl.ds(i * step, step)
        copies.append(
            pltpu.make_async_copy(coeffs.at[part, pl.ds(0, width)], direct.at[part], sem.at[i])
        )
        copies[-1].start()
    for copy in copies:
        copy.wait()


def cut(coeffs):
    rows, columns = coeffs.shape
    return pl.pallas_call(
        cut_kernel,
        out_shape=like((rows, columns // CHUNKS), coeffs.dtype),
        in_specs=[IN_HBM],
        out_specs=IN_VMEM,
        scratch_shapes=[pltpu.SemaphoreType.DMA((CUT_COPIES,))],
        compiler_params=pltpu.CompilerParams(vmem_limit_bytes=CUT_LIMIT),
        cost_estimate=pl.CostEstimate(flops=LEAD_FLOPS, bytes_accessed=0, transcendentals=0),
        name="cut",
    )(coeffs)


def rest_kernel(coeffs, first, shared, mine):
    width, half = shared.shape[1], mine.shape[1]
    shared[...] = coeffs[:, width:]
    start = pl.multiple_of(width + lax.axis_index("aux") * half, half)
    mine[...] = coeffs[:, pl.ds(start, half)]


def cut_rest(coeffs, first):
    rows, columns = coeffs.shape
    width = columns // CHUNKS
    return local_call(
        rest_kernel, "cut_rest", [like((rows, n), coeffs.dtype) for n in (width, width // 2)], 2, LEAD_FLOPS
    )(coeffs, first)


def scalar_at(values, index):
    ids = lax.broadcasted_iota(jnp.int32, values.shape, 1)
    return jnp.sum(jnp.where(ids == index, values, 0).astype(jnp.float32))


def tables_kernel(counts, table, wants):
    here, orb = lax.axis_index("ao"), lax.axis_index("orb")
    slots = table.shape[1] // GROUPS
    named = jnp.where(table[...] // AO_DEV == here, table[...] % AO_DEV, 0).astype(jnp.float32)
    owner = lax.broadcasted_iota(jnp.int32, table.shape, 1) // slots
    rows = [jnp.max(jnp.where(owner == here ^ s, named, 0.0)) for s in range(GROUPS)]
    for offset in range(AO_DEV):
        count = scalar_at(counts[...], here * AO_DEV + offset)
        rows.append(count - (orb * (ORBS // 2)).astype(jnp.float32))
    row = lax.broadcasted_iota(jnp.int32, wants.shape, 0)
    out = jnp.zeros(wants.shape, jnp.float32)
    for k, value in enumerate(rows):
        out = jnp.where(row == k, value, out)
    wants[...] = out.astype(jnp.int32)


def tables(counts, table, width):
    return local_call(
        tables_kernel, "tables", [like((8, width), jnp.int32)], 2, LEAD_FLOPS
    )(counts.reshape(1, -1), table)[0]


def transform_kernel(start, wants, integrals, own, outer, inner, *outs):
    mid = AO_DEV * BLOCK

    def blocks(prev, following):
        ids = start + lax.broadcasted_iota(jnp.int32, (BLOCK, own.shape[1]), 1)
        for p in range(integrals.shape[0]):
            both = []
            for offset in range(AO_DEV):
                low = mid - offset * BLOCK
                slab = integrals[p, offset * BLOCK : (offset + 1) * BLOCK, :]
                values = dot(slab[:, low : low + mid], own[...])
                values += dot(slab[:, :low], prev[offset * BLOCK :, :])
                values += dot(slab[:, low + mid :], following[: (offset + 1) * BLOCK, :])
                live = ids < wants[GROUPS + offset : GROUPS + offset + 1, :]
                both.append(jnp.where(live, values, 0.0))
            for s, out in enumerate(outs):
                out[p] = jnp.where(wants[s : s + 1, :] == 0, *both).astype(jnp.bfloat16)

    odd = lax.axis_index("ao") & 1
    pl.when(odd == 0)(lambda: blocks(inner, outer))
    pl.when(odd == 1)(lambda: blocks(outer, inner))


def shared_kernel(start, wants, integrals, own, outer, inner, swapped, *refs):
    *outs, whole = refs
    aux = lax.axis_index("aux")
    width = inner.shape[1]
    whole[:, pl.ds(pl.multiple_of(aux * width, width), width)] = inner[...]
    whole[:, pl.ds(pl.multiple_of((1 - aux) * width, width), width)] = swapped[...]
    transform_kernel(start, wants, integrals, own, outer, whole, *outs)


def shared_transform(start, wants, integrals, own, outer, inner, swapped):
    shape = (integrals.shape[0], BLOCK, own.shape[1])
    return local_call(
        functools.partial(shared_kernel, start),
        "transform",
        [like(shape, jnp.bfloat16)] * GROUPS,
        6,
        2 * AO_DEV * math.prod(shape) * integrals.shape[2],
        [pltpu.VMEM(own.shape, jnp.bfloat16)],
    )(wants, integrals, own, outer, inner, swapped)


def transform(start, wants, integrals, own, outer, inner):
    shape = (integrals.shape[0], BLOCK, own.shape[1])
    return local_call(
        functools.partial(transform_kernel, start),
        "transform",
        [like(shape, jnp.bfloat16)] * GROUPS,
        5,
        2 * AO_DEV * math.prod(shape) * integrals.shape[2],
    )(wants, integrals, own, outer, inner)


def form_pairs(pairs, blocks, grams, before=None):
    here = lax.axis_index("ao")
    slices = [[(ref, p) for ref in block for p in range(ref.shape[0])] for block in blocks]

    def product(left, right):
        total = None
        for (a, i), (b, j) in zip(slices[left], slices[right]):
            part = lax.dot_general(
                a[i], b[j], (((1,), (1,)), ((), ())), preferred_element_type=jnp.float32
            )
            total = part if total is None else total + part
        return total.reshape(grams.shape[1:])

    def formed(k, left, right):
        gram = product(left, right)
        return gram if before is None else gram + before[k]

    for bit in (0, 1):
        mine = [(k, a, b) for k, (a, b) in enumerate(pairs) if (a ^ b) >> 1 == bit]
        upper = (here >> bit) & 1

        @pl.when(upper == 0)
        def _(mine=mine):
            for k, a, b in mine:
                grams[k] = formed(k, a, b)

        @pl.when(upper == 1)
        def _(mine=mine):
            for k, a, b in mine:
                grams[k] = formed(k, b, a)


def early_kernel(live, table, *refs):
    used = 3 * CHUNKS
    own, middle, next_to = [refs[i : i + CHUNKS] for i in range(0, used, CHUNKS)]
    blocks = own, next_to, middle
    near, far, place, grams = refs[used:]
    here, aux, orb = (lax.axis_index(axis) for axis in ("ao", "aux", "orb"))
    slots, width = place.shape
    slot = lax.broadcasted_iota(jnp.int32, (slots, table.shape[1]), 0)
    column = lax.broadcasted_iota(jnp.int32, (slots, table.shape[1]), 1)
    shown = column == here * slots + slot
    sides = []
    for side in (0, 1):
        group = (table[side : side + 1, :] // AO_DEV).astype(jnp.float32)
        group = jnp.sum(jnp.where(shown, group, 0.0), axis=1, keepdims=True)
        sides.append(group.astype(jnp.int32) ^ here)
    low, high = jnp.minimum(*sides), jnp.maximum(*sides)
    index = jnp.where(high == 3, low + 3, jnp.where(high == 2, low + 1, 0))
    slot = lax.broadcasted_iota(jnp.int32, (slots, width), 0)
    count = scalar_at(live[...], here).astype(jnp.int32)
    place[...] = jnp.where(slot < count, index, len(ALL_PAIRS))
    form_pairs(EARLY_PAIRS, blocks, grams)
    for k in range(len(EARLY_PAIRS)):
        for core in (0, 1):
            near[core, k] = grams[k, 2 * aux + (orb ^ core)]
            far[core, k] = grams[k, 2 * (1 - aux) + (orb ^ core)].astype(jnp.bfloat16)


def begin_kernel(own, middle, next_to, last, grams):
    form_pairs(LATE_PAIRS, ([own], [next_to], [middle], [last]), grams)


def late_kernel(own, middle, next_to, last, before, *refs):
    keep, give, grams = refs
    blocks = [own], [next_to], [middle], [last]
    aux, orb = lax.axis_index("aux"), lax.axis_index("orb")
    form_pairs(LATE_PAIRS, blocks, grams, before)
    for k in range(len(LATE_PAIRS)):
        for chip in (0, 1):
            row = 2 * (aux ^ chip)
            keep[chip, k] = grams[k, row + orb]
            give[chip, k] = grams[k, row + 1 - orb]


def pair_flops(pairs, blocks):
    return 2 * len(pairs) * BLOCK * CHUNKS * blocks[0][0].size


def quarters(pairs):
    rows = BLOCK // 4
    return (2, len(pairs), rows, BLOCK), pltpu.VMEM((len(pairs), 4, rows, BLOCK), jnp.float32)


def early_pairs(live, table, blocks):
    shape, grams = quarters(EARLY_PAIRS)
    return local_call(
        early_kernel,
        "early_pairs",
        [
            like(shape, jnp.float32),
            like(shape, jnp.bfloat16),
            like((table.shape[1] // GROUPS, BLOCK), jnp.int32),
        ],
        2 + 3 * CHUNKS,
        pair_flops(EARLY_PAIRS, blocks),
        [grams],
    )(live.reshape(1, -1), table, *blocks[0], *blocks[2], *blocks[1])


def late_pairs(blocks):
    shape, grams = quarters(LATE_PAIRS)
    own, next_to, middle, last = blocks
    begun = local_call(
        begin_kernel,
        "begin_pairs",
        [like(grams.shape, jnp.float32)],
        GROUPS,
        pair_flops(LATE_PAIRS, blocks) // CHUNKS,
    )(own[0], middle[0], next_to[0], last[0])
    return local_call(
        late_kernel,
        "late_pairs",
        [like(shape, jnp.float32)] * 2,
        GROUPS + 1,
        pair_flops(LATE_PAIRS, blocks) // CHUNKS,
        [grams],
    )(own[1], middle[1], next_to[1], last[1], *begun)


def spread_kernel(factor, place, near0, far0, got0, near1, got1, far1, out, sums, rows, sems):
    early = near0.shape[1]
    sums[:early] = (near0[0] + far0[0].astype(jnp.float32) + got0[...]) * factor
    sums[early:] = (near1[0] + got1[0] + far1[...].astype(jnp.float32)) * factor
    total, slots, width = out.shape
    masks = [place[...] == k for k in range(sums.shape[0])]

    def one(m, carry):
        row = jnp.zeros((slots, width), jnp.float32)
        for k, mask in enumerate(masks):
            values = jnp.broadcast_to(sums[k, pl.ds(m, 1), :], (slots, width))
            row = jnp.where(mask, values, row)
        rows[m] = row
        return carry

    step = total // SPREAD_STEPS
    copies = []
    for i in range(SPREAD_STEPS):
        lax.fori_loop(i * step, (i + 1) * step, one, 0, unroll=8)
        part = pl.ds(i * step, step)
        copies.append(pltpu.make_async_copy(rows.at[part], out.at[part], sems.at[i]))
        copies[-1].start()
    for copy in copies:
        copy.wait()


def spread(factor, place, *parts):
    rows = BLOCK // 4
    shape = (rows, place.shape[0], BLOCK)
    return local_call(
        functools.partial(spread_kernel, factor),
        "spread",
        [like(shape, jnp.float32)],
        1 + len(parts),
        6 * math.prod(shape),
        [
            pltpu.VMEM((len(ALL_PAIRS), rows, BLOCK), jnp.float32),
            pltpu.VMEM(shape, jnp.float32),
            pltpu.SemaphoreType.DMA((SPREAD_STEPS,)),
        ],
        IN_HBM,
    )(place, *parts)[0]


def six_pair_body(integrals, coeffs, pair_blocks, pair_count, orbital_count):
    width = coeffs.shape[1] // CHUNKS
    total_aux = integrals.shape[0] * lax.axis_size("aux")
    table = pair_blocks.T

    direct = cut(coeffs)
    shared, mine = cut_rest(coeffs, direct)
    parts = [direct, shared]
    inner = [lax.ppermute(part, "ao", INSIDE) for part in (parts[0], mine)]
    outer = [lax.ppermute(part, "ao", OUTSIDE) for part in parts]
    wants = tables(orbital_count, table, width)

    pieces = list(transform(0, wants, integrals, parts[0], outer[0], inner[0]))
    blocks = [[piece] for piece in pieces]
    inner[1], blocks[0][0] = lax.optimization_barrier((inner[1], blocks[0][0]))
    swapped = lax.ppermute(inner[1], "aux", SWAP)
    pieces = shared_transform(
        width, wants, integrals, parts[1], outer[1], inner[1], swapped
    )
    for block, piece in zip(blocks, pieces):
        block.append(piece)

    def fetch(s):
        swap = [(j, j ^ s) for j in range(GROUPS)]
        return [lax.ppermute(piece, "ao", swap) for piece in blocks[s]]

    middle = fetch(2)
    got = [blocks[0], fetch(1), middle]
    near0, across0, place = early_pairs(pair_count, table, got)
    far0 = lax.ppermute(across0, "aux", SWAP)
    got.append(fetch(3))
    near1, give1 = late_pairs(got)
    got1 = lax.ppermute(give1, "orb", SWAP)
    far1 = lax.ppermute((near1[1] + got1[1]).astype(jnp.bfloat16), "aux", SWAP)
    got0 = lax.ppermute(near0[1] + far0[1].astype(jnp.float32), "orb", SWAP)
    factor = 1.0 / math.sqrt(total_aux * ORBS)
    return spread(factor, place, near0, far0, got0, near1, got1, far1)


def solution(mesh):
    sizes = dict(mesh.shape)
    body = general_body
    if sizes["ao"] == 4 and sizes["aux"] == 2 and sizes["orb"] == 2:
        body = six_pair_body
    return jax.shard_map(
        body,
        mesh=mesh,
        in_specs=(
            P(("grp", "aux"), "ao", None),
            P(("grp", "ao"), "orb"),
            P("grp", None),
            P("grp"),
            P("grp"),
        ),
        out_specs=P(("aux", "orb"), ("grp", "ao"), None),
        check_vma=False,
    )
```

```python
import functools
import math

import jax
import jax.numpy as jnp
from jax import lax
from jax.experimental import pallas as pl
from jax.experimental.pallas import tpu as pltpu
from jax.sharding import PartitionSpec as P

BLOCK = 256
AO_DEV = 2
WIN = 5
ORBS = 1024
CHUNKS = 2
SPREAD_STEPS = 4
SPREAD_STEPS = 4
SPREAD_STEPS = 4
SPREAD_STEPS = 4
SPREAD_STEPS = 4
SPREAD_STEPS = 4
VMEM_LIMIT = 40 * 1024 * 1024
LEAD_FLOPS = 1 << 32
LATE_WEIGHT = 10
CUT_COPIES = 4
CUT_LIMIT = 53 * 1024 * 1024 + 256 * 1024


def with_halo(cells, sides, width):
    for axis, dim in sides:
        count = lax.axis_size(axis)
        ends = count - 1
        head = lax.slice_in_dim(cells, 0, width, axis=dim)
        tail = lax.slice_in_dim(cells, cells.shape[dim] - width, cells.shape[dim], axis=dim)
        cells = jnp.concatenate(
            [
                lax.ppermute(tail, axis, [(i, (i + 1) % count) for i in range(ends)]),
                cells,
                lax.ppermute(head, axis, [((i + 1) % count, i) for i in range(ends)]),
            ],
            axis=dim,
        )
    return cells


def general_body(integrals, coeffs, pair_blocks, pair_count, orbital_count):
    orb_local = coeffs.shape[1]
    aux_devices = lax.axis_size("aux")
    total_aux = integrals.shape[0] * aux_devices
    rim = WIN // 2 * BLOCK
    extended = with_halo(coeffs, (("ao", 0),), rim)
    ao_here = lax.axis_index("ao")
    orbital_ids = lax.axis_index("orb") * orb_local + jnp.arange(orb_local, dtype=jnp.int32)
    pieces = []
    for offset in range(AO_DEV):
        slab = integrals[:, offset * BLOCK : (offset + 1) * BLOCK, :]
        slot_range = extended[offset * BLOCK : offset * BLOCK + WIN * BLOCK]
        values = jnp.einsum("pml,li->pmi", slab, slot_range, preferred_element_type=jnp.float32)
        limit = orbital_count[ao_here * AO_DEV + offset]
        values = jnp.where((orbital_ids < limit)[None, None, :], values, 0.0)
        pieces.append(values.astype(jnp.bfloat16))
    transformed = jnp.stack(pieces)
    owners = lax.axis_size("ao")
    table = pair_blocks.reshape(owners, -1, 2)
    slots = table.shape[1]
    live = jnp.arange(slots, dtype=jnp.int32)[None, :] < pair_count[:, None]
    touched = live[:, :, None] & (table // AO_DEV == ao_here)
    wanted = jnp.max(jnp.where(touched, table % AO_DEV, 0), axis=(1, 2))
    outgoing = transformed[wanted]
    received = lax.all_to_all(outgoing, "ao", split_axis=0, concat_axis=0, tiled=True)
    owned = table[ao_here]
    factor = 1.0 / math.sqrt(total_aux * ORBS)
    weights = jnp.where(live[ao_here], factor, 0.0).astype(jnp.float32)
    left_source = owned[:, 0] // AO_DEV
    right_source = owned[:, 1] // AO_DEV
    right_factors = received[right_source]
    lefts = received[left_source]
    term = jnp.einsum("spmi,spni->msn", lefts, right_factors, preferred_element_type=jnp.float32)
    return lax.psum_scatter(
        term * weights[None, :, None], ("aux", "orb"), scatter_dimension=0, tiled=True
    )


EARLY_PAIRS = ((0, 1), (0, 2), (1, 2))
LATE_PAIRS = ((0, 3), (1, 3), (2, 3))
ALL_PAIRS = EARLY_PAIRS + LATE_PAIRS
GROUPS = 4
SWAP = [(0, 1), (1, 0)]
OUTSIDE = [(0, 1), (1, 0), (2, 3), (3, 2)]
INSIDE = [(1, 2), (2, 1)]

IN_HBM = pl.BlockSpec(memory_space=pltpu.HBM)
IN_VMEM = pl.BlockSpec(memory_space=pltpu.VMEM)


def like(shape, dtype):
    return jax.ShapeDtypeStruct(shape, dtype)


def local_call(kernel, name, out_shape, inputs, flops, scratch=(), out_spec=IN_VMEM):
    moved = sum(math.prod(o.shape) * o.dtype.itemsize for o in out_shape)
    return pl.pallas_call(
        kernel,
        out_shape=out_shape,
        in_specs=[IN_VMEM] * inputs,
        out_specs=[out_spec] * len(out_shape),
        scratch_shapes=list(scratch),
        compiler_params=pltpu.CompilerParams(vmem_limit_bytes=VMEM_LIMIT),
        cost_estimate=pl.CostEstimate(flops=flops, bytes_accessed=2 * moved, transcendentals=0),
        name=name,
    )


def dot(a, b):
    return jnp.dot(a, b, preferred_element_type=jnp.float32)


def cut_kernel(coeffs, direct, sem):
    rows, width = direct.shape
    step = rows // CUT_COPIES
    copies = []
    for i in range(CUT_COPIES):
        part = pl.ds(i * step, step)
        copies.append(
            pltpu.make_async_copy(coeffs.at[part, pl.ds(0, width)], direct.at[part], sem.at[i])
        )
        copies[-1].start()
    for copy in copies:
        copy.wait()


def cut(coeffs):
    rows, columns = coeffs.shape
    return pl.pallas_call(
        cut_kernel,
        out_shape=like((rows, columns // CHUNKS), coeffs.dtype),
        in_specs=[IN_HBM],
        out_specs=IN_VMEM,
        scratch_shapes=[pltpu.SemaphoreType.DMA((CUT_COPIES,))],
        compiler_params=pltpu.CompilerParams(vmem_limit_bytes=CUT_LIMIT),
        cost_estimate=pl.CostEstimate(flops=LEAD_FLOPS, bytes_accessed=0, transcendentals=0),
        name="cut",
    )(coeffs)


def rest_kernel(coeffs, first, shared, mine):
    width, half = shared.shape[1], mine.shape[1]
    shared[...] = coeffs[:, width:]
    start = pl.multiple_of(width + lax.axis_index("aux") * half, half)
    mine[...] = coeffs[:, pl.ds(start, half)]


def cut_rest(coeffs, first):
    rows, columns = coeffs.shape
    width = columns // CHUNKS
    return local_call(
        rest_kernel, "cut_rest", [like((rows, n), coeffs.dtype) for n in (width, width // 2)], 2, LEAD_FLOPS
    )(coeffs, first)


def scalar_at(values, index):
    ids = lax.broadcasted_iota(jnp.int32, values.shape, 1)
    return jnp.sum(jnp.where(ids == index, values, 0).astype(jnp.float32))


def tables_kernel(counts, table, wants):
    here, orb = lax.axis_index("ao"), lax.axis_index("orb")
    slots = table.shape[1] // GROUPS
    named = jnp.where(table[...] // AO_DEV == here, table[...] % AO_DEV, 0).astype(jnp.float32)
    owner = lax.broadcasted_iota(jnp.int32, table.shape, 1) // slots
    rows = [jnp.max(jnp.where(owner == here ^ s, named, 0.0)) for s in range(GROUPS)]
    for offset in range(AO_DEV):
        count = scalar_at(counts[...], here * AO_DEV + offset)
        rows.append(count - (orb * (ORBS // 2)).astype(jnp.float32))
    row = lax.broadcasted_iota(jnp.int32, wants.shape, 0)
    out = jnp.zeros(wants.shape, jnp.float32)
    for k, value in enumerate(rows):
        out = jnp.where(row == k, value, out)
    wants[...] = out.astype(jnp.int32)


def tables(counts, table, width):
    return local_call(
        tables_kernel, "tables", [like((8, width), jnp.int32)], 2, LEAD_FLOPS
    )(counts.reshape(1, -1), table)[0]


def transform_kernel(start, wants, integrals, own, outer, inner, *outs):
    mid = AO_DEV * BLOCK

    def blocks(prev, following):
        ids = start + lax.broadcasted_iota(jnp.int32, (BLOCK, own.shape[1]), 1)
        for p in range(integrals.shape[0]):
            both = []
            for offset in range(AO_DEV):
                low = mid - offset * BLOCK
                slab = integrals[p, offset * BLOCK : (offset + 1) * BLOCK, :]
                values = dot(slab[:, low : low + mid], own[...])
                values += dot(slab[:, :low], prev[offset * BLOCK :, :])
                values += dot(slab[:, low + mid :], following[: (offset + 1) * BLOCK, :])
                live = ids < wants[GROUPS + offset : GROUPS + offset + 1, :]
                both.append(jnp.where(live, values, 0.0))
            for s, out in enumerate(outs):
                out[p] = jnp.where(wants[s : s + 1, :] == 0, *both).astype(jnp.bfloat16)

    odd = lax.axis_index("ao") & 1
    pl.when(odd == 0)(lambda: blocks(inner, outer))
    pl.when(odd == 1)(lambda: blocks(outer, inner))


def shared_kernel(start, wants, integrals, own, outer, inner, swapped, *refs):
    *outs, whole = refs
    aux = lax.axis_index("aux")
    width = inner.shape[1]
    whole[:, pl.ds(pl.multiple_of(aux * width, width), width)] = inner[...]
    whole[:, pl.ds(pl.multiple_of((1 - aux) * width, width), width)] = swapped[...]
    transform_kernel(start, wants, integrals, own, outer, whole, *outs)


def shared_transform(start, wants, integrals, own, outer, inner, swapped):
    shape = (integrals.shape[0], BLOCK, own.shape[1])
    return local_call(
        functools.partial(shared_kernel, start),
        "transform",
        [like(shape, jnp.bfloat16)] * GROUPS,
        6,
        2 * AO_DEV * math.prod(shape) * integrals.shape[2],
        [pltpu.VMEM(own.shape, jnp.bfloat16)],
    )(wants, integrals, own, outer, inner, swapped)


def transform(start, wants, integrals, own, outer, inner):
    shape = (integrals.shape[0], BLOCK, own.shape[1])
    return local_call(
        functools.partial(transform_kernel, start),
        "transform",
        [like(shape, jnp.bfloat16)] * GROUPS,
        5,
        2 * AO_DEV * math.prod(shape) * integrals.shape[2],
    )(wants, integrals, own, outer, inner)


def form_pairs(pairs, blocks, grams, before=None):
    here = lax.axis_index("ao")
    slices = [[(ref, p) for ref in block for p in range(ref.shape[0])] for block in blocks]

    def product(left, right):
        total = None
        for (a, i), (b, j) in zip(slices[left], slices[right]):
            part = lax.dot_general(
                a[i], b[j], (((1,), (1,)), ((), ())), preferred_element_type=jnp.float32
            )
            total = part if total is None else total + part
        return total.reshape(grams.shape[1:])

    def formed(k, left, right):
        gram = product(left, right)
        return gram if before is None else gram + before[k]

    for bit in (0, 1):
        mine = [(k, a, b) for k, (a, b) in enumerate(pairs) if (a ^ b) >> 1 == bit]
        upper = (here >> bit) & 1

        @pl.when(upper == 0)
        def _(mine=mine):
            for k, a, b in mine:
                grams[k] = formed(k, a, b)

        @pl.when(upper == 1)
        def _(mine=mine):
            for k, a, b in mine:
                grams[k] = formed(k, b, a)


def early_kernel(live, table, *refs):
    used = 3 * CHUNKS
    own, middle, next_to = [refs[i : i + CHUNKS] for i in range(0, used, CHUNKS)]
    blocks = own, next_to, middle
    near, far, place, grams = refs[used:]
    here, aux, orb = (lax.axis_index(axis) for axis in ("ao", "aux", "orb"))
    slots, width = place.shape
    slot = lax.broadcasted_iota(jnp.int32, (slots, table.shape[1]), 0)
    column = lax.broadcasted_iota(jnp.int32, (slots, table.shape[1]), 1)
    shown = column == here * slots + slot
    sides = []
    for side in (0, 1):
        group = (table[side : side + 1, :] // AO_DEV).astype(jnp.float32)
        group = jnp.sum(jnp.where(shown, group, 0.0), axis=1, keepdims=True)
        sides.append(group.astype(jnp.int32) ^ here)
    low, high = jnp.minimum(*sides), jnp.maximum(*sides)
    index = jnp.where(high == 3, low + 3, jnp.where(high == 2, low + 1, 0))
    slot = lax.broadcasted_iota(jnp.int32, (slots, width), 0)
    count = scalar_at(live[...], here).astype(jnp.int32)
    place[...] = jnp.where(slot < count, index, len(ALL_PAIRS))
    form_pairs(EARLY_PAIRS, blocks, grams)
    for k in range(len(EARLY_PAIRS)):
        for core in (0, 1):
            near[core, k] = grams[k, 2 * aux + (orb ^ core)]
            far[core, k] = grams[k, 2 * (1 - aux) + (orb ^ core)].astype(jnp.bfloat16)


def begin_kernel(own, middle, next_to, last, grams):
    form_pairs(LATE_PAIRS, ([own], [next_to], [middle], [last]), grams)


def late_kernel(own, middle, next_to, last, before, *refs):
    keep, give, grams = refs
    blocks = [own], [next_to], [middle], [last]
    aux, orb = lax.axis_index("aux"), lax.axis_index("orb")
    form_pairs(LATE_PAIRS, blocks, grams, before)
    for k in range(len(LATE_PAIRS)):
        for chip in (0, 1):
            row = 2 * (aux ^ chip)
            keep[chip, k] = grams[k, row + orb]
            give[chip, k] = grams[k, row + 1 - orb].astype(jnp.bfloat16)


def pair_flops(pairs, blocks):
    return 2 * len(pairs) * BLOCK * CHUNKS * blocks[0][0].size


def quarters(pairs):
    rows = BLOCK // 4
    return (2, len(pairs), rows, BLOCK), pltpu.VMEM((len(pairs), 4, rows, BLOCK), jnp.float32)


def early_pairs(live, table, blocks):
    shape, grams = quarters(EARLY_PAIRS)
    return local_call(
        early_kernel,
        "early_pairs",
        [
            like(shape, jnp.float32),
            like(shape, jnp.bfloat16),
            like((table.shape[1] // GROUPS, BLOCK), jnp.int32),
        ],
        2 + 3 * CHUNKS,
        pair_flops(EARLY_PAIRS, blocks),
        [grams],
    )(live.reshape(1, -1), table, *blocks[0], *blocks[2], *blocks[1])


def late_pairs(blocks):
    shape, grams = quarters(LATE_PAIRS)
    own, next_to, middle, last = blocks
    begun = local_call(
        begin_kernel,
        "begin_pairs",
        [like(grams.shape, jnp.float32)],
        GROUPS,
        pair_flops(LATE_PAIRS, blocks) // CHUNKS,
    )(own[0], middle[0], next_to[0], last[0])
    return local_call(
        late_kernel,
        "late_pairs",
        [like(shape, jnp.float32), like(shape, jnp.bfloat16)],
        GROUPS + 1,
        LATE_WEIGHT * pair_flops(LATE_PAIRS, blocks) // CHUNKS,
        [grams],
    )(own[1], middle[1], next_to[1], last[1], *begun)


def spread_kernel(factor, place, near0, far0, got0, near1, got1, far1, out, sums, rows, sems):
    early = near0.shape[1]
    sums[:early] = (near0[0] + far0[0].astype(jnp.float32) + got0[...]) * factor
    sums[early:] = (near1[0] + got1[0].astype(jnp.float32) + far1[...].astype(jnp.float32)) * factor
    total, slots, width = out.shape
    masks = [place[...] == k for k in range(sums.shape[0])]

    def one(m, carry):
        row = jnp.zeros((slots, width), jnp.float32)
        for k, mask in enumerate(masks):
            values = jnp.broadcast_to(sums[k, pl.ds(m, 1), :], (slots, width))
            row = jnp.where(mask, values, row)
        rows[m] = row
        return carry

    step = total // SPREAD_STEPS
    copies = []
    for i in range(SPREAD_STEPS):
        lax.fori_loop(i * step, (i + 1) * step, one, 0, unroll=8)
        part = pl.ds(i * step, step)
        copies.append(pltpu.make_async_copy(rows.at[part], out.at[part], sems.at[i]))
        copies[-1].start()
    for copy in copies:
        copy.wait()


def spread(factor, place, *parts):
    rows = BLOCK // 4
    shape = (rows, place.shape[0], BLOCK)
    return local_call(
        functools.partial(spread_kernel, factor),
        "spread",
        [like(shape, jnp.float32)],
        1 + len(parts),
        6 * math.prod(shape),
        [
            pltpu.VMEM((len(ALL_PAIRS), rows, BLOCK), jnp.float32),
            pltpu.VMEM(shape, jnp.float32),
            pltpu.SemaphoreType.DMA((SPREAD_STEPS,)),
        ],
        IN_HBM,
    )(place, *parts)[0]


def six_pair_body(integrals, coeffs, pair_blocks, pair_count, orbital_count):
    width = coeffs.shape[1] // CHUNKS
    total_aux = integrals.shape[0] * lax.axis_size("aux")
    table = pair_blocks.T

    direct = cut(coeffs)
    shared, mine = cut_rest(coeffs, direct)
    parts = [direct, shared]
    inner = [lax.ppermute(part, "ao", INSIDE) for part in (parts[0], mine)]
    outer = [lax.ppermute(part, "ao", OUTSIDE) for part in parts]
    wants = tables(orbital_count, table, width)

    pieces = list(transform(0, wants, integrals, parts[0], outer[0], inner[0]))
    blocks = [[piece] for piece in pieces]
    inner[1], blocks[0][0] = lax.optimization_barrier((inner[1], blocks[0][0]))
    swapped = lax.ppermute(inner[1], "aux", SWAP)
    pieces = shared_transform(
        width, wants, integrals, parts[1], outer[1], inner[1], swapped
    )
    for block, piece in zip(blocks, pieces):
        block.append(piece)

    def fetch(s):
        swap = [(j, j ^ s) for j in range(GROUPS)]
        return [lax.ppermute(piece, "ao", swap) for piece in blocks[s]]

    middle = fetch(2)
    got = [blocks[0], fetch(1), middle]
    near0, across0, place = early_pairs(pair_count, table, got)
    far0 = lax.ppermute(across0, "aux", SWAP)
    got.append(fetch(3))
    near1, give1 = late_pairs(got)
    got1 = lax.ppermute(give1, "orb", SWAP)
    far1 = lax.ppermute((near1[1] + got1[1].astype(jnp.float32)).astype(jnp.bfloat16), "aux", SWAP)
    got0 = lax.ppermute(near0[1] + far0[1].astype(jnp.float32), "orb", SWAP)
    factor = 1.0 / math.sqrt(total_aux * ORBS)
    return spread(factor, place, near0, far0, got0, near1, got1, far1)


def solution(mesh):
    sizes = dict(mesh.shape)
    body = general_body
    if sizes["ao"] == 4 and sizes["aux"] == 2 and sizes["orb"] == 2:
        body = six_pair_body
    return jax.shard_map(
        body,
        mesh=mesh,
        in_specs=(
            P(("grp", "aux"), "ao", None),
            P(("grp", "ao"), "orb"),
            P("grp", None),
            P("grp"),
            P("grp"),
        ),
        out_specs=P(("aux", "orb"), ("grp", "ao"), None),
        check_vma=False,
    )
```
